32 devices in a mesh: row: 4 (over y, core), col: 8 (over z, x).
Axes of the slice: x: 2, y: 2, z: 4, core: 2. Of those that a mesh axis runs over, the one named last changes fastest.
Arguments:
- amplitudes: bfloat16 [2048, 1024], P('row', 'col'), may hold values from -6 to 6
- packed_tiles: bfloat16 [4, 128, 128, 128], P('row', 'col'), may hold values from -0.1875 to 0.1875
- tile_ids: int32 [4, 128], P('row', 'col'), may hold values from 0 to 127, as said below
- residual_in: float32 [2048, 8192], P('row', 'col'), may hold values from -6 to 6
Outputs:
- ladder: float32 [2048, 8192], P('row', 'col')
The draws below stay inside these ranges and needn't reach their ends.
Inputs may be any that keep to these rules, and one draw needn't show every extreme that they name: `tile_ids`: in each grid row the ids are a permutation of 0 to 127; no device holds more than 2 ids of one value of id // 16, and some device holds exactly 2.
All inputs are finite; a program needn't handle non-finite values.
Results may differ from the reference program's by a relative error of at most 0.0003.
Values may be sent and summed in bfloat16 or wider, within the bound.
No kernel may reach another device: no remote copies, remote signals or barrier semaphores. Data moves between devices by JAX's collectives and lax.ppermute only.
A program may use at most 64 MiB of HBM per device.

```python
import jax
import jax.numpy as jnp

TILE = 128
KT_DEV = 2
QT_DEV = 8
TILES_DEV = 16
KDIM = 1024
QDIM = 8192
PAIRS = 2048
N_ROW = 4
N_COL = 8


def draw_tile_ids(key, part):
    total = N_COL * TILES_DEV

    def one_row(row_key):
        key_perm, key_pos, key_mix = jax.random.split(row_key, 3)
        source_perm = jax.random.permutation(key_perm, N_COL)
        dest_col = jnp.repeat(jnp.arange(N_COL), TILES_DEV)
        serial = jnp.tile(jnp.arange(TILES_DEV), N_COL)
        local_pos = jax.vmap(lambda sub_key: jax.random.permutation(sub_key, TILES_DEV))(jax.random.split(key_pos, N_COL)).reshape(-1)
        source = source_perm[(dest_col + serial) % N_COL]
        identity = dest_col * TILES_DEV + local_pos
        shuffle = jax.random.permutation(key_mix, total)
        scores = source * total + shuffle
        ordering = jnp.argsort(scores, stable=True)
        return identity[ordering]
    return jax.vmap(one_row)(jax.random.split(key, N_ROW)).astype(jnp.int32)


def shard_levels(own_key, extent, pieces, smallest, top_value):
    level = 1.0
    for dim, parts in pieces:
        draws = jax.random.uniform(jax.random.fold_in(jax.random.fold_in(own_key, 6), dim), (parts,), jnp.float32, smallest / len(pieces), top_value / len(pieces))
        level = level * jnp.repeat(jnp.exp(draws), extent[dim] // parts).reshape((-1,) + (1,) * (len(extent) - 1 - dim))
    return level


def noise(rng, extent, spread, bound, shards=(), held_as=jnp.bfloat16):
    loudness = shard_levels(rng, extent, shards, -0.22, 0.18) if shards else 1.0
    result = jax.random.normal(rng, extent, jnp.float32) * spread * loudness
    return jnp.minimum(jnp.maximum(result, -bound), bound).astype(held_as)


def setup_inputs(seed: int = 0) -> dict:
    arg_keys = jax.random.split(jax.random.key(seed), 5)
    amplitudes = noise(arg_keys[0], (PAIRS, KDIM), 1.0, 6.0, ((0, 4), (1, 8)))
    packed_tiles = noise(arg_keys[1], (N_ROW, N_COL * TILES_DEV, TILE, TILE), KDIM ** -0.5, 0.1875, ((0, 4), (1, 8)))
    tile_ids = draw_tile_ids(jax.random.fold_in(arg_keys[4], 71), 0)
    residual_in = noise(arg_keys[3], (PAIRS, QDIM), 1.0, 6.0, ((0, 4), (1, 8)), jnp.float32)
    return dict(amplitudes=amplitudes, packed_tiles=packed_tiles, tile_ids=tile_ids, residual_in=residual_in)


def reference(amplitudes, packed_tiles, tile_ids, residual_in):
    ordering = jnp.argsort(tile_ids, axis=1)
    arranged = jnp.take_along_axis(packed_tiles, ordering[:, :, None, None], axis=1)
    arranged = arranged.reshape(N_ROW, N_COL, KT_DEV, QT_DEV, TILE, TILE)
    arranged = arranged.transpose(0, 2, 4, 1, 3, 5).reshape(KDIM, QDIM)
    product = jnp.dot(amplitudes, arranged, preferred_element_type=jnp.float32)
    return residual_in + product
```

```python
import functools
import math

import jax
import jax.numpy as jnp
from jax import lax
from jax.experimental import pallas as pl
from jax.experimental.pallas import tpu as pltpu
from jax.sharding import PartitionSpec as P

KT_DEV = 2
QT_DEV = 8
CORES = 2
META = 16


def pack_kernel(
    columns, capacity, ids_ref, tiles_ref, out_ref, table, count, meta, tile_sem, meta_sem
):
    per_device, width = tiles_ref.shape[1], tiles_ref.shape[2]
    empty = jnp.int32(per_device)

    def clear(d, _):
        count[d] = 0
        for s in range(capacity):
            table[d * capacity + s] = empty
        return 0

    lax.fori_loop(0, columns, clear, 0)

    def place(t, _):
        tile_id = ids_ref[0, t]
        target = tile_id // per_device
        rank = count[target]
        count[target] = rank + 1
        table[target * capacity + rank] = tile_id % per_device
        pltpu.make_async_copy(
            tiles_ref.at[0, t],
            out_ref.at[target, pl.ds(pl.multiple_of(rank * width, width), width), :],
            tile_sem,
        ).start()
        return 0

    lax.fori_loop(0, per_device, place, 0)
    lane = lax.broadcasted_iota(jnp.int32, (META, width), 1)

    def describe(d, _):
        row = jnp.full((META, width), empty)
        for s in range(capacity):
            row = jnp.where(lane == s, table[d * capacity + s], row)
        meta[d] = row.astype(jnp.float32).astype(jnp.bfloat16)
        return 0

    lax.fori_loop(0, columns, describe, 0)
    meta_copy = pltpu.make_async_copy(
        meta, out_ref.at[:, pl.ds(capacity * width, META), :], meta_sem
    )
    meta_copy.start()
    meta_copy.wait()
    pltpu.make_async_copy(tiles_ref, tiles_ref, tile_sem).wait()


def pack(packed_tiles, tile_ids, columns, capacity):
    _, per_device, width, _ = packed_tiles.shape
    return pl.pallas_call(
        functools.partial(pack_kernel, columns, capacity),
        out_shape=jax.ShapeDtypeStruct(
            (columns, capacity * width + META, width), packed_tiles.dtype
        ),
        in_specs=[
            pl.BlockSpec(memory_space=pltpu.SMEM),
            pl.BlockSpec(memory_space=pl.ANY),
        ],
        out_specs=pl.BlockSpec(memory_space=pl.ANY),
        scratch_shapes=[
            pltpu.SMEM((columns * capacity,), jnp.int32),
            pltpu.SMEM((columns,), jnp.int32),
            pltpu.VMEM((columns, META, width), jnp.bfloat16),
            pltpu.SemaphoreType.DMA,
            pltpu.SemaphoreType.DMA,
        ],
        name="pack",
    )(tile_ids, packed_tiles)


def ladder_kernel(n_pieces, n_amps, capacity, where_ref, *refs):
    pieces = refs[:n_pieces]
    amps = refs[n_pieces : n_pieces + n_amps]
    residual, out = refs[n_pieces + n_amps : n_pieces + n_amps + 2]
    (
        meta,
        places,
        table,
        amp,
        block,
        total,
        meta_sem,
        table_sem,
        amp_sem,
        tile_sem,
        res_sem,
        out_sem,
    ) = refs[n_pieces + n_amps + 2 :]
    columns = pieces[0].shape[0]
    width = pieces[0].shape[2]
    per_device = KT_DEV * QT_DEV
    for p, piece in enumerate(pieces):
        pltpu.make_async_copy(
            piece.at[:, pl.ds(capacity * width, META), :],
            meta.at[pl.ds(p * columns, columns)],
            meta_sem,
        ).start()
    for a, source in enumerate(amps):
        column = where_ref[n_pieces + a]

        @pl.when(column >= 0)
        def _():
            pltpu.make_async_copy(
                source,
                amp.at[:, pl.ds(pl.multiple_of(column * width, width), width)],
                amp_sem,
            ).start()

    res_copy = pltpu.make_async_copy(residual, total, res_sem)
    res_copy.start()
    pltpu.make_async_copy(meta, meta, meta_sem).wait()
    for p in range(n_pieces):
        rows = meta[p * columns : (p + 1) * columns]
        places[p * columns : (p + 1) * columns] = jnp.max(
            rows.astype(jnp.float32), axis=1
        ).astype(jnp.int32)
    table_copy = pltpu.make_async_copy(places, table, table_sem)
    table_copy.start()
    table_copy.wait()
    for p, piece in enumerate(pieces):
        row = where_ref[p]

        def place(c, _, p=p, piece=piece, row=row):
            for s in range(capacity):
                position = table[p * columns + c, s]
                k = row * KT_DEV + position // QT_DEV
                q = position % QT_DEV

                @pl.when(position < per_device)
                def _():
                    pltpu.make_async_copy(
                        piece.at[c, pl.ds(s * width, width), :],
                        block.at[
                            pl.ds(pl.multiple_of(k * width, width), width),
                            pl.ds(pl.multiple_of(q * width, width), width),
                        ],
                        tile_sem,
                    ).start()

            return 0

        lax.fori_loop(0, columns, place, 0)
    pltpu.make_async_copy(amp, amp, amp_sem).wait()
    res_copy.wait()
    pltpu.make_async_copy(block, block, tile_sem).wait()
    step = 2 * width
    outs = []
    for n in range(block.shape[1] // step):
        cols = slice(n * step, (n + 1) * step)
        total[:, cols] += jnp.dot(
            amp[...], block[:, cols], preferred_element_type=jnp.float32
        )
        copy = pltpu.make_async_copy(
            total.at[:, pl.ds(n * step, step)],
            out.at[:, pl.ds(n * step, step)],
            out_sem.at[n],
        )
        copy.start()
        outs.append(copy)
    for copy in outs:
        copy.wait()


def ladder(where, pieces, amps, residual, capacity):
    columns, _, width = pieces[0].shape
    n_pieces, n_amps = len(pieces), len(amps)
    rows, n_cols = residual.shape
    depth = n_pieces * KT_DEV * width
    any_spec = pl.BlockSpec(memory_space=pl.ANY)
    return pl.pallas_call(
        functools.partial(ladder_kernel, n_pieces, n_amps, capacity),
        out_shape=jax.ShapeDtypeStruct(residual.shape, residual.dtype),
        in_specs=[pl.BlockSpec(memory_space=pltpu.SMEM)]
        + [any_spec] * (n_pieces + n_amps + 1),
        out_specs=any_spec,
        scratch_shapes=[
            pltpu.VMEM((n_pieces * columns, META, width), jnp.bfloat16),
            pltpu.VMEM((n_pieces * columns, width), jnp.int32),
            pltpu.SMEM((n_pieces * columns, width), jnp.int32),
            pltpu.VMEM((rows, depth), jnp.bfloat16),
            pltpu.VMEM((depth, n_cols), jnp.bfloat16),
            pltpu.VMEM((rows, n_cols), jnp.float32),
            pltpu.SemaphoreType.DMA,
            pltpu.SemaphoreType.DMA,
            pltpu.SemaphoreType.DMA,
            pltpu.SemaphoreType.DMA,
            pltpu.SemaphoreType.DMA,
            pltpu.SemaphoreType.DMA((n_cols // (2 * width),)),
        ],
        compiler_params=pltpu.CompilerParams(vmem_limit_bytes=40 * 1024 * 1024),
        name="ladder",
    )(where, *pieces, *amps, residual)


def gather_amps(amplitudes, outer, inner):
    col = lax.axis_index("col")
    place, lane = col // inner, col % inner
    held, owners = [amplitudes], [place]
    up = down = amplitudes
    for s in range(1, outer):
        rising = [
            (z * inner + x, (z + 1) * inner + x)
            for z in range(s - 1, outer - 1)
            for x in range(inner)
        ]
        falling = [
            ((z + 1) * inner + x, z * inner + x)
            for z in range(0, outer - s)
            for x in range(inner)
        ]
        up = lax.ppermute(up, "col", rising)
        down = lax.ppermute(down, "col", falling)
        held += [up, down]
        owners += [
            jnp.where(place >= s, place - s, -1),
            jnp.where(place + s < outer, place + s, -1),
        ]
    shards, columns = [], []
    for shift in range(inner):
        source_lane = (lane - shift) % inner
        for shard, owner in zip(held, owners):
            if shift:
                pairs = [
                    (z * inner + x, z * inner + (x + shift) % inner)
                    for z in range(outer)
                    for x in range(inner)
                ]
                shard = lax.ppermute(shard, "col", pairs)
            shards.append(shard)
            columns.append(jnp.where(owner >= 0, owner * inner + source_lane, -1))
    return shards, columns


def gather_pieces(piece, groups):
    row = lax.axis_index("row")
    group, core = row // CORES, row % CORES
    pieces, rows = [], []
    for shift in range(groups):
        pairs = [
            (g * CORES + c, (g + shift) % groups * CORES + c)
            for g in range(groups)
            for c in range(CORES)
        ]
        mine = lax.ppermute(piece, "row", pairs) if shift else piece
        swap = [
            (g * CORES + c, g * CORES + 1 - c) for g in range(groups) for c in range(CORES)
        ]
        pieces += [mine, lax.ppermute(mine, "row", swap)]
        source = (group - shift) % groups * CORES
        rows += [source + core, source + 1 - core]
    return pieces, rows


def body(amplitudes, packed_tiles, tile_ids, residual_in):
    n_col, n_row = lax.axis_size("col"), lax.axis_size("row")
    inner = 2 ** (int(math.log2(n_col)) // 2)
    outer = n_col // inner
    capacity = -(-packed_tiles.shape[1] // n_col)
    shards, columns = gather_amps(amplitudes, outer, inner)
    outgoing = pack(packed_tiles, tile_ids, n_col, capacity)
    incoming = lax.all_to_all(outgoing, "col", split_axis=0, concat_axis=0, tiled=True)
    pieces, rows = gather_pieces(incoming, n_row // CORES)
    where = jnp.stack(rows + columns).astype(jnp.int32)
    return ladder(where, pieces, shards, residual_in, capacity)


def solution(mesh):
    in_specs = (P("row", "col"), P("row", "col", None, None), P("row", "col"), P("row", "col"))
    out_specs = P("row", "col")
    return jax.shard_map(body, mesh=mesh, in_specs=in_specs, out_specs=out_specs, check_vma=False)
```

```python
import functools
import math

import jax
import jax.numpy as jnp
from jax import lax
from jax.experimental import pallas as pl
from jax.experimental.pallas import tpu as pltpu
from jax.sharding import PartitionSpec as P

KT_DEV = 2
QT_DEV = 8
CORES = 2
META = 16
MIB = 1024 * 1024


def pack_kernel(columns, capacity, me_ref, ids_ref, tiles_ref, *refs):
    outs, slot_tile, slot_place, count = refs[:columns], *refs[columns:]
    per_device, width = tiles_ref.shape[1], tiles_ref.shape[2]
    shift = per_device.bit_length() - 1
    for d in range(columns):
        count[d] = 0
        for s in range(capacity):
            slot_place[d * capacity + s] = per_device
    for t in range(per_device):
        tile_id = ids_ref[0, t]
        target = lax.shift_right_logical(tile_id, shift)
        rank = count[target]
        count[target] = rank + 1
        slot_tile[target * capacity + rank] = t
        slot_place[target * capacity + rank] = tile_id & (per_device - 1)
    lane = lax.broadcasted_iota(jnp.int32, (META, width), 1)
    for d, out in enumerate(outs):
        target = me_ref[0] ^ d
        row = jnp.full((META, width), per_device, jnp.int32)
        for s in range(capacity):
            place = slot_place[target * capacity + s]
            row = jnp.where(lane == s, place, row)

            @pl.when(place < per_device)
            def _():
                out[s * width : (s + 1) * width, :] = tiles_ref[
                    0, slot_tile[target * capacity + s]
                ]

        out[capacity * width :, :] = row.astype(jnp.float32).astype(jnp.bfloat16)


def pack(col, packed_tiles, tile_ids, columns, capacity):
    _, per_device, width, _ = packed_tiles.shape
    chunk = jax.ShapeDtypeStruct((capacity * width + META, width), packed_tiles.dtype)
    smem = pl.BlockSpec(memory_space=pltpu.SMEM)
    vmem = pl.BlockSpec(memory_space=pltpu.VMEM)
    return pl.pallas_call(
        functools.partial(pack_kernel, columns, capacity),
        out_shape=[chunk] * columns,
        in_specs=[smem, smem, vmem],
        out_specs=[vmem] * columns,
        scratch_shapes=[
            pltpu.SMEM((columns * capacity,), jnp.int32),
            pltpu.SMEM((columns * capacity,), jnp.int32),
            pltpu.SMEM((columns,), jnp.int32),
        ],
        compiler_params=pltpu.CompilerParams(vmem_limit_bytes=8 * MIB),
        name="pack",
    )(col[None], tile_ids, packed_tiles)


def join_kernel(*refs):
    for c, chunk in enumerate(refs[:-1]):
        refs[-1][c] = chunk[...]


def join(chunks):
    vmem = pl.BlockSpec(memory_space=pltpu.VMEM)
    return pl.pallas_call(
        join_kernel,
        out_shape=jax.ShapeDtypeStruct((len(chunks), *chunks[0].shape), chunks[0].dtype),
        in_specs=[vmem] * len(chunks),
        out_specs=vmem,
        compiler_params=pltpu.CompilerParams(vmem_limit_bytes=8 * MIB),
        name="join",
    )(*chunks)


def ladder_kernel(n_pieces, n_amps, capacity, where_ref, *refs):
    pieces = refs[:n_pieces]
    amps = refs[n_pieces : n_pieces + n_amps]
    residual, out = refs[n_pieces + n_amps : n_pieces + n_amps + 2]
    places, table, amp, block, total, table_sem, res_sem, out_sem = refs[
        n_pieces + n_amps + 2 :
    ]
    columns = pieces[0].shape[0]
    width = pieces[0].shape[2]
    per_device = KT_DEV * QT_DEV
    res_copy = pltpu.make_async_copy(residual, total, res_sem)
    res_copy.start()
    for p, piece in enumerate(pieces):
        rows = piece[:, capacity * width :, :]
        places[p * columns : (p + 1) * columns] = jnp.max(
            rows.astype(jnp.float32), axis=1
        ).astype(jnp.int32)
    table_copy = pltpu.make_async_copy(places, table, table_sem)
    table_copy.start()
    for a, source in enumerate(amps):
        column = where_ref[n_pieces + a]
        amp[:, pl.ds(pl.multiple_of(column * width, width), width)] = source[...]
    table_copy.wait()
    for p, piece in enumerate(pieces):
        row = where_ref[p]

        def place(c, _, p=p, piece=piece, row=row):
            for s in range(capacity):
                position = table[p * columns + c, s]
                k = row * KT_DEV + lax.shift_right_logical(position, QT_DEV.bit_length() - 1)
                q = position & (QT_DEV - 1)

                @pl.when(position < per_device)
                def _():
                    block[
                        pl.ds(pl.multiple_of(k * width, width), width),
                        pl.ds(pl.multiple_of(q * width, width), width),
                    ] = piece[c, s * width : (s + 1) * width, :]

            return 0

        lax.fori_loop(0, columns, place, 0)
    res_copy.wait()
    step = 2 * width
    outs = []
    for n in range(block.shape[1] // step):
        cols = slice(n * step, (n + 1) * step)
        total[:, cols] += jnp.dot(
            amp[...], block[:, cols], preferred_element_type=jnp.float32
        )
        copy = pltpu.make_async_copy(
            total.at[:, pl.ds(n * step, step)],
            out.at[:, pl.ds(n * step, step)],
            out_sem.at[n],
        )
        copy.start()
        outs.append(copy)
    for copy in outs:
        copy.wait()


def ladder(where, pieces, amps, residual, capacity):
    columns, _, width = pieces[0].shape
    n_pieces, n_amps = len(pieces), len(amps)
    rows, n_cols = residual.shape
    depth = n_amps * width
    any_spec = pl.BlockSpec(memory_space=pl.ANY)
    vmem = pl.BlockSpec(memory_space=pltpu.VMEM)
    held = sum(x.size * x.dtype.itemsize for x in (*pieces, *amps))
    held += 2 * rows * depth + 2 * depth * n_cols + 4 * rows * n_cols
    return pl.pallas_call(
        functools.partial(ladder_kernel, n_pieces, n_amps, capacity),
        out_shape=jax.ShapeDtypeStruct(residual.shape, residual.dtype),
        in_specs=[pl.BlockSpec(memory_space=pltpu.SMEM)]
        + [vmem] * (n_pieces + n_amps)
        + [any_spec],
        out_specs=any_spec,
        scratch_shapes=[
            pltpu.VMEM((n_pieces * columns, width), jnp.int32),
            pltpu.SMEM((n_pieces * columns, width), jnp.int32),
            pltpu.VMEM((rows, depth), jnp.bfloat16),
            pltpu.VMEM((depth, n_cols), jnp.bfloat16),
            pltpu.VMEM((rows, n_cols), jnp.float32),
            pltpu.SemaphoreType.DMA,
            pltpu.SemaphoreType.DMA,
            pltpu.SemaphoreType.DMA((n_cols // (2 * width),)),
        ],
        compiler_params=pltpu.CompilerParams(vmem_limit_bytes=held + 6 * MIB),
        name="ladder",
    )(where, *pieces, *amps, residual)


def exchange(x, axis, flip):
    size = lax.axis_size(axis)
    return lax.ppermute(x, axis, [(i, i ^ flip) for i in range(size)])


def body(amplitudes, packed_tiles, tile_ids, residual_in):
    n_col, n_row = lax.axis_size("col"), lax.axis_size("row")
    col, row = lax.axis_index("col"), lax.axis_index("row")
    inner = 2 ** (int(math.log2(n_col)) // 2)
    capacity = -(-packed_tiles.shape[1] // n_col)
    near = n_col // 2
    outgoing = pack(col, packed_tiles, tile_ids, n_col, capacity)
    chunks = [outgoing[0]] + [exchange(outgoing[s], "col", s) for s in range(1, n_col)]
    groups = [join(chunks[:near]), join(chunks[near:])]
    pieces, rows = [], []
    for group in groups:
        for flip in range(0, n_row, CORES):
            mine = exchange(group, "row", flip) if flip else group
            pieces += [mine, exchange(mine, "row", 1)]
            rows += [row ^ flip, row ^ flip ^ 1]
    shards, columns = [], []
    for flip in range(0, n_col, inner):
        shard = exchange(amplitudes, "col", flip) if flip else amplitudes
        for lane in range(inner):
            shards.append(exchange(shard, "col", lane) if lane else shard)
            columns.append(col ^ flip ^ lane)
    where = jnp.stack(rows + columns).astype(jnp.int32)
    return ladder(where, pieces, shards, residual_in, capacity)


def solution(mesh):
    in_specs = (P("row", "col"), P("row", "col", None, None), P("row", "col"), P("row", "col"))
    out_specs = P("row", "col")
    return jax.shard_map(body, mesh=mesh, in_specs=in_specs, out_specs=out_specs, check_vma=False)
```

```python
import functools
import math

import jax
import jax.numpy as jnp
from jax import lax
from jax.experimental import pallas as pl
from jax.experimental.pallas import tpu as pltpu
from jax.sharding import PartitionSpec as P

KT_DEV = 2
QT_DEV = 8
CORES = 2
META = 16
MIB = 1024 * 1024


def pack_kernel(columns, capacity, me_ref, ids_ref, tiles_ref, *refs):
    outs, slot_tile, slot_place, count = refs[:columns], *refs[columns:]
    per_device, width = tiles_ref.shape[1], tiles_ref.shape[2]
    shift = per_device.bit_length() - 1
    for d in range(columns):
        count[d] = 0
        for s in range(capacity):
            slot_place[d * capacity + s] = per_device
    for t in range(per_device):
        tile_id = ids_ref[0, t]
        target = lax.shift_right_logical(tile_id, shift)
        rank = count[target]
        count[target] = rank + 1
        slot_tile[target * capacity + rank] = t
        slot_place[target * capacity + rank] = tile_id & (per_device - 1)
    lane = lax.broadcasted_iota(jnp.int32, (META, width), 1)
    for d, out in enumerate(outs):
        target = me_ref[0] ^ d
        row = jnp.full((META, width), per_device, jnp.int32)
        for s in range(capacity):
            place = slot_place[target * capacity + s]
            row = jnp.where(lane == s, place, row)

            @pl.when(place < per_device)
            def _():
                out[s * width : (s + 1) * width, :] = tiles_ref[
                    0, slot_tile[target * capacity + s]
                ]

        out[capacity * width :, :] = row.astype(jnp.float32).astype(jnp.bfloat16)


def pack(col, packed_tiles, tile_ids, columns, capacity):
    _, per_device, width, _ = packed_tiles.shape
    chunk = jax.ShapeDtypeStruct((capacity * width + META, width), packed_tiles.dtype)
    smem = pl.BlockSpec(memory_space=pltpu.SMEM)
    vmem = pl.BlockSpec(memory_space=pltpu.VMEM)
    return pl.pallas_call(
        functools.partial(pack_kernel, columns, capacity),
        out_shape=[chunk] * columns,
        in_specs=[smem, smem, vmem],
        out_specs=[vmem] * columns,
        scratch_shapes=[
            pltpu.SMEM((columns * capacity,), jnp.int32),
            pltpu.SMEM((columns * capacity,), jnp.int32),
            pltpu.SMEM((columns,), jnp.int32),
        ],
        compiler_params=pltpu.CompilerParams(vmem_limit_bytes=8 * MIB),
        name="pack",
    )(col[None], tile_ids, packed_tiles)


def join_kernel(*refs):
    at = 0
    for part in refs[:-1]:
        refs[-1][at : at + part.shape[0]] = part[...]
        at += part.shape[0]


def join(chunks):
    vmem = pl.BlockSpec(memory_space=pltpu.VMEM)
    total = sum(c.shape[0] for c in chunks)
    return pl.pallas_call(
        join_kernel,
        out_shape=jax.ShapeDtypeStruct((total, *chunks[0].shape[1:]), chunks[0].dtype),
        in_specs=[vmem] * len(chunks),
        out_specs=vmem,
        compiler_params=pltpu.CompilerParams(vmem_limit_bytes=8 * MIB),
        name="join",
    )(*chunks)


def ladder_kernel(n_pieces, offsets, capacity, where_ref, *refs):
    n_amps = len(offsets)
    pieces = refs[:n_pieces]
    amps = refs[n_pieces : n_pieces + n_amps]
    residual, out = refs[n_pieces + n_amps : n_pieces + n_amps + 2]
    places, table, amp, block, total, table_sem, res_sem, out_sem = refs[
        n_pieces + n_amps + 2 :
    ]
    columns = pieces[0].shape[0]
    width = pieces[0].shape[2]
    per_device = KT_DEV * QT_DEV
    res_copy = pltpu.make_async_copy(residual, total, res_sem)
    res_copy.start()
    for p, piece in enumerate(pieces):
        rows = piece[:, capacity * width :, :]
        places[p * columns : (p + 1) * columns] = jnp.max(
            rows.astype(jnp.float32), axis=1
        ).astype(jnp.int32)
    table_copy = pltpu.make_async_copy(places, table, table_sem)
    table_copy.start()
    for source, slots in zip(amps, offsets):
        for i, slot in enumerate(slots):
            amp[:, slot * width : (slot + 1) * width] = source[i]
    table_copy.wait()
    col = where_ref[n_pieces]
    for p, piece in enumerate(pieces):
        row = where_ref[p]

        def place(c, _, p=p, piece=piece, row=row):
            for s in range(capacity):
                position = table[p * columns + c, s]
                k = row * KT_DEV + lax.shift_right_logical(position, QT_DEV.bit_length() - 1)
                q = position & (QT_DEV - 1)

                @pl.when(position < per_device)
                def _():
                    block[
                        pl.ds(pl.multiple_of((k ^ col) * width, width), width),
                        pl.ds(pl.multiple_of(q * width, width), width),
                    ] = piece[c, s * width : (s + 1) * width, :]

            return 0

        lax.fori_loop(0, columns, place, 0)
    res_copy.wait()
    step = 2 * width
    outs = []
    for n in range(block.shape[1] // step):
        cols = slice(n * step, (n + 1) * step)
        total[:, cols] += jnp.dot(
            amp[...], block[:, cols], preferred_element_type=jnp.float32
        )
        copy = pltpu.make_async_copy(
            total.at[:, pl.ds(n * step, step)],
            out.at[:, pl.ds(n * step, step)],
            out_sem.at[n],
        )
        copy.start()
        outs.append(copy)
    for copy in outs:
        copy.wait()


def ladder(where, pieces, amps, offsets, residual, capacity):
    columns, _, width = pieces[0].shape
    n_pieces, n_amps = len(pieces), len(amps)
    rows, n_cols = residual.shape
    depth = sum(map(len, offsets)) * width
    hbm = pl.BlockSpec(memory_space=pltpu.HBM)
    vmem = pl.BlockSpec(memory_space=pltpu.VMEM)
    held = sum(x.size * x.dtype.itemsize for x in (*pieces, *amps))
    held += 2 * rows * depth + 2 * depth * n_cols + 4 * rows * n_cols
    return pl.pallas_call(
        functools.partial(ladder_kernel, n_pieces, offsets, capacity),
        out_shape=jax.ShapeDtypeStruct(residual.shape, residual.dtype),
        in_specs=[pl.BlockSpec(memory_space=pltpu.SMEM)]
        + [vmem] * (n_pieces + n_amps)
        + [hbm],
        out_specs=hbm,
        scratch_shapes=[
            pltpu.VMEM((n_pieces * columns, width), jnp.int32),
            pltpu.SMEM((n_pieces * columns, width), jnp.int32),
            pltpu.VMEM((rows, depth), jnp.bfloat16),
            pltpu.VMEM((depth, n_cols), jnp.bfloat16),
            pltpu.VMEM((rows, n_cols), jnp.float32),
            pltpu.SemaphoreType.DMA,
            pltpu.SemaphoreType.DMA,
            pltpu.SemaphoreType.DMA((n_cols // (2 * width),)),
        ],
        compiler_params=pltpu.CompilerParams(vmem_limit_bytes=held + 6 * MIB),
        name="ladder",
    )(where, *pieces, *amps, residual)


def exchange(x, axis, flip):
    size = lax.axis_size(axis)
    return lax.ppermute(x, axis, [(i, i ^ flip) for i in range(size)])


def gather_amps(amplitudes, n_col, inner):
    held, slots = [amplitudes[None]], [[0]]
    flip = inner
    while flip < n_col:
        if len(held) > 1:
            held = [join(held)]
            slots = [sum(slots, [])]
        held.append(exchange(held[0], "col", flip))
        slots.append([s ^ flip for s in slots[0]])
        if flip == inner:
            held, slots = [join(held)], [sum(slots, [])]
        flip *= 2
    for lane in range(1, inner):
        for group in range(len(held)):
            held.append(exchange(held[group], "col", lane))
            slots.append([s ^ lane for s in slots[group]])
    return held, slots


def body(amplitudes, packed_tiles, tile_ids, residual_in):
    n_col, n_row = lax.axis_size("col"), lax.axis_size("row")
    col, row = lax.axis_index("col"), lax.axis_index("row")
    inner = 2 ** (int(math.log2(n_col)) // 2)
    capacity = -(-packed_tiles.shape[1] // n_col)
    near = n_col // 2
    outgoing = pack(col, packed_tiles, tile_ids, n_col, capacity)
    chunks = [outgoing[0][None]]
    chunks += [exchange(outgoing[s][None], "col", s) for s in range(1, n_col)]
    shards, slots = gather_amps(amplitudes, n_col, inner)
    groups = [join(chunks[near:]), join(chunks[:near])]
    pieces, rows = [], []
    for group in groups:
        for flip in range(0, n_row, CORES):
            mine = exchange(group, "row", flip) if flip else group
            pieces += [mine, exchange(mine, "row", 1)]
            rows += [row ^ flip, row ^ flip ^ 1]
    where = jnp.stack(rows + [col]).astype(jnp.int32)
    return ladder(where, pieces, shards, slots, residual_in, capacity)


def solution(mesh):
    in_specs = (P("row", "col"), P("row", "col", None, None), P("row", "col"), P("row", "col"))
    out_specs = P("row", "col")
    return jax.shard_map(body, mesh=mesh, in_specs=in_specs, out_specs=out_specs, check_vma=False)
```

```python
import functools
import math

import jax
import jax.numpy as jnp
from jax import lax
from jax.experimental import pallas as pl
from jax.experimental.pallas import tpu as pltpu
from jax.sharding import PartitionSpec as P

KT_DEV = 2
QT_DEV = 8
CORES = 2
META = 16
MIB = 1024 * 1024


def pack_kernel(columns, capacity, me_ref, ids_hbm, tiles_hbm, *refs):
    outs = refs[:columns]
    ids_ref, tiles_ref, slot_tile, slot_place, count, ids_sem, tiles_sem = refs[columns:]
    ids_copy = pltpu.make_async_copy(ids_hbm, ids_ref, ids_sem)
    tiles_copy = pltpu.make_async_copy(tiles_hbm, tiles_ref, tiles_sem)
    ids_copy.start()
    tiles_copy.start()
    per_device, width = tiles_ref.shape[1], tiles_ref.shape[2]
    shift = per_device.bit_length() - 1
    for d in range(columns):
        count[d] = 0
        for s in range(capacity):
            slot_place[d * capacity + s] = per_device
    ids_copy.wait()
    for t in range(per_device):
        tile_id = ids_ref[0, t]
        target = lax.shift_right_logical(tile_id, shift)
        rank = count[target]
        count[target] = rank + 1
        slot_tile[target * capacity + rank] = t
        slot_place[target * capacity + rank] = tile_id & (per_device - 1)
    tiles_copy.wait()
    lane = lax.broadcasted_iota(jnp.int32, (META, width), 1)
    for d, out in enumerate(outs):
        target = me_ref[0] ^ d
        row = jnp.full((META, width), per_device, jnp.int32)
        for s in range(capacity):
            place = slot_place[target * capacity + s]
            row = jnp.where(lane == s, place, row)

            @pl.when(place < per_device)
            def _():
                out[s * width : (s + 1) * width, :] = tiles_ref[
                    0, slot_tile[target * capacity + s]
                ]

        out[capacity * width :, :] = row.astype(jnp.float32).astype(jnp.bfloat16)


def pack(col, packed_tiles, tile_ids, columns, capacity):
    _, per_device, width, _ = packed_tiles.shape
    chunk = jax.ShapeDtypeStruct((capacity * width + META, width), packed_tiles.dtype)
    smem = pl.BlockSpec(memory_space=pltpu.SMEM)
    vmem = pl.BlockSpec(memory_space=pltpu.VMEM)
    hbm = pl.BlockSpec(memory_space=pltpu.HBM)
    return pl.pallas_call(
        functools.partial(pack_kernel, columns, capacity),
        out_shape=[chunk] * columns,
        in_specs=[smem, hbm, hbm],
        out_specs=[vmem] * columns,
        scratch_shapes=[
            pltpu.SMEM(tile_ids.shape, jnp.int32),
            pltpu.VMEM(packed_tiles.shape, packed_tiles.dtype),
            pltpu.SMEM((columns * capacity,), jnp.int32),
            pltpu.SMEM((columns * capacity,), jnp.int32),
            pltpu.SMEM((columns,), jnp.int32),
            pltpu.SemaphoreType.DMA,
            pltpu.SemaphoreType.DMA,
        ],
        compiler_params=pltpu.CompilerParams(vmem_limit_bytes=8 * MIB),
        name="pack",
    )(col[None], tile_ids, packed_tiles)


def join_kernel(*refs):
    at = 0
    for part in refs[:-1]:
        refs[-1][at : at + part.shape[0]] = part[...]
        at += part.shape[0]


def join(chunks):
    vmem = pl.BlockSpec(memory_space=pltpu.VMEM)
    total = sum(c.shape[0] for c in chunks)
    return pl.pallas_call(
        join_kernel,
        out_shape=jax.ShapeDtypeStruct((total, *chunks[0].shape[1:]), chunks[0].dtype),
        in_specs=[vmem] * len(chunks),
        out_specs=vmem,
        compiler_params=pltpu.CompilerParams(vmem_limit_bytes=8 * MIB),
        name="join",
    )(*chunks)


def multiply(amp, block, start, out, sems, step):
    copies = []
    for n in range(block.shape[1] // step):
        cols = slice(n * step, (n + 1) * step)
        held = out[0] if sems is not None else out
        held[:, cols] = start[:, cols] + jnp.dot(
            amp[...], block[:, cols], preferred_element_type=jnp.float32
        )
        if sems is not None:
            part = pl.ds(n * step, step)
            copies.append(
                pltpu.make_async_copy(held.at[:, part], out[1].at[:, part], sems.at[n])
            )
            copies[-1].start()
    for copy in copies:
        copy.wait()


def near_kernel(n_pieces, offsets, capacity, where_ref, *refs):
    n_amps = len(offsets)
    pieces = refs[:n_pieces]
    amps = refs[n_pieces : n_pieces + n_amps]
    residual, total, far = refs[n_pieces + n_amps : n_pieces + n_amps + 3]
    places, table, amp, near, res, table_sem, res_sem = refs[n_pieces + n_amps + 3 :]
    columns = pieces[0].shape[0]
    width = pieces[0].shape[2]
    per_device = KT_DEV * QT_DEV
    half = amp.shape[1] // width
    res_copy = pltpu.make_async_copy(residual, res, res_sem)
    res_copy.start()
    for p, piece in enumerate(pieces):
        rows = piece[:, capacity * width :, :]
        places[p * columns : (p + 1) * columns] = jnp.max(
            rows.astype(jnp.float32), axis=1
        ).astype(jnp.int32)
    table_copy = pltpu.make_async_copy(places, table, table_sem)
    table_copy.start()
    for source, slots in zip(amps, offsets):
        for i, slot in enumerate(slots):
            amp[:, slot * width : (slot + 1) * width] = source[i]
    table_copy.wait()
    col = where_ref[n_pieces]
    for p, piece in enumerate(pieces):
        row = where_ref[p]

        def place(c, _, p=p, piece=piece, row=row):
            for s in range(capacity):
                position = table[p * columns + c, s]
                k = row * KT_DEV + lax.shift_right_logical(position, QT_DEV.bit_length() - 1)
                slot = k ^ col
                q = pl.multiple_of((position & (QT_DEV - 1)) * width, width)
                at = pl.multiple_of((slot & (half - 1)) * width, width)
                tile = piece.at[c, pl.ds(s * width, width), :]

                @pl.when((position < per_device) & (slot < half))
                def _():
                    near[pl.ds(at, width), pl.ds(q, width)] = tile[...]

                @pl.when((position < per_device) & (slot >= half))
                def _():
                    far[pl.ds(at, width), pl.ds(q, width)] = tile[...]

            return 0

        lax.fori_loop(0, columns, place, 0)
    res_copy.wait()
    multiply(amp, near, res, total, None, 2 * width)


def near_half(where, pieces, amps, offsets, residual, capacity):
    columns, _, width = pieces[0].shape
    n_pieces, n_amps = len(pieces), len(amps)
    rows, n_cols = residual.shape
    depth = sum(map(len, offsets)) * width
    hbm = pl.BlockSpec(memory_space=pltpu.HBM)
    vmem = pl.BlockSpec(memory_space=pltpu.VMEM)
    held = 2 * rows * depth + 4 * depth * n_cols + 8 * rows * n_cols
    held += sum(x.size * x.dtype.itemsize for x in pieces) // 2
    return pl.pallas_call(
        functools.partial(near_kernel, n_pieces, offsets, capacity),
        out_shape=[
            jax.ShapeDtypeStruct(residual.shape, residual.dtype),
            jax.ShapeDtypeStruct((depth, n_cols), pieces[0].dtype),
        ],
        in_specs=[pl.BlockSpec(memory_space=pltpu.SMEM)]
        + [vmem] * (n_pieces + n_amps)
        + [hbm],
        out_specs=[vmem, vmem],
        scratch_shapes=[
            pltpu.VMEM((n_pieces * columns, width), jnp.int32),
            pltpu.SMEM((n_pieces * columns, width), jnp.int32),
            pltpu.VMEM((rows, depth), pieces[0].dtype),
            pltpu.VMEM((depth, n_cols), pieces[0].dtype),
            pltpu.VMEM((rows, n_cols), residual.dtype),
            pltpu.SemaphoreType.DMA,
            pltpu.SemaphoreType.DMA,
        ],
        compiler_params=pltpu.CompilerParams(vmem_limit_bytes=held + 2 * MIB),
        cost_estimate=pl.CostEstimate(
            flops=2 * rows * depth * n_cols,
            bytes_accessed=16 * rows * n_cols,
            transcendentals=0,
        ),
        name="near_half",
    )(where, *pieces, *amps, residual)


def far_kernel(offsets, half, *refs):
    amps = refs[: len(offsets)]
    start, far, out, amp, total, sems = refs[len(offsets) :]
    width = amps[0].shape[2]
    for source, slots in zip(amps, offsets):
        for i, slot in enumerate(slots):
            at = (slot - half) * width
            amp[:, at : at + width] = source[i]
    multiply(amp, far, start, (total, out), sems, 2 * width)


def far_half(amps, offsets, total, far):
    rows, n_cols = total.shape
    depth, width = far.shape[0], amps[0].shape[2]
    vmem = pl.BlockSpec(memory_space=pltpu.VMEM)
    held = 4 * rows * depth + 2 * depth * n_cols + 8 * rows * n_cols
    return pl.pallas_call(
        functools.partial(far_kernel, offsets, depth // width),
        out_shape=jax.ShapeDtypeStruct(total.shape, total.dtype),
        in_specs=[vmem] * (len(amps) + 2),
        out_specs=pl.BlockSpec(memory_space=pltpu.HBM),
        scratch_shapes=[
            pltpu.VMEM((rows, depth), far.dtype),
            pltpu.VMEM((rows, n_cols), total.dtype),
            pltpu.SemaphoreType.DMA((n_cols // (2 * width),)),
        ],
        compiler_params=pltpu.CompilerParams(vmem_limit_bytes=held + 2 * MIB),
        cost_estimate=pl.CostEstimate(
            flops=2 * rows * depth * n_cols,
            bytes_accessed=16 * rows * n_cols,
            transcendentals=0,
        ),
        name="far_half",
    )(*amps, total, far)


def exchange(x, axis, flip):
    size = lax.axis_size(axis)
    return lax.ppermute(x, axis, [(i, i ^ flip) for i in range(size)])


def over_lanes(shard, slots, inner):
    held = [(shard, slots)]
    for lane in range(1, inner):
        held.append((exchange(shard, "col", lane), [s ^ lane for s in slots]))
    return held


def body(amplitudes, packed_tiles, tile_ids, residual_in):
    n_col, n_row = lax.axis_size("col"), lax.axis_size("row")
    col, row = lax.axis_index("col"), lax.axis_index("row")
    inner = 2 ** (int(math.log2(n_col)) // 2)
    capacity = -(-packed_tiles.shape[1] // n_col)
    half = n_col // 2
    outgoing = list(pack(col, packed_tiles, tile_ids, n_col, capacity))
    flips = range(inner, half, inner)
    held = [amplitudes[None]] + [exchange(amplitudes[None], "col", f) for f in flips]
    outgoing[half:], held = lax.optimization_barrier((outgoing[half:], held))
    chunks = [outgoing[0][None]]
    chunks += [exchange(outgoing[s][None], "col", s) for s in range(1, n_col)]
    slots = [0, *flips]
    passed = [exchange(shard, "col", half) for shard in held]
    near = over_lanes(join(held), slots, inner)
    pieces, rows = [], []
    for group in (join(chunks[half:]), join(chunks[:half])):
        for flip in range(0, n_row, CORES):
            mine = exchange(group, "row", flip) if flip else group
            if flip == CORES and len(pieces) > CORES:
                mine, passed[0] = lax.optimization_barrier((mine, passed[0]))
            pieces += [mine, exchange(mine, "row", 1)]
            rows += [row ^ flip, row ^ flip ^ 1]
    far = []
    for shard, slot in zip(passed, slots):
        far += over_lanes(shard, [slot ^ half], inner)
    where = jnp.stack(rows + [col]).astype(jnp.int32)
    total, far_block = near_half(where, pieces, *zip(*near), residual_in, capacity)
    return far_half(*zip(*far), total, far_block)


def solution(mesh):
    in_specs = (P("row", "col"), P("row", "col", None, None), P("row", "col"), P("row", "col"))
    out_specs = P("row", "col")
    return jax.shard_map(body, mesh=mesh, in_specs=in_specs, out_specs=out_specs, check_vma=False)
```

```python
import functools
import math

import jax
import jax.numpy as jnp
from jax import lax
from jax.experimental import pallas as pl
from jax.experimental.pallas import tpu as pltpu
from jax.sharding import PartitionSpec as P

KT_DEV = 2
QT_DEV = 8
CORES = 2
META = 16
MIB = 1024 * 1024


def pack_kernel(columns, capacity, me_ref, ids_hbm, tiles_hbm, *refs):
    outs = refs[:columns]
    ids_ref, tiles_ref, slot_tile, slot_place, count, ids_sem, tiles_sem = refs[columns:]
    ids_copy = pltpu.make_async_copy(ids_hbm, ids_ref, ids_sem)
    tiles_copy = pltpu.make_async_copy(tiles_hbm, tiles_ref, tiles_sem)
    ids_copy.start()
    tiles_copy.start()
    per_device, width = tiles_ref.shape[1], tiles_ref.shape[2]
    shift = per_device.bit_length() - 1
    for d in range(columns):
        count[d] = 0
        for s in range(capacity):
            slot_place[d * capacity + s] = per_device
    ids_copy.wait()
    for t in range(per_device):
        tile_id = ids_ref[0, t]
        target = lax.shift_right_logical(tile_id, shift)
        rank = count[target]
        count[target] = rank + 1
        slot_tile[target * capacity + rank] = t
        slot_place[target * capacity + rank] = tile_id & (per_device - 1)
    tiles_copy.wait()
    lane = lax.broadcasted_iota(jnp.int32, (META, width), 1)
    for d, out in enumerate(outs):
        target = me_ref[0] ^ d
        row = jnp.full((META, width), per_device, jnp.int32)
        for s in range(capacity):
            place = slot_place[target * capacity + s]
            row = jnp.where(lane == s, place, row)

            @pl.when(place < per_device)
            def _():
                out[s * width : (s + 1) * width, :] = tiles_ref[
                    0, slot_tile[target * capacity + s]
                ]

        out[capacity * width :, :] = row.astype(jnp.float32).astype(jnp.bfloat16)


def pack(col, packed_tiles, tile_ids, columns, capacity):
    _, per_device, width, _ = packed_tiles.shape
    chunk = jax.ShapeDtypeStruct((capacity * width + META, width), packed_tiles.dtype)
    smem = pl.BlockSpec(memory_space=pltpu.SMEM)
    vmem = pl.BlockSpec(memory_space=pltpu.VMEM)
    hbm = pl.BlockSpec(memory_space=pltpu.HBM)
    return pl.pallas_call(
        functools.partial(pack_kernel, columns, capacity),
        out_shape=[chunk] * columns,
        in_specs=[smem, hbm, hbm],
        out_specs=[vmem] * columns,
        scratch_shapes=[
            pltpu.SMEM(tile_ids.shape, jnp.int32),
            pltpu.VMEM(packed_tiles.shape, packed_tiles.dtype),
            pltpu.SMEM((columns * capacity,), jnp.int32),
            pltpu.SMEM((columns * capacity,), jnp.int32),
            pltpu.SMEM((columns,), jnp.int32),
            pltpu.SemaphoreType.DMA,
            pltpu.SemaphoreType.DMA,
        ],
        compiler_params=pltpu.CompilerParams(vmem_limit_bytes=8 * MIB),
        name="pack",
    )(
        col[None],
        pltpu.with_memory_space_constraint(tile_ids, pltpu.HBM),
        pltpu.with_memory_space_constraint(packed_tiles, pltpu.HBM),
    )


def join_kernel(*refs):
    at = 0
    for part in refs[:-1]:
        refs[-1][at : at + part.shape[0]] = part[...]
        at += part.shape[0]


def join(chunks):
    vmem = pl.BlockSpec(memory_space=pltpu.VMEM)
    total = sum(c.shape[0] for c in chunks)
    return pl.pallas_call(
        join_kernel,
        out_shape=jax.ShapeDtypeStruct((total, *chunks[0].shape[1:]), chunks[0].dtype),
        in_specs=[vmem] * len(chunks),
        out_specs=vmem,
        compiler_params=pltpu.CompilerParams(vmem_limit_bytes=8 * MIB),
        name="join",
    )(*chunks)


def multiply(amp, block, start, out, sems, step):
    copies = []
    for n in range(block.shape[1] // step):
        cols = slice(n * step, (n + 1) * step)
        held = out[0] if sems is not None else out
        held[:, cols] = start[:, cols] + jnp.dot(
            amp[...], block[:, cols], preferred_element_type=jnp.float32
        )
        if sems is not None:
            part = pl.ds(n * step, step)
            copies.append(
                pltpu.make_async_copy(held.at[:, part], out[1].at[:, part], sems.at[n])
            )
            copies[-1].start()
    for copy in copies:
        copy.wait()


def near_kernel(n_pieces, offsets, capacity, where_ref, *refs):
    n_amps = len(offsets)
    pieces = refs[:n_pieces]
    amps = refs[n_pieces : n_pieces + n_amps]
    own, residual, total, far = refs[n_pieces + n_amps : n_pieces + n_amps + 4]
    places, table, amp, near, res, table_sem, own_sem, res_sem = refs[n_pieces + n_amps + 4 :]
    columns = pieces[0].shape[0]
    width = pieces[0].shape[2]
    per_device = KT_DEV * QT_DEV
    half = amp.shape[1] // width
    own_copy = pltpu.make_async_copy(own, amp.at[:, pl.ds(0, width)], own_sem)
    own_copy.start()
    res_copy = pltpu.make_async_copy(residual, res, res_sem)
    res_copy.start()
    for p, piece in enumerate(pieces):
        rows = piece[:, capacity * width :, :]
        places[p * columns : (p + 1) * columns] = jnp.max(
            rows.astype(jnp.float32), axis=1
        ).astype(jnp.int32)
    table_copy = pltpu.make_async_copy(places, table, table_sem)
    table_copy.start()
    for source, slot in zip(amps, offsets):
        amp[:, slot * width : (slot + 1) * width] = source[...]
    table_copy.wait()
    col = where_ref[n_pieces]
    for p, piece in enumerate(pieces):
        row = where_ref[p]

        def place(c, _, p=p, piece=piece, row=row):
            for s in range(capacity):
                position = table[p * columns + c, s]
                k = row * KT_DEV + lax.shift_right_logical(position, QT_DEV.bit_length() - 1)
                slot = k ^ col
                q = pl.multiple_of((position & (QT_DEV - 1)) * width, width)
                at = pl.multiple_of((slot & (half - 1)) * width, width)
                tile = piece.at[c, pl.ds(s * width, width), :]

                @pl.when((position < per_device) & (slot < half))
                def _():
                    near[pl.ds(at, width), pl.ds(q, width)] = tile[...]

                @pl.when((position < per_device) & (slot >= half))
                def _():
                    far[pl.ds(at, width), pl.ds(q, width)] = tile[...]

            return 0

        lax.fori_loop(0, columns, place, 0)
    own_copy.wait()
    res_copy.wait()
    multiply(amp, near, res, total, None, 2 * width)


def near_half(where, pieces, amps, offsets, own, residual, capacity):
    columns, _, width = pieces[0].shape
    n_pieces, n_amps = len(pieces), len(amps)
    rows, n_cols = residual.shape
    depth = (1 + n_amps) * width
    hbm = pl.BlockSpec(memory_space=pltpu.HBM)
    vmem = pl.BlockSpec(memory_space=pltpu.VMEM)
    held = 2 * rows * depth + 4 * depth * n_cols + 8 * rows * n_cols
    held += sum(x.size * x.dtype.itemsize for x in pieces) // 2
    return pl.pallas_call(
        functools.partial(near_kernel, n_pieces, offsets, capacity),
        out_shape=[
            jax.ShapeDtypeStruct(residual.shape, residual.dtype),
            jax.ShapeDtypeStruct((depth, n_cols), pieces[0].dtype),
        ],
        in_specs=[pl.BlockSpec(memory_space=pltpu.SMEM)]
        + [vmem] * (n_pieces + n_amps)
        + [hbm, hbm],
        out_specs=[vmem, vmem],
        scratch_shapes=[
            pltpu.VMEM((n_pieces * columns, width), jnp.int32),
            pltpu.SMEM((n_pieces * columns, width), jnp.int32),
            pltpu.VMEM((rows, depth), pieces[0].dtype),
            pltpu.VMEM((depth, n_cols), pieces[0].dtype),
            pltpu.VMEM((rows, n_cols), residual.dtype),
            pltpu.SemaphoreType.DMA,
            pltpu.SemaphoreType.DMA,
            pltpu.SemaphoreType.DMA,
        ],
        compiler_params=pltpu.CompilerParams(vmem_limit_bytes=held + 2 * MIB),
        cost_estimate=pl.CostEstimate(
            flops=2 * rows * depth * n_cols,
            bytes_accessed=16 * rows * n_cols,
            transcendentals=0,
        ),
        name="near_half",
    )(
        where,
        *pieces,
        *amps,
        pltpu.with_memory_space_constraint(own, pltpu.HBM),
        pltpu.with_memory_space_constraint(residual, pltpu.HBM),
    )


def far_kernel(offsets, half, *refs):
    amps = refs[: len(offsets)]
    start, far, out, amp, total, sems = refs[len(offsets) :]
    width = amps[0].shape[1]
    for source, slot in zip(amps, offsets):
        at = (slot - half) * width
        amp[:, at : at + width] = source[...]
    multiply(amp, far, start, (total, out), sems, 2 * width)


def far_half(amps, offsets, total, far):
    rows, n_cols = total.shape
    depth, width = far.shape[0], amps[0].shape[1]
    vmem = pl.BlockSpec(memory_space=pltpu.VMEM)
    held = 4 * rows * depth + 2 * depth * n_cols + 8 * rows * n_cols
    return pl.pallas_call(
        functools.partial(far_kernel, offsets, depth // width),
        out_shape=jax.ShapeDtypeStruct(total.shape, total.dtype),
        in_specs=[vmem] * (len(amps) + 2),
        out_specs=pl.BlockSpec(memory_space=pltpu.HBM),
        scratch_shapes=[
            pltpu.VMEM((rows, depth), far.dtype),
            pltpu.VMEM((rows, n_cols), total.dtype),
            pltpu.SemaphoreType.DMA((n_cols // (2 * width),)),
        ],
        compiler_params=pltpu.CompilerParams(vmem_limit_bytes=held + 2 * MIB),
        cost_estimate=pl.CostEstimate(
            flops=2 * rows * depth * n_cols,
            bytes_accessed=16 * rows * n_cols,
            transcendentals=0,
        ),
        name="far_half",
    )(*amps, total, far)


def exchange(x, axis, flip):
    size = lax.axis_size(axis)
    return lax.ppermute(x, axis, [(i, i ^ flip) for i in range(size)])


def tie(late, *early):
    return lax.optimization_barrier((late, *early))


def body(amplitudes, packed_tiles, tile_ids, residual_in):
    n_col, n_row = lax.axis_size("col"), lax.axis_size("row")
    col, row = lax.axis_index("col"), lax.axis_index("row")
    inner = 2 ** (int(math.log2(n_col)) // 2)
    capacity = -(-packed_tiles.shape[1] // n_col)
    half = n_col // 2
    outgoing = list(pack(col, packed_tiles, tile_ids, n_col, capacity))

    amps = {0: amplitudes}
    for s in [*range(1, inner), *range(inner, half, inner), half]:
        amps[s] = exchange(amplitudes, "col", s)
    outgoing[half:], amps = tie(outgoing[half:], amps)

    chunks = [outgoing[0][None]]
    chunks += [exchange(outgoing[s][None], "col", s) for s in range(1, n_col)]
    for flip in range(inner, half, inner):
        for lane in range(1, inner):
            amps[flip ^ lane] = exchange(amps[flip], "col", lane)
        amps[flip ^ half] = exchange(amps[flip], "col", half)
    for lane in range(1, inner):
        amps[half ^ lane] = exchange(amps[half], "col", lane)

    early = [s for s in amps if s and (s < half or half < s < half + inner)]
    late = [flip ^ half for flip in range(inner, half, inner)]
    pieces, rows = [], []
    for group in (join(chunks[half:]), join(chunks[:half])):
        passed = [exchange(group, "row", flip) for flip in range(CORES, n_row, CORES)]
        due = late if pieces else early
        passed, got = tie(passed, [amps[s] for s in due])
        amps.update(zip(due, got))
        own, passed = tie(group, passed)
        for flip, mine in zip(range(0, n_row, CORES), [own, *passed]):
            pieces += [mine, exchange(mine, "row", 1)]
            rows += [row ^ flip, row ^ flip ^ 1]
    for flip in range(half + inner, n_col, inner):
        for lane in range(1, inner):
            amps[flip ^ lane] = exchange(amps[flip], "col", lane)

    where = jnp.stack(rows + [col]).astype(jnp.int32)
    near = [s for s in sorted(amps) if 0 < s < half]
    far = [s for s in sorted(amps) if s >= half]
    total, far_block = near_half(
        where, pieces, [amps[s] for s in near], near, amplitudes, residual_in, capacity
    )
    return far_half([amps[s] for s in far], far, total, far_block)


def solution(mesh):
    in_specs = (P("row", "col"), P("row", "col", None, None), P("row", "col"), P("row", "col"))
    out_specs = P("row", "col")
    return jax.shard_map(body, mesh=mesh, in_specs=in_specs, out_specs=out_specs, check_vma=False)
```

```python
import functools
import math

import jax
import jax.numpy as jnp
from jax import lax
from jax.experimental import pallas as pl
from jax.experimental.pallas import tpu as pltpu
from jax.sharding import PartitionSpec as P

KT_DEV = 2
QT_DEV = 8
CORES = 2
META = 16
MIB = 1024 * 1024


def pack_kernel(columns, capacity, me_ref, ids_hbm, tiles_hbm, *refs):
    outs = refs[:columns]
    ids_ref, tiles_ref, slot_tile, slot_place, count, ids_sem, tiles_sem = refs[columns:]
    ids_copy = pltpu.make_async_copy(ids_hbm, ids_ref, ids_sem)
    tiles_copy = pltpu.make_async_copy(tiles_hbm, tiles_ref, tiles_sem)
    ids_copy.start()
    tiles_copy.start()
    per_device, width = tiles_ref.shape[1], tiles_ref.shape[2]
    shift = per_device.bit_length() - 1
    for d in range(columns):
        count[d] = 0
        for s in range(capacity):
            slot_place[d * capacity + s] = per_device
    ids_copy.wait()
    for t in range(per_device):
        tile_id = ids_ref[0, t]
        target = lax.shift_right_logical(tile_id, shift)
        rank = count[target]
        count[target] = rank + 1
        slot_tile[target * capacity + rank] = t
        slot_place[target * capacity + rank] = tile_id & (per_device - 1)
    tiles_copy.wait()
    lane = lax.broadcasted_iota(jnp.int32, (META, width), 1)
    for d, out in enumerate(outs):
        target = me_ref[0] ^ d
        row = jnp.full((META, width), per_device, jnp.int32)
        for s in range(capacity):
            place = slot_place[target * capacity + s]
            row = jnp.where(lane == s, place, row)

            @pl.when(place < per_device)
            def _():
                out[s * width : (s + 1) * width, :] = tiles_ref[
                    0, slot_tile[target * capacity + s]
                ]

        out[capacity * width :, :] = row.astype(jnp.float32).astype(jnp.bfloat16)


def pack(col, packed_tiles, tile_ids, columns, capacity):
    _, per_device, width, _ = packed_tiles.shape
    chunk = jax.ShapeDtypeStruct((capacity * width + META, width), packed_tiles.dtype)
    smem = pl.BlockSpec(memory_space=pltpu.SMEM)
    vmem = pl.BlockSpec(memory_space=pltpu.VMEM)
    hbm = pl.BlockSpec(memory_space=pltpu.HBM)
    return pl.pallas_call(
        functools.partial(pack_kernel, columns, capacity),
        out_shape=[chunk] * columns,
        in_specs=[smem, hbm, hbm],
        out_specs=[vmem] * columns,
        scratch_shapes=[
            pltpu.SMEM(tile_ids.shape, jnp.int32),
            pltpu.VMEM(packed_tiles.shape, packed_tiles.dtype),
            pltpu.SMEM((columns * capacity,), jnp.int32),
            pltpu.SMEM((columns * capacity,), jnp.int32),
            pltpu.SMEM((columns,), jnp.int32),
            pltpu.SemaphoreType.DMA,
            pltpu.SemaphoreType.DMA,
        ],
        compiler_params=pltpu.CompilerParams(vmem_limit_bytes=8 * MIB),
        name="pack",
    )(
        col[None],
        pltpu.with_memory_space_constraint(tile_ids, pltpu.HBM),
        pltpu.with_memory_space_constraint(packed_tiles, pltpu.HBM),
    )


def join_kernel(*refs):
    at = 0
    for part in refs[:-1]:
        refs[-1][at : at + part.shape[0]] = part[...]
        at += part.shape[0]


def join(chunks):
    vmem = pl.BlockSpec(memory_space=pltpu.VMEM)
    total = sum(c.shape[0] for c in chunks)
    return pl.pallas_call(
        join_kernel,
        out_shape=jax.ShapeDtypeStruct((total, *chunks[0].shape[1:]), chunks[0].dtype),
        in_specs=[vmem] * len(chunks),
        out_specs=vmem,
        compiler_params=pltpu.CompilerParams(vmem_limit_bytes=8 * MIB),
        name="join",
    )(*chunks)


def multiply(amp, block, start, out, sems, step):
    copies = []
    for n in range(block.shape[1] // step):
        cols = slice(n * step, (n + 1) * step)
        held = out[0] if sems is not None else out
        held[:, cols] = start[:, cols] + jnp.dot(
            amp[...], block[:, cols], preferred_element_type=jnp.float32
        )
        if sems is not None:
            part = pl.ds(n * step, step)
            copies.append(
                pltpu.make_async_copy(held.at[:, part], out[1].at[:, part], sems.at[n])
            )
            copies[-1].start()
    for copy in copies:
        copy.wait()


def near_kernel(n_pieces, n_amps, capacity, where_ref, *refs):
    pieces = refs[:n_pieces]
    amps = refs[n_pieces : n_pieces + n_amps]
    own, residual, total, far = refs[n_pieces + n_amps : n_pieces + n_amps + 4]
    places, table, amp, near, res, table_sem, own_sem, res_sem = refs[n_pieces + n_amps + 4 :]
    columns = pieces[0].shape[0]
    width = pieces[0].shape[2]
    per_device = KT_DEV * QT_DEV
    half = amp.shape[1] // width
    own_copy = pltpu.make_async_copy(own, amp.at[:, pl.ds(0, width)], own_sem)
    own_copy.start()
    res_copy = pltpu.make_async_copy(residual, res, res_sem)
    res_copy.start()
    for p, piece in enumerate(pieces):
        rows = piece[:, capacity * width :, :]
        places[p * columns : (p + 1) * columns] = jnp.max(
            rows.astype(jnp.float32), axis=1
        ).astype(jnp.int32)
    table_copy = pltpu.make_async_copy(places, table, table_sem)
    table_copy.start()
    for i, source in enumerate(amps):
        at = pl.multiple_of(where_ref[n_pieces + 1 + i] * width, width)
        amp[:, pl.ds(at, width)] = source[...]
    table_copy.wait()
    col = where_ref[n_pieces]
    for p, piece in enumerate(pieces):
        row = where_ref[p]

        def place(c, _, p=p, piece=piece, row=row):
            for s in range(capacity):
                position = table[p * columns + c, s]
                k = row * KT_DEV + lax.shift_right_logical(position, QT_DEV.bit_length() - 1)
                slot = k ^ col
                q = pl.multiple_of((position & (QT_DEV - 1)) * width, width)
                at = pl.multiple_of((slot & (half - 1)) * width, width)
                tile = piece.at[c, pl.ds(s * width, width), :]

                @pl.when((position < per_device) & (slot < half))
                def _():
                    near[pl.ds(at, width), pl.ds(q, width)] = tile[...]

                @pl.when((position < per_device) & (slot >= half))
                def _():
                    far[pl.ds(at, width), pl.ds(q, width)] = tile[...]

            return 0

        lax.fori_loop(0, columns, place, 0)
    own_copy.wait()
    res_copy.wait()
    multiply(amp, near, res, total, None, 2 * width)


def near_half(where, pieces, amps, own, residual, capacity):
    columns, _, width = pieces[0].shape
    n_pieces, n_amps = len(pieces), len(amps)
    rows, n_cols = residual.shape
    depth = (1 + n_amps) * width
    hbm = pl.BlockSpec(memory_space=pltpu.HBM)
    vmem = pl.BlockSpec(memory_space=pltpu.VMEM)
    held = 2 * rows * depth + 4 * depth * n_cols + 8 * rows * n_cols
    held += sum(x.size * x.dtype.itemsize for x in pieces) // 2
    return pl.pallas_call(
        functools.partial(near_kernel, n_pieces, n_amps, capacity),
        out_shape=[
            jax.ShapeDtypeStruct(residual.shape, residual.dtype),
            jax.ShapeDtypeStruct((depth, n_cols), pieces[0].dtype),
        ],
        in_specs=[pl.BlockSpec(memory_space=pltpu.SMEM)]
        + [vmem] * (n_pieces + n_amps)
        + [hbm, hbm],
        out_specs=[vmem, vmem],
        scratch_shapes=[
            pltpu.VMEM((n_pieces * columns, width), jnp.int32),
            pltpu.SMEM((n_pieces * columns, width), jnp.int32),
            pltpu.VMEM((rows, depth), pieces[0].dtype),
            pltpu.VMEM((depth, n_cols), pieces[0].dtype),
            pltpu.VMEM((rows, n_cols), residual.dtype),
            pltpu.SemaphoreType.DMA,
            pltpu.SemaphoreType.DMA,
            pltpu.SemaphoreType.DMA,
        ],
        compiler_params=pltpu.CompilerParams(vmem_limit_bytes=held + 2 * MIB),
        cost_estimate=pl.CostEstimate(
            flops=2 * rows * depth * n_cols,
            bytes_accessed=16 * rows * n_cols,
            transcendentals=0,
        ),
        name="near_half",
    )(
        where,
        *pieces,
        *amps,
        pltpu.with_memory_space_constraint(own, pltpu.HBM),
        pltpu.with_memory_space_constraint(residual, pltpu.HBM),
    )


def far_kernel(half, slots_ref, *refs):
    amps, (start, far, out, amp, total, sems) = refs[:-6], refs[-6:]
    width = amps[0].shape[1]
    for i, source in enumerate(amps):
        at = pl.multiple_of((slots_ref[i] - half) * width, width)
        amp[:, pl.ds(at, width)] = source[...]
    multiply(amp, far, start, (total, out), sems, 2 * width)


def far_half(slots, amps, total, far):
    rows, n_cols = total.shape
    depth, width = far.shape[0], amps[0].shape[1]
    vmem = pl.BlockSpec(memory_space=pltpu.VMEM)
    held = 4 * rows * depth + 2 * depth * n_cols + 8 * rows * n_cols
    return pl.pallas_call(
        functools.partial(far_kernel, depth // width),
        out_shape=jax.ShapeDtypeStruct(total.shape, total.dtype),
        in_specs=[pl.BlockSpec(memory_space=pltpu.SMEM)] + [vmem] * (len(amps) + 2),
        out_specs=pl.BlockSpec(memory_space=pltpu.HBM),
        scratch_shapes=[
            pltpu.VMEM((rows, depth), far.dtype),
            pltpu.VMEM((rows, n_cols), total.dtype),
            pltpu.SemaphoreType.DMA((n_cols // (2 * width),)),
        ],
        compiler_params=pltpu.CompilerParams(vmem_limit_bytes=held + 2 * MIB),
        cost_estimate=pl.CostEstimate(
            flops=2 * rows * depth * n_cols,
            bytes_accessed=16 * rows * n_cols,
            transcendentals=0,
        ),
        name="far_half",
    )(slots, *amps, total, far)


def exchange(x, axis, flip):
    size = lax.axis_size(axis)
    return lax.ppermute(x, axis, [(i, i ^ flip) for i in range(size)])


def choose_kernel(flag_ref, first, second, out):
    @pl.when(flag_ref[0] == 1)
    def _():
        out[...] = first[...]

    @pl.when(flag_ref[0] == 0)
    def _():
        out[...] = second[...]


def choose(flag, first, second):
    vmem = pl.BlockSpec(memory_space=pltpu.VMEM)
    return pl.pallas_call(
        choose_kernel,
        out_shape=jax.ShapeDtypeStruct(first.shape, first.dtype),
        in_specs=[pl.BlockSpec(memory_space=pltpu.SMEM), vmem, vmem],
        out_specs=vmem,
        compiler_params=pltpu.CompilerParams(vmem_limit_bytes=4 * MIB),
        name="choose",
    )(flag[None], first, second)


def tie(late, *early):
    return lax.optimization_barrier((late, *early))


def body(amplitudes, packed_tiles, tile_ids, residual_in):
    n_col, n_row = lax.axis_size("col"), lax.axis_size("row")
    col, row = lax.axis_index("col"), lax.axis_index("row")
    inner = 2 ** (int(math.log2(n_col)) // 2)
    capacity = -(-packed_tiles.shape[1] // n_col)
    half = n_col // 2
    lanes = range(1, inner)
    outgoing = list(pack(col, packed_tiles, tile_ids, n_col, capacity))

    amps = {0: amplitudes}
    for s in [*lanes, inner]:
        amps[s] = exchange(amplitudes, "col", s)
    mids = [(i // inner) % 4 in (1, 2) for i in range(n_col)]
    swap = [(i, i ^ (3 * inner) if m else i) for i, m in enumerate(mids)]
    across = lax.ppermute(amplitudes, "col", swap)
    outgoing[half:], amps, across = tie(outgoing[half:], amps, across)

    chunks = [outgoing[0][None]]
    chunks += [exchange(outgoing[s][None], "col", s) for s in range(1, n_col)]
    outer = col // inner % 4
    is_mid = ((outer == 1) | (outer == 2)).astype(jnp.int32)
    onward = exchange(across, "col", inner)
    leaving = choose(is_mid, amps[inner], amplitudes)
    chunks[half], onward, leaving = tie(chunks[half], onward, leaving)
    passed_on = choose(is_mid, across, onward)
    straight = exchange(leaving, "col", 2 * inner)
    for lane in lanes:
        amps[inner ^ lane] = exchange(amps[inner], "col", lane)
    passed_over = [exchange(passed_on, "col", lane) for lane in lanes]

    early = [inner ^ lane for lane in lanes]
    pieces, rows = [], []
    for group in (join(chunks[half:]), join(chunks[:half])):
        passed = [exchange(group, "row", flip) for flip in range(CORES, n_row, CORES)]
        if pieces:
            passed, straight = tie(passed, straight)
        else:
            passed, got, passed_over = tie(passed, [amps[s] for s in early], passed_over)
            amps.update(zip(early, got))
        own, passed = tie(group, passed)
        for flip, mine in zip(range(0, n_row, CORES), [own, *passed]):
            pieces += [mine, exchange(mine, "row", 1)]
            rows += [row ^ flip, row ^ flip ^ 1]
    straight_over = [exchange(straight, "col", lane) for lane in lanes]

    here, there = (2 + is_mid) * inner, (3 - is_mid) * inner
    far = [(here, passed_on), *zip([here ^ x for x in lanes], passed_over)]
    far += [(there, straight), *zip([there ^ x for x in lanes], straight_over)]
    near = [(s, amps[s]) for s in sorted(amps) if s]
    flip = 4 * inner
    while flip < n_col:
        near, far = near + far, [
            (s ^ flip, exchange(x, "col", flip)) for s, x in [(0, amplitudes), *near, *far]
        ]
        flip *= 2
    where = jnp.stack(rows + [col]).astype(jnp.int32)
    near_slots, near_amps = zip(*near)
    far_slots, far_amps = zip(*far)
    near_slots = jnp.stack([jnp.asarray(s, jnp.int32) for s in near_slots])
    far_slots = jnp.stack([jnp.asarray(s, jnp.int32) for s in far_slots])
    where = jnp.concatenate([where, near_slots])
    total, far_block = near_half(
        where, pieces, near_amps, amplitudes, residual_in, capacity
    )
    return far_half(far_slots, far_amps, total, far_block)


def solution(mesh):
    in_specs = (P("row", "col"), P("row", "col", None, None), P("row", "col"), P("row", "col"))
    out_specs = P("row", "col")
    return jax.shard_map(body, mesh=mesh, in_specs=in_specs, out_specs=out_specs, check_vma=False)
```

```python
import functools
import math

import jax
import jax.numpy as jnp
from jax import lax
from jax.experimental import pallas as pl
from jax.experimental.pallas import tpu as pltpu
from jax.sharding import PartitionSpec as P

KT_DEV = 2
QT_DEV = 8
CORES = 2
META = 16
MIB = 1024 * 1024


def pack_kernel(columns, capacity, me_ref, ids_hbm, tiles_hbm, *refs):
    outs = refs[:columns]
    ids_ref, tiles_ref, slot_tile, slot_place, count, ids_sem, tiles_sem = refs[columns:]
    ids_copy = pltpu.make_async_copy(ids_hbm, ids_ref, ids_sem)
    tiles_copy = pltpu.make_async_copy(tiles_hbm, tiles_ref, tiles_sem)
    ids_copy.start()
    tiles_copy.start()
    per_device, width = tiles_ref.shape[1], tiles_ref.shape[2]
    shift = per_device.bit_length() - 1
    for d in range(columns):
        count[d] = 0
        for s in range(capacity):
            slot_place[d * capacity + s] = per_device
    ids_copy.wait()
    for t in range(per_device):
        tile_id = ids_ref[0, t]
        target = lax.shift_right_logical(tile_id, shift)
        rank = count[target]
        count[target] = rank + 1
        slot_tile[target * capacity + rank] = t
        slot_place[target * capacity + rank] = tile_id & (per_device - 1)
    tiles_copy.wait()
    lane = lax.broadcasted_iota(jnp.int32, (META, width), 1)
    for d, out in enumerate(outs):
        target = me_ref[0] ^ d
        row = jnp.full((META, width), per_device, jnp.int32)
        for s in range(capacity):
            place = slot_place[target * capacity + s]
            row = jnp.where(lane == s, place, row)

            @pl.when(place < per_device)
            def _():
                out[s * width : (s + 1) * width, :] = tiles_ref[
                    0, slot_tile[target * capacity + s]
                ]

        out[capacity * width :, :] = row.astype(jnp.float32).astype(jnp.bfloat16)


def pack(col, packed_tiles, tile_ids, columns, capacity):
    _, per_device, width, _ = packed_tiles.shape
    chunk = jax.ShapeDtypeStruct((capacity * width + META, width), packed_tiles.dtype)
    smem = pl.BlockSpec(memory_space=pltpu.SMEM)
    vmem = pl.BlockSpec(memory_space=pltpu.VMEM)
    hbm = pl.BlockSpec(memory_space=pltpu.HBM)
    return pl.pallas_call(
        functools.partial(pack_kernel, columns, capacity),
        out_shape=[chunk] * columns,
        in_specs=[smem, hbm, hbm],
        out_specs=[vmem] * columns,
        scratch_shapes=[
            pltpu.SMEM(tile_ids.shape, jnp.int32),
            pltpu.VMEM(packed_tiles.shape, packed_tiles.dtype),
            pltpu.SMEM((columns * capacity,), jnp.int32),
            pltpu.SMEM((columns * capacity,), jnp.int32),
            pltpu.SMEM((columns,), jnp.int32),
            pltpu.SemaphoreType.DMA,
            pltpu.SemaphoreType.DMA,
        ],
        compiler_params=pltpu.CompilerParams(vmem_limit_bytes=8 * MIB),
        name="pack",
    )(
        col[None],
        pltpu.with_memory_space_constraint(tile_ids, pltpu.HBM),
        pltpu.with_memory_space_constraint(packed_tiles, pltpu.HBM),
    )


def join_kernel(*refs):
    at = 0
    for part in refs[:-1]:
        refs[-1][at : at + part.shape[0]] = part[...]
        at += part.shape[0]


def join(chunks):
    vmem = pl.BlockSpec(memory_space=pltpu.VMEM)
    total = sum(c.shape[0] for c in chunks)
    return pl.pallas_call(
        join_kernel,
        out_shape=jax.ShapeDtypeStruct((total, *chunks[0].shape[1:]), chunks[0].dtype),
        in_specs=[vmem] * len(chunks),
        out_specs=vmem,
        compiler_params=pltpu.CompilerParams(vmem_limit_bytes=8 * MIB),
        name="join",
    )(*chunks)


def multiply(amp, block, start, out, sems, step):
    copies = []
    for n in range(block.shape[1] // step):
        cols = slice(n * step, (n + 1) * step)
        held = out[0] if sems is not None else out
        held[:, cols] = start[:, cols] + jnp.dot(
            amp[...], block[:, cols], preferred_element_type=jnp.float32
        )
        if sems is not None:
            part = pl.ds(n * step, step)
            copies.append(
                pltpu.make_async_copy(held.at[:, part], out[1].at[:, part], sems.at[n])
            )
            copies[-1].start()
    for copy in copies:
        copy.wait()


def put_in_order(flag, amps, offsets, first, amp):
    width = amps[0].shape[2]
    for kind in (0, 1):

        @pl.when(flag == kind)
        def _(kind=kind):
            for source, slots in zip(amps, offsets):
                for i, slot in enumerate(slots[kind]):
                    at = (slot - first) * width
                    amp[:, at : at + width] = source[i]


def near_kernel(n_pieces, offsets, capacity, where_ref, *refs):
    n_amps = len(offsets)
    pieces = refs[:n_pieces]
    amps = refs[n_pieces : n_pieces + n_amps]
    own, residual, total, far = refs[n_pieces + n_amps : n_pieces + n_amps + 4]
    places, table, amp, near, res, table_sem, own_sem, res_sem = refs[n_pieces + n_amps + 4 :]
    columns = pieces[0].shape[0]
    width = pieces[0].shape[2]
    per_device = KT_DEV * QT_DEV
    half = amp.shape[1] // width
    own_copy = pltpu.make_async_copy(own, amp.at[:, pl.ds(0, width)], own_sem)
    own_copy.start()
    res_copy = pltpu.make_async_copy(residual, res, res_sem)
    res_copy.start()
    for p, piece in enumerate(pieces):
        rows = piece[:, capacity * width :, :]
        places[p * columns : (p + 1) * columns] = jnp.max(
            rows.astype(jnp.float32), axis=1
        ).astype(jnp.int32)
    table_copy = pltpu.make_async_copy(places, table, table_sem)
    table_copy.start()
    put_in_order(where_ref[n_pieces + 1], amps, offsets, 0, amp)
    table_copy.wait()
    col = where_ref[n_pieces]
    for p, piece in enumerate(pieces):
        row = where_ref[p]

        def place(c, _, p=p, piece=piece, row=row):
            for s in range(capacity):
                position = table[p * columns + c, s]
                k = row * KT_DEV + lax.shift_right_logical(position, QT_DEV.bit_length() - 1)
                slot = k ^ col
                q = pl.multiple_of((position & (QT_DEV - 1)) * width, width)
                at = pl.multiple_of((slot & (half - 1)) * width, width)
                tile = piece.at[c, pl.ds(s * width, width), :]

                @pl.when((position < per_device) & (slot < half))
                def _():
                    near[pl.ds(at, width), pl.ds(q, width)] = tile[...]

                @pl.when((position < per_device) & (slot >= half))
                def _():
                    far[pl.ds(at, width), pl.ds(q, width)] = tile[...]

            return 0

        lax.fori_loop(0, columns, place, 0)
    own_copy.wait()
    res_copy.wait()
    multiply(amp, near, res, total, None, 2 * width)


def near_half(where, pieces, amps, offsets, own, residual, capacity):
    columns, _, width = pieces[0].shape
    n_pieces, n_amps = len(pieces), len(amps)
    rows, n_cols = residual.shape
    depth = (1 + sum(len(s[0]) for s in offsets)) * width
    hbm = pl.BlockSpec(memory_space=pltpu.HBM)
    vmem = pl.BlockSpec(memory_space=pltpu.VMEM)
    held = 2 * rows * depth + 4 * depth * n_cols + 8 * rows * n_cols
    held += sum(x.size * x.dtype.itemsize for x in pieces) // 2
    return pl.pallas_call(
        functools.partial(near_kernel, n_pieces, offsets, capacity),
        out_shape=[
            jax.ShapeDtypeStruct(residual.shape, residual.dtype),
            jax.ShapeDtypeStruct((depth, n_cols), pieces[0].dtype),
        ],
        in_specs=[pl.BlockSpec(memory_space=pltpu.SMEM)]
        + [vmem] * (n_pieces + n_amps)
        + [hbm, hbm],
        out_specs=[vmem, vmem],
        scratch_shapes=[
            pltpu.VMEM((n_pieces * columns, width), jnp.int32),
            pltpu.SMEM((n_pieces * columns, width), jnp.int32),
            pltpu.VMEM((rows, depth), pieces[0].dtype),
            pltpu.VMEM((depth, n_cols), pieces[0].dtype),
            pltpu.VMEM((rows, n_cols), residual.dtype),
            pltpu.SemaphoreType.DMA,
            pltpu.SemaphoreType.DMA,
            pltpu.SemaphoreType.DMA,
        ],
        compiler_params=pltpu.CompilerParams(vmem_limit_bytes=held + 2 * MIB),
        cost_estimate=pl.CostEstimate(
            flops=2 * rows * depth * n_cols,
            bytes_accessed=16 * rows * n_cols,
            transcendentals=0,
        ),
        name="near_half",
    )(
        where,
        *pieces,
        *amps,
        pltpu.with_memory_space_constraint(own, pltpu.HBM),
        pltpu.with_memory_space_constraint(residual, pltpu.HBM),
    )


def far_kernel(offsets, half, flag_ref, *refs):
    amps, (start, far, out, amp, total, sems) = refs[:-6], refs[-6:]
    width = amps[0].shape[2]
    put_in_order(flag_ref[0], amps, offsets, half, amp)
    multiply(amp, far, start, (total, out), sems, 2 * width)


def far_half(flag, amps, offsets, total, far):
    rows, n_cols = total.shape
    depth, width = far.shape[0], amps[0].shape[2]
    vmem = pl.BlockSpec(memory_space=pltpu.VMEM)
    held = 4 * rows * depth + 2 * depth * n_cols + 8 * rows * n_cols
    return pl.pallas_call(
        functools.partial(far_kernel, offsets, depth // width),
        out_shape=jax.ShapeDtypeStruct(total.shape, total.dtype),
        in_specs=[pl.BlockSpec(memory_space=pltpu.SMEM)] + [vmem] * (len(amps) + 2),
        out_specs=pl.BlockSpec(memory_space=pltpu.HBM),
        scratch_shapes=[
            pltpu.VMEM((rows, depth), far.dtype),
            pltpu.VMEM((rows, n_cols), total.dtype),
            pltpu.SemaphoreType.DMA((n_cols // (2 * width),)),
        ],
        compiler_params=pltpu.CompilerParams(vmem_limit_bytes=held + 2 * MIB),
        cost_estimate=pl.CostEstimate(
            flops=2 * rows * depth * n_cols,
            bytes_accessed=16 * rows * n_cols,
            transcendentals=0,
        ),
        name="far_half",
    )(flag[None], *amps, total, far)


def exchange(x, axis, flip):
    size = lax.axis_size(axis)
    return lax.ppermute(x, axis, [(i, i ^ flip) for i in range(size)])


def choose_kernel(flag_ref, pair, out):
    out[0] = pair[flag_ref[0]]


def choose(flag, pair):
    vmem = pl.BlockSpec(memory_space=pltpu.VMEM)
    return pl.pallas_call(
        choose_kernel,
        out_shape=jax.ShapeDtypeStruct((1, *pair.shape[1:]), pair.dtype),
        in_specs=[pl.BlockSpec(memory_space=pltpu.SMEM), vmem],
        out_specs=vmem,
        compiler_params=pltpu.CompilerParams(vmem_limit_bytes=4 * MIB),
        name="choose",
    )(flag[None], pair)


def leave_kernel(flag_ref, beside, own, out, sem):
    @pl.when(flag_ref[0] == 1)
    def _():
        out[...] = beside[...]

    @pl.when(flag_ref[0] == 0)
    def _():
        copy = pltpu.make_async_copy(own, out, sem)
        copy.start()
        copy.wait()


def leave(flag, beside, own):
    vmem = pl.BlockSpec(memory_space=pltpu.VMEM)
    return pl.pallas_call(
        leave_kernel,
        out_shape=jax.ShapeDtypeStruct(beside.shape, beside.dtype),
        in_specs=[
            pl.BlockSpec(memory_space=pltpu.SMEM),
            vmem,
            pl.BlockSpec(memory_space=pltpu.HBM),
        ],
        out_specs=vmem,
        scratch_shapes=[pltpu.SemaphoreType.DMA],
        compiler_params=pltpu.CompilerParams(vmem_limit_bytes=4 * MIB),
        name="leave",
    )(flag[None], beside, pltpu.with_memory_space_constraint(own, pltpu.HBM))


def pick(flag, first, second):
    return choose(1 - flag, join([first, second]))


def tie(late, *early):
    return lax.optimization_barrier((late, *early))


def body(amplitudes, packed_tiles, tile_ids, residual_in):
    n_col, n_row = lax.axis_size("col"), lax.axis_size("row")
    col, row = lax.axis_index("col"), lax.axis_index("row")
    inner = 2 ** (int(math.log2(n_col)) // 2)
    capacity = -(-packed_tiles.shape[1] // n_col)
    half = n_col // 2
    lanes = range(1, inner)
    outgoing = list(pack(col, packed_tiles, tile_ids, n_col, capacity))

    mids = [(i // inner) % 4 in (1, 2) for i in range(n_col)]
    swap = [(i, i ^ (3 * inner) if m else i ^ 1) for i, m in enumerate(mids)]
    own = amplitudes[None]
    across = lax.ppermute(own, "col", swap)
    beside = exchange(own, "col", inner)
    outgoing[half:], across, beside = tie(outgoing[half:], across, beside)

    chunks = [outgoing[0][None]]
    chunks += [exchange(outgoing[s][None], "col", s) for s in range(1, n_col)]
    outer = col // inner % 4
    is_mid = ((outer == 1) | (outer == 2)).astype(jnp.int32)
    onward = exchange(across, "col", inner)
    leaving = leave(is_mid, beside, own)
    chunks[half], onward, leaving = tie(chunks[half], onward, leaving)
    own_over = [exchange(own, "col", lane) for lane in lanes]
    chunks[half + 1], own_over = tie(chunks[half + 1], own_over)
    beside_over = [exchange(beside, "col", lane) for lane in lanes]
    passed_on = pick(is_mid, across, onward)
    straight = exchange(leaving, "col", 2 * inner)
    passed_over = [exchange(passed_on, "col", lane) for lane in lanes]

    pieces, rows = [], []
    for group in (join(chunks[half:]), join(chunks[:half])):
        passed = [exchange(group, "row", flip) for flip in range(CORES, n_row, CORES)]
        if pieces:
            passed, straight = tie(passed, straight)
        else:
            passed, beside_over, passed_over = tie(passed, beside_over, passed_over)
        mine, passed = tie(group, passed)
        for flip, mine in zip(range(0, n_row, CORES), [mine, *passed]):
            pieces += [mine, exchange(mine, "row", 1)]
            rows += [row ^ flip, row ^ flip ^ 1]
    straight_over = [exchange(straight, "col", lane) for lane in lanes]

    def over(shards, ends, middles):
        return [
            (x, [[s ^ lane for s in kind] for kind in (ends, middles)])
            for lane, x in enumerate(shards)
            if x is not None
        ]

    near = over([None, *own_over], [0], [0]) + over([beside, *beside_over], [inner], [inner])
    far = over([passed_on, *passed_over], [2 * inner], [3 * inner])
    far += over([straight, *straight_over], [3 * inner], [2 * inner])
    flip = 4 * inner
    while flip < n_col:
        held = [(own, [[0], [0]]), *near, *far]
        near = near + far
        far = [
            (exchange(x, "col", flip), [[s ^ flip for s in kind] for kind in slots])
            for x, slots in held
        ]
        flip *= 2
    where = jnp.stack([*rows, col, is_mid]).astype(jnp.int32)
    total, far_block = near_half(
        where, pieces, *zip(*near), amplitudes, residual_in, capacity
    )
    return far_half(is_mid, *zip(*far), total, far_block)


def solution(mesh):
    in_specs = (P("row", "col"), P("row", "col", None, None), P("row", "col"), P("row", "col"))
    out_specs = P("row", "col")
    return jax.shard_map(body, mesh=mesh, in_specs=in_specs, out_specs=out_specs, check_vma=False)
```

```python
import functools
import math

import jax
import jax.numpy as jnp
from jax import lax
from jax.experimental import pallas as pl
from jax.experimental.pallas import tpu as pltpu
from jax.sharding import PartitionSpec as P

KT_DEV = 2
QT_DEV = 8
CORES = 2
META = 16
MIB = 1024 * 1024


def pack_kernel(columns, capacity, me_ref, ids_hbm, tiles_hbm, *refs):
    outs = refs[:columns]
    ids_ref, tiles_ref, slot_tile, slot_place, count, ids_sem, tiles_sem = refs[columns:]
    ids_copy = pltpu.make_async_copy(ids_hbm, ids_ref, ids_sem)
    tiles_copy = pltpu.make_async_copy(tiles_hbm, tiles_ref, tiles_sem)
    ids_copy.start()
    tiles_copy.start()
    per_device, width = tiles_ref.shape[1], tiles_ref.shape[2]
    shift = per_device.bit_length() - 1
    for d in range(columns):
        count[d] = 0
        for s in range(capacity):
            slot_place[d * capacity + s] = per_device
    ids_copy.wait()
    for t in range(per_device):
        tile_id = ids_ref[0, t]
        target = lax.shift_right_logical(tile_id, shift)
        rank = count[target]
        count[target] = rank + 1
        slot_tile[target * capacity + rank] = t
        slot_place[target * capacity + rank] = tile_id & (per_device - 1)
    tiles_copy.wait()
    lane = lax.broadcasted_iota(jnp.int32, (META, width), 1)
    for d, out in enumerate(outs):
        target = me_ref[0] ^ d
        row = jnp.full((META, width), per_device, jnp.int32)
        for s in range(capacity):
            place = slot_place[target * capacity + s]
            row = jnp.where(lane == s, place, row)

            @pl.when(place < per_device)
            def _():
                out[s * width : (s + 1) * width, :] = tiles_ref[
                    0, slot_tile[target * capacity + s]
                ]

        out[capacity * width :, :] = row.astype(jnp.float32).astype(jnp.bfloat16)


def pack(col, packed_tiles, tile_ids, columns, capacity):
    _, per_device, width, _ = packed_tiles.shape
    chunk = jax.ShapeDtypeStruct((capacity * width + META, width), packed_tiles.dtype)
    smem = pl.BlockSpec(memory_space=pltpu.SMEM)
    vmem = pl.BlockSpec(memory_space=pltpu.VMEM)
    hbm = pl.BlockSpec(memory_space=pltpu.HBM)
    return pl.pallas_call(
        functools.partial(pack_kernel, columns, capacity),
        out_shape=[chunk] * columns,
        in_specs=[smem, hbm, hbm],
        out_specs=[vmem] * columns,
        scratch_shapes=[
            pltpu.SMEM(tile_ids.shape, jnp.int32),
            pltpu.VMEM(packed_tiles.shape, packed_tiles.dtype),
            pltpu.SMEM((columns * capacity,), jnp.int32),
            pltpu.SMEM((columns * capacity,), jnp.int32),
            pltpu.SMEM((columns,), jnp.int32),
            pltpu.SemaphoreType.DMA,
            pltpu.SemaphoreType.DMA,
        ],
        compiler_params=pltpu.CompilerParams(vmem_limit_bytes=8 * MIB),
        name="pack",
    )(
        col[None],
        pltpu.with_memory_space_constraint(tile_ids, pltpu.HBM),
        pltpu.with_memory_space_constraint(packed_tiles, pltpu.HBM),
    )


def join_kernel(*refs):
    at = 0
    for part in refs[:-1]:
        refs[-1][at : at + part.shape[0]] = part[...]
        at += part.shape[0]


def join(chunks):
    vmem = pl.BlockSpec(memory_space=pltpu.VMEM)
    total = sum(c.shape[0] for c in chunks)
    return pl.pallas_call(
        join_kernel,
        out_shape=jax.ShapeDtypeStruct((total, *chunks[0].shape[1:]), chunks[0].dtype),
        in_specs=[vmem] * len(chunks),
        out_specs=vmem,
        compiler_params=pltpu.CompilerParams(vmem_limit_bytes=8 * MIB),
        name="join",
    )(*chunks)


def multiply(amp, block, start, out, sems, step):
    copies = []
    for n in range(block.shape[1] // step):
        cols = slice(n * step, (n + 1) * step)
        held = out[0] if sems is not None else out
        held[:, cols] = start[:, cols] + jnp.dot(
            amp[...], block[:, cols], preferred_element_type=jnp.float32
        )
        if sems is not None:
            part = pl.ds(n * step, step)
            copies.append(
                pltpu.make_async_copy(held.at[:, part], out[1].at[:, part], sems.at[n])
            )
            copies[-1].start()
    for copy in copies:
        copy.wait()


def put_in_order(flag, amps, offsets, first, amp):
    width = amps[0].shape[2]
    for kind in (0, 1):

        @pl.when(flag == kind)
        def _(kind=kind):
            for source, slots in zip(amps, offsets):
                for i, slot in enumerate(slots[kind]):
                    at = (slot - first) * width
                    amp[:, at : at + width] = source[i]


def near_kernel(n_pieces, offsets, capacity, where_ref, *refs):
    n_amps = len(offsets)
    pieces = refs[:n_pieces]
    amps = refs[n_pieces : n_pieces + n_amps]
    own, residual, total, far = refs[n_pieces + n_amps : n_pieces + n_amps + 4]
    places, table, amp, near, res, table_sem, own_sem, res_sem = refs[n_pieces + n_amps + 4 :]
    columns = pieces[0].shape[0]
    width = pieces[0].shape[2]
    per_device = KT_DEV * QT_DEV
    half = amp.shape[1] // width
    own_copy = pltpu.make_async_copy(own, amp.at[:, pl.ds(0, width)], own_sem)
    own_copy.start()
    res_copy = pltpu.make_async_copy(residual, res, res_sem)
    res_copy.start()
    for p, piece in enumerate(pieces):
        rows = piece[:, capacity * width :, :]
        places[p * columns : (p + 1) * columns] = jnp.max(
            rows.astype(jnp.float32), axis=1
        ).astype(jnp.int32)
    table_copy = pltpu.make_async_copy(places, table, table_sem)
    table_copy.start()
    put_in_order(where_ref[n_pieces + 1], amps, offsets, 0, amp)
    table_copy.wait()
    col = where_ref[n_pieces]
    for p, piece in enumerate(pieces):
        row = where_ref[p]

        def place(c, _, p=p, piece=piece, row=row):
            for s in range(capacity):
                position = table[p * columns + c, s]
                k = row * KT_DEV + lax.shift_right_logical(position, QT_DEV.bit_length() - 1)
                slot = k ^ col
                q = pl.multiple_of((position & (QT_DEV - 1)) * width, width)
                at = pl.multiple_of((slot & (half - 1)) * width, width)
                tile = piece.at[c, pl.ds(s * width, width), :]

                @pl.when((position < per_device) & (slot < half))
                def _():
                    near[pl.ds(at, width), pl.ds(q, width)] = tile[...]

                @pl.when((position < per_device) & (slot >= half))
                def _():
                    far[pl.ds(at, width), pl.ds(q, width)] = tile[...]

            return 0

        lax.fori_loop(0, columns, place, 0)
    own_copy.wait()
    res_copy.wait()
    multiply(amp, near, res, total, None, 2 * width)


def near_half(where, pieces, amps, offsets, own, residual, capacity):
    columns, _, width = pieces[0].shape
    n_pieces, n_amps = len(pieces), len(amps)
    rows, n_cols = residual.shape
    depth = (1 + sum(len(s[0]) for s in offsets)) * width
    hbm = pl.BlockSpec(memory_space=pltpu.HBM)
    vmem = pl.BlockSpec(memory_space=pltpu.VMEM)
    held = 2 * rows * depth + 4 * depth * n_cols + 8 * rows * n_cols
    held += sum(x.size * x.dtype.itemsize for x in pieces) // 2
    return pl.pallas_call(
        functools.partial(near_kernel, n_pieces, offsets, capacity),
        out_shape=[
            jax.ShapeDtypeStruct(residual.shape, residual.dtype),
            jax.ShapeDtypeStruct((depth, n_cols), pieces[0].dtype),
        ],
        in_specs=[pl.BlockSpec(memory_space=pltpu.SMEM)]
        + [vmem] * (n_pieces + n_amps)
        + [hbm, hbm],
        out_specs=[vmem, vmem],
        scratch_shapes=[
            pltpu.VMEM((n_pieces * columns, width), jnp.int32),
            pltpu.SMEM((n_pieces * columns, width), jnp.int32),
            pltpu.VMEM((rows, depth), pieces[0].dtype),
            pltpu.VMEM((depth, n_cols), pieces[0].dtype),
            pltpu.VMEM((rows, n_cols), residual.dtype),
            pltpu.SemaphoreType.DMA,
            pltpu.SemaphoreType.DMA,
            pltpu.SemaphoreType.DMA,
        ],
        compiler_params=pltpu.CompilerParams(vmem_limit_bytes=held + 2 * MIB),
        cost_estimate=pl.CostEstimate(
            flops=2 * rows * depth * n_cols,
            bytes_accessed=16 * rows * n_cols,
            transcendentals=0,
        ),
        name="near_half",
    )(
        where,
        *pieces,
        *amps,
        pltpu.with_memory_space_constraint(own, pltpu.HBM),
        pltpu.with_memory_space_constraint(residual, pltpu.HBM),
    )


def far_kernel(offsets, half, flag_ref, *refs):
    amps, (start, far, out, amp, total, sems) = refs[:-6], refs[-6:]
    width = amps[0].shape[2]
    put_in_order(flag_ref[0], amps, offsets, half, amp)
    multiply(amp, far, start, (total, out), sems, 2 * width)


def far_half(flag, amps, offsets, total, far):
    rows, n_cols = total.shape
    depth, width = far.shape[0], amps[0].shape[2]
    vmem = pl.BlockSpec(memory_space=pltpu.VMEM)
    held = 4 * rows * depth + 2 * depth * n_cols + 8 * rows * n_cols
    return pl.pallas_call(
        functools.partial(far_kernel, offsets, depth // width),
        out_shape=jax.ShapeDtypeStruct(total.shape, total.dtype),
        in_specs=[pl.BlockSpec(memory_space=pltpu.SMEM)] + [vmem] * (len(amps) + 2),
        out_specs=pl.BlockSpec(memory_space=pltpu.HBM),
        scratch_shapes=[
            pltpu.VMEM((rows, depth), far.dtype),
            pltpu.VMEM((rows, n_cols), total.dtype),
            pltpu.SemaphoreType.DMA((n_cols // (2 * width),)),
        ],
        compiler_params=pltpu.CompilerParams(vmem_limit_bytes=held + 2 * MIB),
        cost_estimate=pl.CostEstimate(
            flops=2 * rows * depth * n_cols,
            bytes_accessed=16 * rows * n_cols,
            transcendentals=0,
        ),
        name="far_half",
    )(flag[None], *amps, total, far)


def exchange(x, axis, flip):
    size = lax.axis_size(axis)
    return lax.ppermute(x, axis, [(i, i ^ flip) for i in range(size)])


def choose_kernel(flag_ref, pair, out):
    out[0] = pair[flag_ref[0]]


def choose(flag, pair):
    vmem = pl.BlockSpec(memory_space=pltpu.VMEM)
    return pl.pallas_call(
        choose_kernel,
        out_shape=jax.ShapeDtypeStruct((1, *pair.shape[1:]), pair.dtype),
        in_specs=[pl.BlockSpec(memory_space=pltpu.SMEM), vmem],
        out_specs=vmem,
        compiler_params=pltpu.CompilerParams(vmem_limit_bytes=4 * MIB),
        name="choose",
    )(flag[None], pair)


def leave_kernel(flag_ref, beside, own, out, sem):
    @pl.when(flag_ref[0] == 1)
    def _():
        out[...] = beside[...]

    @pl.when(flag_ref[0] == 0)
    def _():
        copy = pltpu.make_async_copy(own, out, sem)
        copy.start()
        copy.wait()


def leave(flag, beside, own):
    vmem = pl.BlockSpec(memory_space=pltpu.VMEM)
    return pl.pallas_call(
        leave_kernel,
        out_shape=jax.ShapeDtypeStruct(beside.shape, beside.dtype),
        in_specs=[
            pl.BlockSpec(memory_space=pltpu.SMEM),
            vmem,
            pl.BlockSpec(memory_space=pltpu.HBM),
        ],
        out_specs=vmem,
        scratch_shapes=[pltpu.SemaphoreType.DMA],
        compiler_params=pltpu.CompilerParams(vmem_limit_bytes=4 * MIB),
        name="leave",
    )(flag[None], beside, pltpu.with_memory_space_constraint(own, pltpu.HBM))


def pick(flag, first, second):
    return choose(1 - flag, join([first, second]))


def tie(late, *early):
    return lax.optimization_barrier((late, *early))


def body(amplitudes, packed_tiles, tile_ids, residual_in):
    n_col, n_row = lax.axis_size("col"), lax.axis_size("row")
    col, row = lax.axis_index("col"), lax.axis_index("row")
    inner = 2 ** (int(math.log2(n_col)) // 2)
    capacity = -(-packed_tiles.shape[1] // n_col)
    half = n_col // 2
    lanes = range(1, inner)
    outgoing = list(pack(col, packed_tiles, tile_ids, n_col, capacity))

    mids = [(i // inner) % 4 in (1, 2) for i in range(n_col)]
    swap = [(i, i ^ (3 * inner) if m else i ^ 1) for i, m in enumerate(mids)]
    own = amplitudes[None]
    across = lax.ppermute(own, "col", swap)
    beside = exchange(own, "col", inner)

    chunks = [outgoing[0][None]]
    chunks += [exchange(outgoing[s][None], "col", s) for s in range(1, n_col)]
    outer = col // inner % 4
    is_mid = ((outer == 1) | (outer == 2)).astype(jnp.int32)
    onward = exchange(across, "col", inner)
    leaving = leave(is_mid, beside, own)
    own_over = [exchange(own, "col", lane) for lane in lanes]
    chunks[half + 1], own_over, leaving = tie(chunks[half + 1], own_over, leaving)
    straight = exchange(leaving, "col", 2 * inner)
    beside_over = [exchange(beside, "col", lane) for lane in lanes]
    passed_on = pick(is_mid, across, onward)
    passed_over = [exchange(passed_on, "col", lane) for lane in lanes]

    pieces, rows = [], []
    for group in (join(chunks[half:]), join(chunks[:half])):
        passed = [exchange(group, "row", flip) for flip in range(CORES, n_row, CORES)]
        if pieces:
            passed, straight, passed_over = tie(passed, straight, passed_over)
        else:
            passed, beside_over = tie(passed, beside_over)
        mine, passed = tie(group, passed)
        for flip, mine in zip(range(0, n_row, CORES), [mine, *passed]):
            pieces += [mine, exchange(mine, "row", 1)]
            rows += [row ^ flip, row ^ flip ^ 1]
    straight_over = [exchange(straight, "col", lane) for lane in lanes]

    def over(shards, ends, middles):
        return [
            (x, [[s ^ lane for s in kind] for kind in (ends, middles)])
            for lane, x in enumerate(shards)
            if x is not None
        ]

    near = over([None, *own_over], [0], [0]) + over([beside, *beside_over], [inner], [inner])
    far = over([passed_on, *passed_over], [2 * inner], [3 * inner])
    far += over([straight, *straight_over], [3 * inner], [2 * inner])
    flip = 4 * inner
    while flip < n_col:
        held = [(own, [[0], [0]]), *near, *far]
        near = near + far
        far = [
            (exchange(x, "col", flip), [[s ^ flip for s in kind] for kind in slots])
            for x, slots in held
        ]
        flip *= 2
    where = jnp.stack([*rows, col, is_mid]).astype(jnp.int32)
    total, far_block = near_half(
        where, pieces, *zip(*near), amplitudes, residual_in, capacity
    )
    return far_half(is_mid, *zip(*far), total, far_block)


def solution(mesh):
    in_specs = (P("row", "col"), P("row", "col", None, None), P("row", "col"), P("row", "col"))
    out_specs = P("row", "col")
    return jax.shard_map(body, mesh=mesh, in_specs=in_specs, out_specs=out_specs, check_vma=False)
```

```python
import functools
import math

import jax
import jax.numpy as jnp
from jax import lax
from jax.experimental import pallas as pl
from jax.experimental.pallas import tpu as pltpu
from jax.sharding import PartitionSpec as P

KT_DEV = 2
QT_DEV = 8
CORES = 2
META = 16
MIB = 1024 * 1024


def pack_kernel(columns, capacity, me_ref, ids_hbm, tiles_hbm, *refs):
    outs = refs[:columns]
    ids_ref, tiles_ref, slot_tile, slot_place, count, ids_sem, tiles_sem = refs[columns:]
    ids_copy = pltpu.make_async_copy(ids_hbm, ids_ref, ids_sem)
    tiles_copy = pltpu.make_async_copy(tiles_hbm, tiles_ref, tiles_sem)
    ids_copy.start()
    tiles_copy.start()
    per_device, width = tiles_ref.shape[1], tiles_ref.shape[2]
    shift = per_device.bit_length() - 1
    for d in range(columns):
        count[d] = 0
        for s in range(capacity):
            slot_place[d * capacity + s] = per_device
    ids_copy.wait()
    for t in range(per_device):
        tile_id = ids_ref[0, t]
        target = lax.shift_right_logical(tile_id, shift)
        rank = count[target]
        count[target] = rank + 1
        slot_tile[target * capacity + rank] = t
        slot_place[target * capacity + rank] = tile_id & (per_device - 1)
    tiles_copy.wait()
    lane = lax.broadcasted_iota(jnp.int32, (META, width), 1)
    for d, out in enumerate(outs):
        target = me_ref[0] ^ d
        row = jnp.full((META, width), per_device, jnp.int32)
        for s in range(capacity):
            place = slot_place[target * capacity + s]
            row = jnp.where(lane == s, place, row)

            @pl.when(place < per_device)
            def _():
                out[s * width : (s + 1) * width, :] = tiles_ref[
                    0, slot_tile[target * capacity + s]
                ]

        out[capacity * width :, :] = row.astype(jnp.float32).astype(jnp.bfloat16)


def pack(col, packed_tiles, tile_ids, columns, capacity):
    _, per_device, width, _ = packed_tiles.shape
    chunk = jax.ShapeDtypeStruct((capacity * width + META, width), packed_tiles.dtype)
    smem = pl.BlockSpec(memory_space=pltpu.SMEM)
    vmem = pl.BlockSpec(memory_space=pltpu.VMEM)
    hbm = pl.BlockSpec(memory_space=pltpu.HBM)
    return pl.pallas_call(
        functools.partial(pack_kernel, columns, capacity),
        out_shape=[chunk] * columns,
        in_specs=[smem, hbm, hbm],
        out_specs=[vmem] * columns,
        scratch_shapes=[
            pltpu.SMEM(tile_ids.shape, jnp.int32),
            pltpu.VMEM(packed_tiles.shape, packed_tiles.dtype),
            pltpu.SMEM((columns * capacity,), jnp.int32),
            pltpu.SMEM((columns * capacity,), jnp.int32),
            pltpu.SMEM((columns,), jnp.int32),
            pltpu.SemaphoreType.DMA,
            pltpu.SemaphoreType.DMA,
        ],
        compiler_params=pltpu.CompilerParams(vmem_limit_bytes=8 * MIB),
        name="pack",
    )(
        col[None],
        pltpu.with_memory_space_constraint(tile_ids, pltpu.HBM),
        pltpu.with_memory_space_constraint(packed_tiles, pltpu.HBM),
    )


def join_kernel(*refs):
    at = 0
    for part in refs[:-1]:
        refs[-1][at : at + part.shape[0]] = part[...]
        at += part.shape[0]


def join(chunks):
    vmem = pl.BlockSpec(memory_space=pltpu.VMEM)
    total = sum(c.shape[0] for c in chunks)
    return pl.pallas_call(
        join_kernel,
        out_shape=jax.ShapeDtypeStruct((total, *chunks[0].shape[1:]), chunks[0].dtype),
        in_specs=[vmem] * len(chunks),
        out_specs=vmem,
        compiler_params=pltpu.CompilerParams(vmem_limit_bytes=8 * MIB),
        name="join",
    )(*chunks)


def multiply(amp, block, start, out, sems, step):
    copies = []
    for n in range(block.shape[1] // step):
        cols = slice(n * step, (n + 1) * step)
        held = out[0] if sems is not None else out
        held[:, cols] = start[:, cols] + jnp.dot(
            amp[...], block[:, cols], preferred_element_type=jnp.float32
        )
        if sems is not None:
            part = pl.ds(n * step, step)
            copies.append(
                pltpu.make_async_copy(held.at[:, part], out[1].at[:, part], sems.at[n])
            )
            copies[-1].start()
    for copy in copies:
        copy.wait()


def put_in_order(flag, amps, offsets, first, amp):
    width = amps[0].shape[2]
    for kind in (0, 1):

        @pl.when(flag == kind)
        def _(kind=kind):
            for source, slots in zip(amps, offsets):
                for i, slot in enumerate(slots[kind]):
                    at = (slot - first) * width
                    amp[:, at : at + width] = source[i]


def near_kernel(n_pieces, offsets, capacity, where_ref, *refs):
    n_amps = len(offsets)
    pieces = refs[:n_pieces]
    amps = refs[n_pieces : n_pieces + n_amps]
    own, residual, total, far = refs[n_pieces + n_amps : n_pieces + n_amps + 4]
    places, table, amp, near, res, table_sem, own_sem, res_sem = refs[n_pieces + n_amps + 4 :]
    columns = pieces[0].shape[0]
    width = pieces[0].shape[2]
    per_device = KT_DEV * QT_DEV
    half = amp.shape[1] // width
    own_copy = pltpu.make_async_copy(own, amp.at[:, pl.ds(0, width)], own_sem)
    own_copy.start()
    res_copy = pltpu.make_async_copy(residual, res, res_sem)
    res_copy.start()
    for p, piece in enumerate(pieces):
        rows = piece[:, capacity * width :, :]
        places[p * columns : (p + 1) * columns] = jnp.max(
            rows.astype(jnp.float32), axis=1
        ).astype(jnp.int32)
    table_copy = pltpu.make_async_copy(places, table, table_sem)
    table_copy.start()
    put_in_order(where_ref[n_pieces + 1], amps, offsets, 0, amp)
    table_copy.wait()
    col = where_ref[n_pieces]
    for p, piece in enumerate(pieces):
        row = where_ref[p]

        def place(c, _, p=p, piece=piece, row=row):
            for s in range(capacity):
                position = table[p * columns + c, s]
                k = row * KT_DEV + lax.shift_right_logical(position, QT_DEV.bit_length() - 1)
                slot = k ^ col
                q = pl.multiple_of((position & (QT_DEV - 1)) * width, width)
                at = pl.multiple_of((slot & (half - 1)) * width, width)
                tile = piece.at[c, pl.ds(s * width, width), :]

                @pl.when((position < per_device) & (slot < half))
                def _():
                    near[pl.ds(at, width), pl.ds(q, width)] = tile[...]

                @pl.when((position < per_device) & (slot >= half))
                def _():
                    far[pl.ds(at, width), pl.ds(q, width)] = tile[...]

            return 0

        lax.fori_loop(0, columns, place, 0)
    own_copy.wait()
    res_copy.wait()
    multiply(amp, near, res, total, None, 2 * width)


def near_half(where, pieces, amps, offsets, own, residual, capacity):
    columns, _, width = pieces[0].shape
    n_pieces, n_amps = len(pieces), len(amps)
    rows, n_cols = residual.shape
    depth = (1 + sum(len(s[0]) for s in offsets)) * width
    hbm = pl.BlockSpec(memory_space=pltpu.HBM)
    vmem = pl.BlockSpec(memory_space=pltpu.VMEM)
    held = 2 * rows * depth + 4 * depth * n_cols + 8 * rows * n_cols
    held += sum(x.size * x.dtype.itemsize for x in pieces) // 2
    return pl.pallas_call(
        functools.partial(near_kernel, n_pieces, offsets, capacity),
        out_shape=[
            jax.ShapeDtypeStruct(residual.shape, residual.dtype),
            jax.ShapeDtypeStruct((depth, n_cols), pieces[0].dtype),
        ],
        in_specs=[pl.BlockSpec(memory_space=pltpu.SMEM)]
        + [vmem] * (n_pieces + n_amps)
        + [hbm, hbm],
        out_specs=[vmem, vmem],
        scratch_shapes=[
            pltpu.VMEM((n_pieces * columns, width), jnp.int32),
            pltpu.SMEM((n_pieces * columns, width), jnp.int32),
            pltpu.VMEM((rows, depth), pieces[0].dtype),
            pltpu.VMEM((depth, n_cols), pieces[0].dtype),
            pltpu.VMEM((rows, n_cols), residual.dtype),
            pltpu.SemaphoreType.DMA,
            pltpu.SemaphoreType.DMA,
            pltpu.SemaphoreType.DMA,
        ],
        compiler_params=pltpu.CompilerParams(vmem_limit_bytes=held + 2 * MIB),
        cost_estimate=pl.CostEstimate(
            flops=2 * rows * depth * n_cols,
            bytes_accessed=16 * rows * n_cols,
            transcendentals=0,
        ),
        name="near_half",
    )(
        where,
        *pieces,
        *amps,
        pltpu.with_memory_space_constraint(own, pltpu.HBM),
        pltpu.with_memory_space_constraint(residual, pltpu.HBM),
    )


def far_kernel(offsets, half, flag_ref, *refs):
    amps, (start, far, out, amp, total, sems) = refs[:-6], refs[-6:]
    width = amps[0].shape[2]
    put_in_order(flag_ref[0], amps, offsets, half, amp)
    multiply(amp, far, start, (total, out), sems, 2 * width)


def far_half(flag, amps, offsets, total, far):
    rows, n_cols = total.shape
    depth, width = far.shape[0], amps[0].shape[2]
    vmem = pl.BlockSpec(memory_space=pltpu.VMEM)
    held = 4 * rows * depth + 2 * depth * n_cols + 8 * rows * n_cols
    return pl.pallas_call(
        functools.partial(far_kernel, offsets, depth // width),
        out_shape=jax.ShapeDtypeStruct(total.shape, total.dtype),
        in_specs=[pl.BlockSpec(memory_space=pltpu.SMEM)] + [vmem] * (len(amps) + 2),
        out_specs=pl.BlockSpec(memory_space=pltpu.HBM),
        scratch_shapes=[
            pltpu.VMEM((rows, depth), far.dtype),
            pltpu.VMEM((rows, n_cols), total.dtype),
            pltpu.SemaphoreType.DMA((n_cols // (2 * width),)),
        ],
        compiler_params=pltpu.CompilerParams(vmem_limit_bytes=held + 2 * MIB),
        cost_estimate=pl.CostEstimate(
            flops=2 * rows * depth * n_cols,
            bytes_accessed=16 * rows * n_cols,
            transcendentals=0,
        ),
        name="far_half",
    )(flag[None], *amps, total, far)


def exchange(x, axis, flip):
    size = lax.axis_size(axis)
    return lax.ppermute(x, axis, [(i, i ^ flip) for i in range(size)])


def choose_kernel(flag_ref, pair, out):
    out[0] = pair[flag_ref[0]]


def choose(flag, pair):
    vmem = pl.BlockSpec(memory_space=pltpu.VMEM)
    return pl.pallas_call(
        choose_kernel,
        out_shape=jax.ShapeDtypeStruct((1, *pair.shape[1:]), pair.dtype),
        in_specs=[pl.BlockSpec(memory_space=pltpu.SMEM), vmem],
        out_specs=vmem,
        compiler_params=pltpu.CompilerParams(vmem_limit_bytes=4 * MIB),
        name="choose",
    )(flag[None], pair)


def leave_kernel(flag_ref, beside, own, out, sem):
    @pl.when(flag_ref[0] == 1)
    def _():
        out[...] = beside[...]

    @pl.when(flag_ref[0] == 0)
    def _():
        copy = pltpu.make_async_copy(own, out, sem)
        copy.start()
        copy.wait()


def leave(flag, beside, own):
    vmem = pl.BlockSpec(memory_space=pltpu.VMEM)
    return pl.pallas_call(
        leave_kernel,
        out_shape=jax.ShapeDtypeStruct(beside.shape, beside.dtype),
        in_specs=[
            pl.BlockSpec(memory_space=pltpu.SMEM),
            vmem,
            pl.BlockSpec(memory_space=pltpu.HBM),
        ],
        out_specs=vmem,
        scratch_shapes=[pltpu.SemaphoreType.DMA],
        compiler_params=pltpu.CompilerParams(vmem_limit_bytes=4 * MIB),
        name="leave",
    )(flag[None], beside, pltpu.with_memory_space_constraint(own, pltpu.HBM))


def pick(flag, first, second):
    return choose(1 - flag, join([first, second]))


def tie(late, *early):
    return lax.optimization_barrier((late, *early))


def body(amplitudes, packed_tiles, tile_ids, residual_in):
    n_col, n_row = lax.axis_size("col"), lax.axis_size("row")
    col, row = lax.axis_index("col"), lax.axis_index("row")
    inner = 2 ** (int(math.log2(n_col)) // 2)
    capacity = -(-packed_tiles.shape[1] // n_col)
    half = n_col // 2
    lanes = range(1, inner)
    outgoing = list(pack(col, packed_tiles, tile_ids, n_col, capacity))

    mids = [(i // inner) % 4 in (1, 2) for i in range(n_col)]
    swap = [(i, i ^ (3 * inner) if m else i ^ 1) for i, m in enumerate(mids)]
    own = amplitudes[None]
    across = lax.ppermute(own, "col", swap)
    beside = exchange(own, "col", inner)
    outgoing[half:], across = tie(outgoing[half:], across)

    chunks = [outgoing[0][None]]
    chunks += [exchange(outgoing[s][None], "col", s) for s in range(1, n_col)]
    outer = col // inner % 4
    is_mid = ((outer == 1) | (outer == 2)).astype(jnp.int32)
    onward = exchange(across, "col", inner)
    leaving = leave(is_mid, beside, own)
    own_over = [exchange(own, "col", lane) for lane in lanes]
    chunks[half + 1], own_over, leaving = tie(chunks[half + 1], own_over, leaving)
    straight = exchange(leaving, "col", 2 * inner)
    beside_over = [exchange(beside, "col", lane) for lane in lanes]

    pieces, rows = [], []
    for group in (join(chunks[half:]), join(chunks[:half])):
        passed = [exchange(group, "row", flip) for flip in range(CORES, n_row, CORES)]
        if pieces:
            passed, straight, onward = tie(passed, straight, onward)
        else:
            passed, beside_over = tie(passed, beside_over)
        mine, passed = tie(group, passed)
        for flip, mine in zip(range(0, n_row, CORES), [mine, *passed]):
            pieces += [mine, exchange(mine, "row", 1)]
            rows += [row ^ flip, row ^ flip ^ 1]
    passed_on = pick(is_mid, across, onward)
    passed_over = [exchange(passed_on, "col", lane) for lane in lanes]
    straight_over = [exchange(straight, "col", lane) for lane in lanes]

    def over(shards, ends, middles):
        return [
            (x, [[s ^ lane for s in kind] for kind in (ends, middles)])
            for lane, x in enumerate(shards)
            if x is not None
        ]

    near = over([None, *own_over], [0], [0]) + over([beside, *beside_over], [inner], [inner])
    far = over([passed_on, *passed_over], [2 * inner], [3 * inner])
    far += over([straight, *straight_over], [3 * inner], [2 * inner])
    flip = 4 * inner
    while flip < n_col:
        held = [(own, [[0], [0]]), *near, *far]
        near = near + far
        far = [
            (exchange(x, "col", flip), [[s ^ flip for s in kind] for kind in slots])
            for x, slots in held
        ]
        flip *= 2
    where = jnp.stack([*rows, col, is_mid]).astype(jnp.int32)
    total, far_block = near_half(
        where, pieces, *zip(*near), amplitudes, residual_in, capacity
    )
    return far_half(is_mid, *zip(*far), total, far_block)


def solution(mesh):
    in_specs = (P("row", "col"), P("row", "col", None, None), P("row", "col"), P("row", "col"))
    out_specs = P("row", "col")
    return jax.shard_map(body, mesh=mesh, in_specs=in_specs, out_specs=out_specs, check_vma=False)
```

```python
import functools
import math

import jax
import jax.numpy as jnp
from jax import lax
from jax.experimental import pallas as pl
from jax.experimental.pallas import tpu as pltpu
from jax.sharding import PartitionSpec as P

KT_DEV = 2
QT_DEV = 8
CORES = 2
META = 16
MIB = 1024 * 1024


def pack_kernel(columns, capacity, me_ref, ids_hbm, tiles_hbm, *refs):
    outs = refs[:columns]
    ids_ref, tiles_ref, slot_tile, slot_place, count, ids_sem, tiles_sem = refs[columns:]
    ids_copy = pltpu.make_async_copy(ids_hbm, ids_ref, ids_sem)
    tiles_copy = pltpu.make_async_copy(tiles_hbm, tiles_ref, tiles_sem)
    ids_copy.start()
    tiles_copy.start()
    per_device, width = tiles_ref.shape[1], tiles_ref.shape[2]
    shift = per_device.bit_length() - 1
    for d in range(columns):
        count[d] = 0
        for s in range(capacity):
            slot_place[d * capacity + s] = per_device
    ids_copy.wait()
    for t in range(per_device):
        tile_id = ids_ref[0, t]
        target = lax.shift_right_logical(tile_id, shift)
        rank = count[target]
        count[target] = rank + 1
        slot_tile[target * capacity + rank] = t
        slot_place[target * capacity + rank] = tile_id & (per_device - 1)
    tiles_copy.wait()
    lane = lax.broadcasted_iota(jnp.int32, (META, width), 1)
    for d, out in enumerate(outs):
        target = me_ref[0] ^ d
        row = jnp.full((META, width), per_device, jnp.int32)
        for s in range(capacity):
            place = slot_place[target * capacity + s]
            row = jnp.where(lane == s, place, row)

            @pl.when(place < per_device)
            def _():
                out[s * width : (s + 1) * width, :] = tiles_ref[
                    0, slot_tile[target * capacity + s]
                ]

        out[capacity * width :, :] = row.astype(jnp.float32).astype(jnp.bfloat16)


def pack(col, packed_tiles, tile_ids, columns, capacity):
    _, per_device, width, _ = packed_tiles.shape
    chunk = jax.ShapeDtypeStruct((capacity * width + META, width), packed_tiles.dtype)
    smem = pl.BlockSpec(memory_space=pltpu.SMEM)
    vmem = pl.BlockSpec(memory_space=pltpu.VMEM)
    hbm = pl.BlockSpec(memory_space=pltpu.HBM)
    return pl.pallas_call(
        functools.partial(pack_kernel, columns, capacity),
        out_shape=[chunk] * columns,
        in_specs=[smem, hbm, hbm],
        out_specs=[vmem] * columns,
        scratch_shapes=[
            pltpu.SMEM(tile_ids.shape, jnp.int32),
            pltpu.VMEM(packed_tiles.shape, packed_tiles.dtype),
            pltpu.SMEM((columns * capacity,), jnp.int32),
            pltpu.SMEM((columns * capacity,), jnp.int32),
            pltpu.SMEM((columns,), jnp.int32),
            pltpu.SemaphoreType.DMA,
            pltpu.SemaphoreType.DMA,
        ],
        compiler_params=pltpu.CompilerParams(vmem_limit_bytes=8 * MIB),
        name="pack",
    )(
        col[None],
        pltpu.with_memory_space_constraint(tile_ids, pltpu.HBM),
        pltpu.with_memory_space_constraint(packed_tiles, pltpu.HBM),
    )


def join_kernel(*refs):
    at = 0
    for part in refs[:-1]:
        refs[-1][at : at + part.shape[0]] = part[...]
        at += part.shape[0]


def join(chunks):
    vmem = pl.BlockSpec(memory_space=pltpu.VMEM)
    total = sum(c.shape[0] for c in chunks)
    return pl.pallas_call(
        join_kernel,
        out_shape=jax.ShapeDtypeStruct((total, *chunks[0].shape[1:]), chunks[0].dtype),
        in_specs=[vmem] * len(chunks),
        out_specs=vmem,
        compiler_params=pltpu.CompilerParams(vmem_limit_bytes=8 * MIB),
        name="join",
    )(*chunks)


def multiply(amp, block, first, start, out, sems, step):
    copies = []
    for n in range(block.shape[1] // step):
        cols = slice(n * step, (n + 1) * step)
        held = out[0] if sems is not None else out
        held[:, cols] = start[:, cols] + jnp.dot(
            amp[...],
            block[first : first + amp.shape[1], cols],
            preferred_element_type=jnp.float32,
        )
        if sems is not None:
            part = pl.ds(n * step, step)
            copies.append(
                pltpu.make_async_copy(held.at[:, part], out[1].at[:, part], sems.at[n])
            )
            copies[-1].start()
    for copy in copies:
        copy.wait()


def near_kernel(n_pieces, offsets, capacity, n_columns, where_ref, *refs):
    n_amps = len(offsets)
    pieces = refs[:n_pieces]
    amps = refs[n_pieces : n_pieces + n_amps]
    own, residual, total, block = refs[n_pieces + n_amps : n_pieces + n_amps + 4]
    places, table, amp, res, table_sem, own_sem, res_sem = refs[n_pieces + n_amps + 4 :]
    width = pieces[0].shape[2]
    per_device = KT_DEV * QT_DEV
    own_copy = pltpu.make_async_copy(own, amp.at[:, pl.ds(0, width)], own_sem)
    own_copy.start()
    res_copy = pltpu.make_async_copy(residual, res, res_sem)
    res_copy.start()
    at = 0
    for piece in pieces:
        rows = piece[:, capacity * width :, :]
        places[at : at + piece.shape[0]] = jnp.max(rows.astype(jnp.float32), axis=1).astype(
            jnp.int32
        )
        at += piece.shape[0]
    table_copy = pltpu.make_async_copy(places, table, table_sem)
    table_copy.start()
    for source, slot in zip(amps, offsets):
        amp[:, slot * width : (slot + 1) * width] = source[...]
    table_copy.wait()
    col = where_ref[n_pieces]
    full = capacity * n_columns == per_device
    at = 0
    for p, piece in enumerate(pieces):
        row = where_ref[p]
        for c in range(piece.shape[0]):
            for s in range(capacity):
                position = table[at, s]

                def put(position=position, piece=piece, c=c, s=s, row=row):
                    k = row * KT_DEV + lax.shift_right_logical(
                        position, QT_DEV.bit_length() - 1
                    )
                    q = position & (QT_DEV - 1)
                    block[
                        pl.ds(pl.multiple_of((k ^ col) * width, width), width),
                        pl.ds(pl.multiple_of(q * width, width), width),
                    ] = piece[c, s * width : (s + 1) * width, :]

                if full:
                    put()
                else:
                    pl.when(position < per_device)(put)
            at += 1
    own_copy.wait()
    res_copy.wait()
    multiply(amp, block, 0, res, total, None, 2 * width)


def near_half(where, pieces, amps, offsets, own, residual, capacity):
    width = pieces[0].shape[2]
    n_pieces, n_amps = len(pieces), len(amps)
    chunks = sum(p.shape[0] for p in pieces)
    rows, n_cols = residual.shape
    depth = (1 + n_amps) * width
    hbm = pl.BlockSpec(memory_space=pltpu.HBM)
    vmem = pl.BlockSpec(memory_space=pltpu.VMEM)
    held = 2 * rows * depth + 4 * depth * n_cols + 8 * rows * n_cols
    held += sum(x.size * x.dtype.itemsize for x in pieces) // 2
    return pl.pallas_call(
        functools.partial(near_kernel, n_pieces, offsets, capacity, 1 + 2 * n_amps + 1),
        out_shape=[
            jax.ShapeDtypeStruct(residual.shape, residual.dtype),
            jax.ShapeDtypeStruct((2 * depth, n_cols), pieces[0].dtype),
        ],
        in_specs=[pl.BlockSpec(memory_space=pltpu.SMEM)]
        + [vmem] * (n_pieces + n_amps)
        + [hbm, hbm],
        out_specs=[vmem, vmem],
        scratch_shapes=[
            pltpu.VMEM((chunks, width), jnp.int32),
            pltpu.SMEM((chunks, width), jnp.int32),
            pltpu.VMEM((rows, depth), pieces[0].dtype),
            pltpu.VMEM((rows, n_cols), residual.dtype),
            pltpu.SemaphoreType.DMA,
            pltpu.SemaphoreType.DMA,
            pltpu.SemaphoreType.DMA,
        ],
        compiler_params=pltpu.CompilerParams(vmem_limit_bytes=held + 2 * MIB),
        cost_estimate=pl.CostEstimate(
            flops=2 * rows * depth * n_cols,
            bytes_accessed=16 * rows * n_cols,
            transcendentals=0,
        ),
        name="near_half",
    )(
        where,
        *pieces,
        *amps,
        pltpu.with_memory_space_constraint(own, pltpu.HBM),
        pltpu.with_memory_space_constraint(residual, pltpu.HBM),
    )


def far_kernel(offsets, half, *refs):
    amps = refs[: len(offsets)]
    start, block, out, amp, total, sems = refs[len(offsets) :]
    width = amps[0].shape[1]
    for source, slot in zip(amps, offsets):
        at = (slot - half) * width
        amp[:, at : at + width] = source[...]
    multiply(amp, block, block.shape[0] - amp.shape[1], start, (total, out), sems, 2 * width)


def far_half(amps, offsets, total, block):
    rows, n_cols = total.shape
    depth, width = block.shape[0] // 2, amps[0].shape[1]
    vmem = pl.BlockSpec(memory_space=pltpu.VMEM)
    held = 4 * rows * depth + 4 * depth * n_cols + 8 * rows * n_cols
    return pl.pallas_call(
        functools.partial(far_kernel, offsets, depth // width),
        out_shape=jax.ShapeDtypeStruct(total.shape, total.dtype),
        in_specs=[vmem] * (len(amps) + 2),
        out_specs=pl.BlockSpec(memory_space=pltpu.HBM),
        scratch_shapes=[
            pltpu.VMEM((rows, depth), block.dtype),
            pltpu.VMEM((rows, n_cols), total.dtype),
            pltpu.SemaphoreType.DMA((n_cols // (2 * width),)),
        ],
        compiler_params=pltpu.CompilerParams(vmem_limit_bytes=held + 2 * MIB),
        cost_estimate=pl.CostEstimate(
            flops=2 * rows * depth * n_cols,
            bytes_accessed=16 * rows * n_cols,
            transcendentals=0,
        ),
        name="far_half",
    )(*amps, total, block)


def exchange(x, axis, flip):
    size = lax.axis_size(axis)
    return lax.ppermute(x, axis, [(i, i ^ flip) for i in range(size)])


def tie(late, *early):
    return lax.optimization_barrier((late, *early))


def body(amplitudes, packed_tiles, tile_ids, residual_in):
    n_col, n_row = lax.axis_size("col"), lax.axis_size("row")
    col, row = lax.axis_index("col"), lax.axis_index("row")
    inner = 2 ** (int(math.log2(n_col)) // 2)
    capacity = -(-packed_tiles.shape[1] // n_col)
    half = n_col // 2
    outgoing = list(pack(col, packed_tiles, tile_ids, n_col, capacity))

    amps = {0: amplitudes}
    for s in [half, *range(inner, half, inner), *range(1, inner)]:
        amps[s] = exchange(amplitudes, "col", s)
    outgoing[half:], amps = tie(outgoing[half:], amps)

    chunks = [outgoing[0][None]]
    chunks += [exchange(outgoing[s][None], "col", s) for s in range(1, n_col)]
    for flip in range(inner, half, inner):
        for lane in range(1, inner):
            amps[flip ^ lane] = exchange(amps[flip], "col", lane)
        amps[flip ^ half] = exchange(amps[flip], "col", half)
    for lane in range(1, inner):
        amps[half ^ lane] = exchange(amps[half], "col", lane)

    early = [s for s in amps if s and (s < half or half < s < half + inner)]
    late = [flip ^ half for flip in range(inner, half, inner)]
    flips = range(CORES, n_row, CORES)
    far_groups = [join(chunks[half:])]
    near_group = join(chunks[:half])
    far_passed = [[exchange(g, "row", flip) for flip in flips] for g in far_groups]
    near_passed = [exchange(near_group, "row", flip) for flip in flips]
    near_passed, got = tie(near_passed, [amps[s] for s in late])
    amps.update(zip(late, got))
    far_passed, got = tie(far_passed, [amps[s] for s in early])
    amps.update(zip(early, got))
    pieces, rows = [], []
    for held, passed in (
        (far_groups[0], far_passed[0]),
        (near_group, near_passed),
    ):
        own, passed = tie(held, passed)
        for flip, mine in zip(range(0, n_row, CORES), [own, *passed]):
            pieces += [mine, exchange(mine, "row", 1)]
            rows += [row ^ flip, row ^ flip ^ 1]
    for flip in range(half + inner, n_col, inner):
        for lane in range(1, inner):
            amps[flip ^ lane] = exchange(amps[flip], "col", lane)

    where = jnp.stack(rows + [col]).astype(jnp.int32)
    near = [s for s in sorted(amps) if 0 < s < half]
    far = [s for s in sorted(amps) if s >= half]
    total, far_block = near_half(
        where, pieces, [amps[s] for s in near], near, amplitudes, residual_in, capacity
    )
    return far_half([amps[s] for s in far], far, total, far_block)


def solution(mesh):
    in_specs = (P("row", "col"), P("row", "col", None, None), P("row", "col"), P("row", "col"))
    out_specs = P("row", "col")
    return jax.shard_map(body, mesh=mesh, in_specs=in_specs, out_specs=out_specs, check_vma=False)
```

```python
import functools
import math

import jax
import jax.numpy as jnp
from jax import lax
from jax.experimental import pallas as pl
from jax.experimental.pallas import tpu as pltpu
from jax.sharding import PartitionSpec as P

KT_DEV = 2
QT_DEV = 8
CORES = 2
META = 16
MIB = 1024 * 1024
WEIGHT = 10**9
WEIGHT_FAR = 4 * 10**9


def pack_kernel(columns, capacity, me_ref, ids_hbm, tiles_hbm, *refs):
    outs = refs[:columns]
    ids_ref, tiles_ref, slot_tile, slot_place, count, ids_sem, tiles_sem = refs[columns:]
    ids_copy = pltpu.make_async_copy(ids_hbm, ids_ref, ids_sem)
    tiles_copy = pltpu.make_async_copy(tiles_hbm, tiles_ref, tiles_sem)
    ids_copy.start()
    tiles_copy.start()
    per_device, width = tiles_ref.shape[1], tiles_ref.shape[2]
    shift = per_device.bit_length() - 1
    for d in range(columns):
        count[d] = 0
        for s in range(capacity):
            slot_place[d * capacity + s] = per_device
    ids_copy.wait()
    for t in range(per_device):
        tile_id = ids_ref[0, t]
        target = lax.shift_right_logical(tile_id, shift)
        rank = count[target]
        count[target] = rank + 1
        slot_tile[target * capacity + rank] = t
        slot_place[target * capacity + rank] = tile_id & (per_device - 1)
    tiles_copy.wait()
    lane = lax.broadcasted_iota(jnp.int32, (META, width), 1)
    for d, out in enumerate(outs):
        target = me_ref[0] ^ d
        row = jnp.full((META, width), per_device, jnp.int32)
        for s in range(capacity):
            place = slot_place[target * capacity + s]
            row = jnp.where(lane == s, place, row)

            @pl.when(place < per_device)
            def _():
                out[s * width : (s + 1) * width, :] = tiles_ref[
                    0, slot_tile[target * capacity + s]
                ]

        out[capacity * width :, :] = row.astype(jnp.float32).astype(jnp.bfloat16)


def pack(col, packed_tiles, tile_ids, columns, capacity):
    _, per_device, width, _ = packed_tiles.shape
    chunk = jax.ShapeDtypeStruct((capacity * width + META, width), packed_tiles.dtype)
    smem = pl.BlockSpec(memory_space=pltpu.SMEM)
    vmem = pl.BlockSpec(memory_space=pltpu.VMEM)
    hbm = pl.BlockSpec(memory_space=pltpu.HBM)
    return pl.pallas_call(
        functools.partial(pack_kernel, columns, capacity),
        out_shape=[chunk] * columns,
        in_specs=[smem, hbm, hbm],
        out_specs=[vmem] * columns,
        scratch_shapes=[
            pltpu.SMEM(tile_ids.shape, jnp.int32),
            pltpu.VMEM(packed_tiles.shape, packed_tiles.dtype),
            pltpu.SMEM((columns * capacity,), jnp.int32),
            pltpu.SMEM((columns * capacity,), jnp.int32),
            pltpu.SMEM((columns,), jnp.int32),
            pltpu.SemaphoreType.DMA,
            pltpu.SemaphoreType.DMA,
        ],
        compiler_params=pltpu.CompilerParams(vmem_limit_bytes=8 * MIB),
        name="pack",
    )(
        col[None],
        pltpu.with_memory_space_constraint(tile_ids, pltpu.HBM),
        pltpu.with_memory_space_constraint(packed_tiles, pltpu.HBM),
    )


def join_kernel(*refs):
    at = 0
    for part in refs[:-1]:
        refs[-1][at : at + part.shape[0]] = part[...]
        at += part.shape[0]


def join(chunks, flops=0):
    vmem = pl.BlockSpec(memory_space=pltpu.VMEM)
    total = sum(c.shape[0] for c in chunks)
    return pl.pallas_call(
        join_kernel,
        out_shape=jax.ShapeDtypeStruct((total, *chunks[0].shape[1:]), chunks[0].dtype),
        in_specs=[vmem] * len(chunks),
        out_specs=vmem,
        compiler_params=pltpu.CompilerParams(vmem_limit_bytes=8 * MIB),
        cost_estimate=pl.CostEstimate(flops=flops, bytes_accessed=0, transcendentals=0),
        name="join",
    )(*chunks)


def multiply(amp, block, first, start, out, sems, step):
    copies = []
    for n in range(block.shape[1] // step):
        cols = slice(n * step, (n + 1) * step)
        held = out[0] if sems is not None else out
        held[:, cols] = start[:, cols] + jnp.dot(
            amp[...],
            block[first : first + amp.shape[1], cols],
            preferred_element_type=jnp.float32,
        )
        if sems is not None:
            part = pl.ds(n * step, step)
            copies.append(
                pltpu.make_async_copy(held.at[:, part], out[1].at[:, part], sems.at[n])
            )
            copies[-1].start()
    for copy in copies:
        copy.wait()


def near_kernel(n_pieces, offsets, capacity, n_columns, where_ref, *refs):
    n_amps = len(offsets)
    pieces = refs[:n_pieces]
    amps = refs[n_pieces : n_pieces + n_amps]
    own, residual, total, block = refs[n_pieces + n_amps : n_pieces + n_amps + 4]
    places, table, amp, res, table_sem, own_sem, res_sem = refs[n_pieces + n_amps + 4 :]
    width = pieces[0].shape[2]
    per_device = KT_DEV * QT_DEV
    own_copy = pltpu.make_async_copy(own, amp.at[:, pl.ds(0, width)], own_sem)
    own_copy.start()
    res_copy = pltpu.make_async_copy(residual, res, res_sem)
    res_copy.start()
    at = 0
    for piece in pieces:
        rows = piece[:, capacity * width :, :]
        places[at : at + piece.shape[0]] = jnp.max(rows.astype(jnp.float32), axis=1).astype(
            jnp.int32
        )
        at += piece.shape[0]
    table_copy = pltpu.make_async_copy(places, table, table_sem)
    table_copy.start()
    for source, slot in zip(amps, offsets):
        amp[:, slot * width : (slot + 1) * width] = source[...]
    table_copy.wait()
    col = where_ref[n_pieces]
    full = capacity * n_columns == per_device
    at = 0
    for p, piece in enumerate(pieces):
        row = where_ref[p]
        for c in range(piece.shape[0]):
            for s in range(capacity):
                position = table[at, s]

                def put(position=position, piece=piece, c=c, s=s, row=row):
                    k = row * KT_DEV + lax.shift_right_logical(
                        position, QT_DEV.bit_length() - 1
                    )
                    q = position & (QT_DEV - 1)
                    block[
                        pl.ds(pl.multiple_of((k ^ col) * width, width), width),
                        pl.ds(pl.multiple_of(q * width, width), width),
                    ] = piece[c, s * width : (s + 1) * width, :]

                if full:
                    put()
                else:
                    pl.when(position < per_device)(put)
            at += 1
    own_copy.wait()
    res_copy.wait()
    multiply(amp, block, 0, res, total, None, 2 * width)


def near_half(where, pieces, amps, offsets, own, residual, capacity):
    width = pieces[0].shape[2]
    n_pieces, n_amps = len(pieces), len(amps)
    chunks = sum(p.shape[0] for p in pieces)
    rows, n_cols = residual.shape
    depth = (1 + n_amps) * width
    hbm = pl.BlockSpec(memory_space=pltpu.HBM)
    vmem = pl.BlockSpec(memory_space=pltpu.VMEM)
    held = 2 * rows * depth + 4 * depth * n_cols + 8 * rows * n_cols
    held += sum(x.size * x.dtype.itemsize for x in pieces) // 2
    return pl.pallas_call(
        functools.partial(near_kernel, n_pieces, offsets, capacity, 1 + 2 * n_amps + 1),
        out_shape=[
            jax.ShapeDtypeStruct(residual.shape, residual.dtype),
            jax.ShapeDtypeStruct((2 * depth, n_cols), pieces[0].dtype),
        ],
        in_specs=[pl.BlockSpec(memory_space=pltpu.SMEM)]
        + [vmem] * (n_pieces + n_amps)
        + [hbm, hbm],
        out_specs=[vmem, vmem],
        scratch_shapes=[
            pltpu.VMEM((chunks, width), jnp.int32),
            pltpu.SMEM((chunks, width), jnp.int32),
            pltpu.VMEM((rows, depth), pieces[0].dtype),
            pltpu.VMEM((rows, n_cols), residual.dtype),
            pltpu.SemaphoreType.DMA,
            pltpu.SemaphoreType.DMA,
            pltpu.SemaphoreType.DMA,
        ],
        compiler_params=pltpu.CompilerParams(vmem_limit_bytes=held + 2 * MIB),
        cost_estimate=pl.CostEstimate(
            flops=2 * rows * depth * n_cols,
            bytes_accessed=16 * rows * n_cols,
            transcendentals=0,
        ),
        name="near_half",
    )(
        where,
        *pieces,
        *amps,
        pltpu.with_memory_space_constraint(own, pltpu.HBM),
        pltpu.with_memory_space_constraint(residual, pltpu.HBM),
    )


def far_kernel(offsets, half, *refs):
    amps = refs[: len(offsets)]
    start, block, out, amp, total, sems = refs[len(offsets) :]
    width = amps[0].shape[1]
    for source, slot in zip(amps, offsets):
        at = (slot - half) * width
        amp[:, at : at + width] = source[...]
    multiply(amp, block, block.shape[0] - amp.shape[1], start, (total, out), sems, 2 * width)


def far_half(amps, offsets, total, block):
    rows, n_cols = total.shape
    depth, width = block.shape[0] // 2, amps[0].shape[1]
    vmem = pl.BlockSpec(memory_space=pltpu.VMEM)
    held = 4 * rows * depth + 4 * depth * n_cols + 8 * rows * n_cols
    return pl.pallas_call(
        functools.partial(far_kernel, offsets, depth // width),
        out_shape=jax.ShapeDtypeStruct(total.shape, total.dtype),
        in_specs=[vmem] * (len(amps) + 2),
        out_specs=pl.BlockSpec(memory_space=pltpu.HBM),
        scratch_shapes=[
            pltpu.VMEM((rows, depth), block.dtype),
            pltpu.VMEM((rows, n_cols), total.dtype),
            pltpu.SemaphoreType.DMA((n_cols // (2 * width),)),
        ],
        compiler_params=pltpu.CompilerParams(vmem_limit_bytes=held + 2 * MIB),
        cost_estimate=pl.CostEstimate(
            flops=2 * rows * depth * n_cols,
            bytes_accessed=16 * rows * n_cols,
            transcendentals=0,
        ),
        name="far_half",
    )(*amps, total, block)


def exchange(x, axis, flip):
    size = lax.axis_size(axis)
    return lax.ppermute(x, axis, [(i, i ^ flip) for i in range(size)])


def tie(late, *early):
    return lax.optimization_barrier((late, *early))


def body(amplitudes, packed_tiles, tile_ids, residual_in):
    n_col, n_row = lax.axis_size("col"), lax.axis_size("row")
    col, row = lax.axis_index("col"), lax.axis_index("row")
    inner = 2 ** (int(math.log2(n_col)) // 2)
    capacity = -(-packed_tiles.shape[1] // n_col)
    half = n_col // 2
    outgoing = list(pack(col, packed_tiles, tile_ids, n_col, capacity))

    amps = {0: amplitudes}
    for s in [*range(1, inner), *range(inner, half, inner), half]:
        amps[s] = exchange(amplitudes, "col", s)
    outgoing[half:], amps = tie(outgoing[half:], amps)

    chunks = [outgoing[0][None]]
    chunks += [exchange(outgoing[s][None], "col", s) for s in range(1, n_col)]
    for flip in range(inner, half, inner):
        for lane in range(1, inner):
            amps[flip ^ lane] = exchange(amps[flip], "col", lane)
        amps[flip ^ half] = exchange(amps[flip], "col", half)
    for lane in range(1, inner):
        amps[half ^ lane] = exchange(amps[half], "col", lane)

    early = [s for s in amps if s and (s < half or half < s < half + inner)]
    flips = range(CORES, n_row, CORES)
    cut = half + half // 2
    far_groups = [join(chunks[half:cut], WEIGHT), join(chunks[cut:], WEIGHT)]
    near_group = join(chunks[:half])
    far_passed = [[exchange(g, "row", flip) for flip in flips] for g in far_groups]
    near_passed = [exchange(near_group, "row", flip) for flip in flips]
    far_passed, got = tie(far_passed, [amps[s] for s in early])
    amps.update(zip(early, got))
    pieces, rows = [], []
    for held, passed in (
        (join(far_groups), [join(x) for x in zip(*far_passed)]),
        (near_group, near_passed),
    ):
        own, passed = tie(held, passed)
        for flip, mine in zip(range(0, n_row, CORES), [own, *passed]):
            pieces += [mine, exchange(mine, "row", 1)]
            rows += [row ^ flip, row ^ flip ^ 1]
    for flip in range(half + inner, n_col, inner):
        there = join([amps[flip]], WEIGHT_FAR)
        for lane in range(1, inner):
            amps[flip ^ lane] = exchange(there, "col", lane)

    where = jnp.stack(rows + [col]).astype(jnp.int32)
    near = [s for s in sorted(amps) if 0 < s < half]
    far = [s for s in sorted(amps) if s >= half]
    total, far_block = near_half(
        where, pieces, [amps[s] for s in near], near, amplitudes, residual_in, capacity
    )
    return far_half([amps[s] for s in far], far, total, far_block)


def solution(mesh):
    in_specs = (P("row", "col"), P("row", "col", None, None), P("row", "col"), P("row", "col"))
    out_specs = P("row", "col")
    return jax.shard_map(body, mesh=mesh, in_specs=in_specs, out_specs=out_specs, check_vma=False)
```

```python
import functools
import math

import jax
import jax.numpy as jnp
from jax import lax
from jax.experimental import pallas as pl
from jax.experimental.pallas import tpu as pltpu
from jax.sharding import PartitionSpec as P

KT_DEV = 2
QT_DEV = 8
CORES = 2
META = 16
MIB = 1024 * 1024
WEIGHT = 10**9
WEIGHT_FAR = 4 * 10**9
WEIGHT_LATE = 10**9


def pack_kernel(columns, capacity, me_ref, ids_hbm, tiles_hbm, *refs):
    outs = refs[:columns]
    ids_ref, tiles_ref, slot_tile, slot_place, count, ids_sem, tiles_sem = refs[columns:]
    ids_copy = pltpu.make_async_copy(ids_hbm, ids_ref, ids_sem)
    tiles_copy = pltpu.make_async_copy(tiles_hbm, tiles_ref, tiles_sem)
    ids_copy.start()
    tiles_copy.start()
    per_device, width = tiles_ref.shape[1], tiles_ref.shape[2]
    shift = per_device.bit_length() - 1
    for d in range(columns):
        count[d] = 0
        for s in range(capacity):
            slot_place[d * capacity + s] = per_device
    ids_copy.wait()
    for t in range(per_device):
        tile_id = ids_ref[0, t]
        target = lax.shift_right_logical(tile_id, shift)
        rank = count[target]
        count[target] = rank + 1
        slot_tile[target * capacity + rank] = t
        slot_place[target * capacity + rank] = tile_id & (per_device - 1)
    tiles_copy.wait()
    lane = lax.broadcasted_iota(jnp.int32, (META, width), 1)
    for d, out in enumerate(outs):
        target = me_ref[0] ^ d
        row = jnp.full((META, width), per_device, jnp.int32)
        for s in range(capacity):
            place = slot_place[target * capacity + s]
            row = jnp.where(lane == s, place, row)

            @pl.when(place < per_device)
            def _():
                out[s * width : (s + 1) * width, :] = tiles_ref[
                    0, slot_tile[target * capacity + s]
                ]

        out[capacity * width :, :] = row.astype(jnp.float32).astype(jnp.bfloat16)


def pack(col, packed_tiles, tile_ids, columns, capacity):
    _, per_device, width, _ = packed_tiles.shape
    chunk = jax.ShapeDtypeStruct((capacity * width + META, width), packed_tiles.dtype)
    smem = pl.BlockSpec(memory_space=pltpu.SMEM)
    vmem = pl.BlockSpec(memory_space=pltpu.VMEM)
    hbm = pl.BlockSpec(memory_space=pltpu.HBM)
    return pl.pallas_call(
        functools.partial(pack_kernel, columns, capacity),
        out_shape=[chunk] * columns,
        in_specs=[smem, hbm, hbm],
        out_specs=[vmem] * columns,
        scratch_shapes=[
            pltpu.SMEM(tile_ids.shape, jnp.int32),
            pltpu.VMEM(packed_tiles.shape, packed_tiles.dtype),
            pltpu.SMEM((columns * capacity,), jnp.int32),
            pltpu.SMEM((columns * capacity,), jnp.int32),
            pltpu.SMEM((columns,), jnp.int32),
            pltpu.SemaphoreType.DMA,
            pltpu.SemaphoreType.DMA,
        ],
        compiler_params=pltpu.CompilerParams(vmem_limit_bytes=8 * MIB),
        name="pack",
    )(
        col[None],
        pltpu.with_memory_space_constraint(tile_ids, pltpu.HBM),
        pltpu.with_memory_space_constraint(packed_tiles, pltpu.HBM),
    )


def join_kernel(*refs):
    at = 0
    for part in refs[:-1]:
        refs[-1][at : at + part.shape[0]] = part[...]
        at += part.shape[0]


def join(chunks, flops=0):
    vmem = pl.BlockSpec(memory_space=pltpu.VMEM)
    total = sum(c.shape[0] for c in chunks)
    return pl.pallas_call(
        join_kernel,
        out_shape=jax.ShapeDtypeStruct((total, *chunks[0].shape[1:]), chunks[0].dtype),
        in_specs=[vmem] * len(chunks),
        out_specs=vmem,
        compiler_params=pltpu.CompilerParams(vmem_limit_bytes=8 * MIB),
        cost_estimate=pl.CostEstimate(flops=flops, bytes_accessed=0, transcendentals=0),
        name="join",
    )(*chunks)


def multiply(amp, block, first, start, out, sems, step):
    copies = []
    for n in range(block.shape[1] // step):
        cols = slice(n * step, (n + 1) * step)
        held = out[0] if sems is not None else out
        held[:, cols] = start[:, cols] + jnp.dot(
            amp[...],
            block[first : first + amp.shape[1], cols],
            preferred_element_type=jnp.float32,
        )
        if sems is not None:
            part = pl.ds(n * step, step)
            copies.append(
                pltpu.make_async_copy(held.at[:, part], out[1].at[:, part], sems.at[n])
            )
            copies[-1].start()
    for copy in copies:
        copy.wait()


def near_kernel(n_pieces, offsets, capacity, n_columns, where_ref, *refs):
    n_amps = len(offsets)
    pieces = refs[:n_pieces]
    amps = refs[n_pieces : n_pieces + n_amps]
    own, residual, total, block = refs[n_pieces + n_amps : n_pieces + n_amps + 4]
    places, table, amp, res, table_sem, own_sem, res_sem = refs[n_pieces + n_amps + 4 :]
    width = pieces[0].shape[2]
    per_device = KT_DEV * QT_DEV
    own_copy = pltpu.make_async_copy(own, amp.at[:, pl.ds(0, width)], own_sem)
    own_copy.start()
    res_copy = pltpu.make_async_copy(residual, res, res_sem)
    res_copy.start()
    at = 0
    for piece in pieces:
        rows = piece[:, capacity * width :, :]
        places[at : at + piece.shape[0]] = jnp.max(rows.astype(jnp.float32), axis=1).astype(
            jnp.int32
        )
        at += piece.shape[0]
    table_copy = pltpu.make_async_copy(places, table, table_sem)
    table_copy.start()
    for source, slot in zip(amps, offsets):
        amp[:, slot * width : (slot + 1) * width] = source[...]
    table_copy.wait()
    col = where_ref[n_pieces]
    full = capacity * n_columns == per_device
    at = 0
    for p, piece in enumerate(pieces):
        row = where_ref[p]
        for c in range(piece.shape[0]):
            for s in range(capacity):
                position = table[at, s]

                def put(position=position, piece=piece, c=c, s=s, row=row):
                    k = row * KT_DEV + lax.shift_right_logical(
                        position, QT_DEV.bit_length() - 1
                    )
                    q = position & (QT_DEV - 1)
                    block[
                        pl.ds(pl.multiple_of((k ^ col) * width, width), width),
                        pl.ds(pl.multiple_of(q * width, width), width),
                    ] = piece[c, s * width : (s + 1) * width, :]

                if full:
                    put()
                else:
                    pl.when(position < per_device)(put)
            at += 1
    own_copy.wait()
    res_copy.wait()
    multiply(amp, block, 0, res, total, None, 2 * width)


def near_half(where, pieces, amps, offsets, own, residual, capacity):
    width = pieces[0].shape[2]
    n_pieces, n_amps = len(pieces), len(amps)
    chunks = sum(p.shape[0] for p in pieces)
    rows, n_cols = residual.shape
    depth = (1 + n_amps) * width
    hbm = pl.BlockSpec(memory_space=pltpu.HBM)
    vmem = pl.BlockSpec(memory_space=pltpu.VMEM)
    held = 2 * rows * depth + 4 * depth * n_cols + 8 * rows * n_cols
    held += sum(x.size * x.dtype.itemsize for x in pieces) // 2
    return pl.pallas_call(
        functools.partial(near_kernel, n_pieces, offsets, capacity, 1 + 2 * n_amps + 1),
        out_shape=[
            jax.ShapeDtypeStruct(residual.shape, residual.dtype),
            jax.ShapeDtypeStruct((2 * depth, n_cols), pieces[0].dtype),
        ],
        in_specs=[pl.BlockSpec(memory_space=pltpu.SMEM)]
        + [vmem] * (n_pieces + n_amps)
        + [hbm, hbm],
        out_specs=[vmem, vmem],
        scratch_shapes=[
            pltpu.VMEM((chunks, width), jnp.int32),
            pltpu.SMEM((chunks, width), jnp.int32),
            pltpu.VMEM((rows, depth), pieces[0].dtype),
            pltpu.VMEM((rows, n_cols), residual.dtype),
            pltpu.SemaphoreType.DMA,
            pltpu.SemaphoreType.DMA,
            pltpu.SemaphoreType.DMA,
        ],
        compiler_params=pltpu.CompilerParams(vmem_limit_bytes=held + 2 * MIB),
        cost_estimate=pl.CostEstimate(
            flops=2 * rows * depth * n_cols,
            bytes_accessed=16 * rows * n_cols,
            transcendentals=0,
        ),
        name="near_half",
    )(
        where,
        *pieces,
        *amps,
        pltpu.with_memory_space_constraint(own, pltpu.HBM),
        pltpu.with_memory_space_constraint(residual, pltpu.HBM),
    )


def far_kernel(offsets, half, *refs):
    amps = refs[: len(offsets)]
    start, block, out, amp, total, sems = refs[len(offsets) :]
    width = amps[0].shape[1]
    for source, slot in zip(amps, offsets):
        at = (slot - half) * width
        amp[:, at : at + width] = source[...]
    multiply(amp, block, block.shape[0] - amp.shape[1], start, (total, out), sems, 2 * width)


def far_half(amps, offsets, total, block):
    rows, n_cols = total.shape
    depth, width = block.shape[0] // 2, amps[0].shape[1]
    vmem = pl.BlockSpec(memory_space=pltpu.VMEM)
    held = 4 * rows * depth + 4 * depth * n_cols + 8 * rows * n_cols
    return pl.pallas_call(
        functools.partial(far_kernel, offsets, depth // width),
        out_shape=jax.ShapeDtypeStruct(total.shape, total.dtype),
        in_specs=[vmem] * (len(amps) + 2),
        out_specs=pl.BlockSpec(memory_space=pltpu.HBM),
        scratch_shapes=[
            pltpu.VMEM((rows, depth), block.dtype),
            pltpu.VMEM((rows, n_cols), total.dtype),
            pltpu.SemaphoreType.DMA((n_cols // (2 * width),)),
        ],
        compiler_params=pltpu.CompilerParams(vmem_limit_bytes=held + 2 * MIB),
        cost_estimate=pl.CostEstimate(
            flops=2 * rows * depth * n_cols,
            bytes_accessed=16 * rows * n_cols,
            transcendentals=0,
        ),
        name="far_half",
    )(*amps, total, block)


def exchange(x, axis, flip):
    size = lax.axis_size(axis)
    return lax.ppermute(x, axis, [(i, i ^ flip) for i in range(size)])


def tie(late, *early):
    return lax.optimization_barrier((late, *early))


def body(amplitudes, packed_tiles, tile_ids, residual_in):
    n_col, n_row = lax.axis_size("col"), lax.axis_size("row")
    col, row = lax.axis_index("col"), lax.axis_index("row")
    inner = 2 ** (int(math.log2(n_col)) // 2)
    capacity = -(-packed_tiles.shape[1] // n_col)
    half = n_col // 2
    outgoing = list(pack(col, packed_tiles, tile_ids, n_col, capacity))

    amps = {0: amplitudes}
    for s in [*range(1, inner), *range(inner, half, inner), half]:
        amps[s] = exchange(amplitudes, "col", s)
    order = sorted(amps, reverse=True)[:-1]
    outgoing[half:], got = tie(outgoing[half:], [amps[s] for s in order])
    amps.update(zip(order, got))

    chunks = [outgoing[0][None]]
    chunks += [exchange(outgoing[s][None], "col", s) for s in range(1, n_col)]
    for flip in range(inner, half, inner):
        for lane in range(1, inner):
            amps[flip ^ lane] = exchange(amps[flip], "col", lane)
        amps[flip ^ half] = exchange(amps[flip], "col", half)
    for lane in range(1, inner):
        amps[half ^ lane] = exchange(amps[half], "col", lane)

    early = [s for s in amps if 0 < s < half]
    late = [s for s in amps if half < s < half + inner]
    flips = range(CORES, n_row, CORES)
    cut = half + half // 2
    far_groups = [join(chunks[half:cut], WEIGHT), join(chunks[cut:], WEIGHT)]
    near_group = join(chunks[:half])
    far_passed = [[exchange(g, "row", flip) for flip in flips] for g in far_groups]
    near_passed = [exchange(near_group, "row", flip) for flip in flips]
    for s in late:
        amps[s] = join([amps[s]], WEIGHT_LATE)
    far_passed, got = tie(far_passed, [amps[s] for s in early])
    amps.update(zip(early, got))
    pieces, rows = [], []
    for held, passed in (
        (join(far_groups), [join(x) for x in zip(*far_passed)]),
        (near_group, near_passed),
    ):
        own, passed = tie(held, passed)
        for flip, mine in zip(range(0, n_row, CORES), [own, *passed]):
            pieces += [mine, exchange(mine, "row", 1)]
            rows += [row ^ flip, row ^ flip ^ 1]
    for flip in range(half + inner, n_col, inner):
        there = join([amps[flip]], WEIGHT_FAR)
        for lane in range(1, inner):
            amps[flip ^ lane] = exchange(there, "col", lane)

    where = jnp.stack(rows + [col]).astype(jnp.int32)
    near = [s for s in sorted(amps) if 0 < s < half]
    far = [s for s in sorted(amps) if s >= half]
    total, far_block = near_half(
        where, pieces, [amps[s] for s in near], near, amplitudes, residual_in, capacity
    )
    return far_half([amps[s] for s in far], far, total, far_block)


def solution(mesh):
    in_specs = (P("row", "col"), P("row", "col", None, None), P("row", "col"), P("row", "col"))
    out_specs = P("row", "col")
    return jax.shard_map(body, mesh=mesh, in_specs=in_specs, out_specs=out_specs, check_vma=False)
```

```python
import functools
import math

import jax
import jax.numpy as jnp
from jax import lax
from jax.experimental import pallas as pl
from jax.experimental.pallas import tpu as pltpu
from jax.sharding import PartitionSpec as P

KT_DEV = 2
QT_DEV = 8
CORES = 2
META = 16
MIB = 1024 * 1024
WEIGHT = 10**9
WEIGHT_FAR = 4 * 10**9


def pack_kernel(columns, capacity, me_ref, ids_hbm, tiles_hbm, *refs):
    outs = refs[:columns]
    ids_ref, tiles_ref, slot_tile, slot_place, count, ids_sem, tiles_sem = refs[columns:]
    ids_copy = pltpu.make_async_copy(ids_hbm, ids_ref, ids_sem)
    tiles_copy = pltpu.make_async_copy(tiles_hbm, tiles_ref, tiles_sem)
    ids_copy.start()
    tiles_copy.start()
    per_device, width = tiles_ref.shape[1], tiles_ref.shape[2]
    shift = per_device.bit_length() - 1
    for d in range(columns):
        count[d] = 0
        for s in range(capacity):
            slot_place[d * capacity + s] = per_device
    ids_copy.wait()
    for t in range(per_device):
        tile_id = ids_ref[0, t]
        target = lax.shift_right_logical(tile_id, shift)
        rank = count[target]
        count[target] = rank + 1
        slot_tile[target * capacity + rank] = t
        slot_place[target * capacity + rank] = tile_id & (per_device - 1)
    tiles_copy.wait()
    lane = lax.broadcasted_iota(jnp.int32, (META, width), 1)
    for d, out in enumerate(outs):
        target = me_ref[0] ^ d
        row = jnp.full((META, width), per_device, jnp.int32)
        for s in range(capacity):
            place = slot_place[target * capacity + s]
            row = jnp.where(lane == s, place, row)

            @pl.when(place < per_device)
            def _():
                out[s * width : (s + 1) * width, :] = tiles_ref[
                    0, slot_tile[target * capacity + s]
                ]

        out[capacity * width :, :] = row.astype(jnp.float32).astype(jnp.bfloat16)


def pack(col, packed_tiles, tile_ids, columns, capacity):
    _, per_device, width, _ = packed_tiles.shape
    chunk = jax.ShapeDtypeStruct((capacity * width + META, width), packed_tiles.dtype)
    smem = pl.BlockSpec(memory_space=pltpu.SMEM)
    vmem = pl.BlockSpec(memory_space=pltpu.VMEM)
    hbm = pl.BlockSpec(memory_space=pltpu.HBM)
    return pl.pallas_call(
        functools.partial(pack_kernel, columns, capacity),
        out_shape=[chunk] * columns,
        in_specs=[smem, hbm, hbm],
        out_specs=[vmem] * columns,
        scratch_shapes=[
            pltpu.SMEM(tile_ids.shape, jnp.int32),
            pltpu.VMEM(packed_tiles.shape, packed_tiles.dtype),
            pltpu.SMEM((columns * capacity,), jnp.int32),
            pltpu.SMEM((columns * capacity,), jnp.int32),
            pltpu.SMEM((columns,), jnp.int32),
            pltpu.SemaphoreType.DMA,
            pltpu.SemaphoreType.DMA,
        ],
        compiler_params=pltpu.CompilerParams(vmem_limit_bytes=8 * MIB),
        name="pack",
    )(
        col[None],
        pltpu.with_memory_space_constraint(tile_ids, pltpu.HBM),
        pltpu.with_memory_space_constraint(packed_tiles, pltpu.HBM),
    )


def join_kernel(*refs):
    at = 0
    for part in refs[:-1]:
        refs[-1][at : at + part.shape[0]] = part[...]
        at += part.shape[0]


def join(chunks, flops=0):
    vmem = pl.BlockSpec(memory_space=pltpu.VMEM)
    total = sum(c.shape[0] for c in chunks)
    return pl.pallas_call(
        join_kernel,
        out_shape=jax.ShapeDtypeStruct((total, *chunks[0].shape[1:]), chunks[0].dtype),
        in_specs=[vmem] * len(chunks),
        out_specs=vmem,
        compiler_params=pltpu.CompilerParams(vmem_limit_bytes=8 * MIB),
        cost_estimate=pl.CostEstimate(flops=flops, bytes_accessed=0, transcendentals=0),
        name="join",
    )(*chunks)


def multiply(amp, block, first, start, out, sems, step):
    copies = []
    for n in range(block.shape[1] // step):
        cols = slice(n * step, (n + 1) * step)
        held = out[0] if sems is not None else out
        held[:, cols] = start[:, cols] + jnp.dot(
            amp[...],
            block[first : first + amp.shape[1], cols],
            preferred_element_type=jnp.float32,
        )
        if sems is not None:
            part = pl.ds(n * step, step)
            copies.append(
                pltpu.make_async_copy(held.at[:, part], out[1].at[:, part], sems.at[n])
            )
            copies[-1].start()
    for copy in copies:
        copy.wait()


def near_kernel(n_pieces, offsets, capacity, n_columns, where_ref, *refs):
    n_amps = len(offsets)
    pieces = refs[:n_pieces]
    amps = refs[n_pieces : n_pieces + n_amps]
    own, residual, total, block = refs[n_pieces + n_amps : n_pieces + n_amps + 4]
    places, table, amp, res, table_sem, own_sem, res_sem = refs[n_pieces + n_amps + 4 :]
    width = pieces[0].shape[2]
    per_device = KT_DEV * QT_DEV
    own_copy = pltpu.make_async_copy(own, amp.at[:, pl.ds(0, width)], own_sem)
    own_copy.start()
    res_copy = pltpu.make_async_copy(residual, res, res_sem)
    res_copy.start()
    at = 0
    for piece in pieces:
        rows = piece[:, capacity * width :, :]
        places[at : at + piece.shape[0]] = jnp.max(rows.astype(jnp.float32), axis=1).astype(
            jnp.int32
        )
        at += piece.shape[0]
    table_copy = pltpu.make_async_copy(places, table, table_sem)
    table_copy.start()
    for source, slot in zip(amps, offsets):
        amp[:, slot * width : (slot + 1) * width] = source[...]
    table_copy.wait()
    col = where_ref[n_pieces]
    full = capacity * n_columns == per_device
    at = 0
    for p, piece in enumerate(pieces):
        row = where_ref[p]
        for c in range(piece.shape[0]):
            for s in range(capacity):
                position = table[at, s]

                def put(position=position, piece=piece, c=c, s=s, row=row):
                    k = row * KT_DEV + lax.shift_right_logical(
                        position, QT_DEV.bit_length() - 1
                    )
                    q = position & (QT_DEV - 1)
                    block[
                        pl.ds(pl.multiple_of((k ^ col) * width, width), width),
                        pl.ds(pl.multiple_of(q * width, width), width),
                    ] = piece[c, s * width : (s + 1) * width, :]

                if full:
                    put()
                else:
                    pl.when(position < per_device)(put)
            at += 1
    own_copy.wait()
    res_copy.wait()
    multiply(amp, block, 0, res, total, None, 2 * width)


def near_half(where, pieces, amps, offsets, own, residual, capacity):
    width = pieces[0].shape[2]
    n_pieces, n_amps = len(pieces), len(amps)
    chunks = sum(p.shape[0] for p in pieces)
    rows, n_cols = residual.shape
    depth = (1 + n_amps) * width
    hbm = pl.BlockSpec(memory_space=pltpu.HBM)
    vmem = pl.BlockSpec(memory_space=pltpu.VMEM)
    held = 2 * rows * depth + 4 * depth * n_cols + 8 * rows * n_cols
    held += sum(x.size * x.dtype.itemsize for x in pieces) // 2
    return pl.pallas_call(
        functools.partial(near_kernel, n_pieces, offsets, capacity, 1 + 2 * n_amps + 1),
        out_shape=[
            jax.ShapeDtypeStruct(residual.shape, residual.dtype),
            jax.ShapeDtypeStruct((2 * depth, n_cols), pieces[0].dtype),
        ],
        in_specs=[pl.BlockSpec(memory_space=pltpu.SMEM)]
        + [vmem] * (n_pieces + n_amps)
        + [hbm, hbm],
        out_specs=[vmem, vmem],
        scratch_shapes=[
            pltpu.VMEM((chunks, width), jnp.int32),
            pltpu.SMEM((chunks, width), jnp.int32),
            pltpu.VMEM((rows, depth), pieces[0].dtype),
            pltpu.VMEM((rows, n_cols), residual.dtype),
            pltpu.SemaphoreType.DMA,
            pltpu.SemaphoreType.DMA,
            pltpu.SemaphoreType.DMA,
        ],
        compiler_params=pltpu.CompilerParams(vmem_limit_bytes=held + 2 * MIB),
        cost_estimate=pl.CostEstimate(
            flops=2 * rows * depth * n_cols,
            bytes_accessed=16 * rows * n_cols,
            transcendentals=0,
        ),
        name="near_half",
    )(
        where,
        *pieces,
        *amps,
        pltpu.with_memory_space_constraint(own, pltpu.HBM),
        pltpu.with_memory_space_constraint(residual, pltpu.HBM),
    )


def far_kernel(offsets, half, *refs):
    amps = refs[: len(offsets)]
    start, block, out, amp, total, sems = refs[len(offsets) :]
    width = amps[0].shape[1]
    for source, slot in zip(amps, offsets):
        at = (slot - half) * width
        amp[:, at : at + width] = source[...]
    multiply(amp, block, block.shape[0] - amp.shape[1], start, (total, out), sems, 2 * width)


def far_half(amps, offsets, total, block):
    rows, n_cols = total.shape
    depth, width = block.shape[0] // 2, amps[0].shape[1]
    vmem = pl.BlockSpec(memory_space=pltpu.VMEM)
    held = 4 * rows * depth + 4 * depth * n_cols + 8 * rows * n_cols
    return pl.pallas_call(
        functools.partial(far_kernel, offsets, depth // width),
        out_shape=jax.ShapeDtypeStruct(total.shape, total.dtype),
        in_specs=[vmem] * (len(amps) + 2),
        out_specs=pl.BlockSpec(memory_space=pltpu.HBM),
        scratch_shapes=[
            pltpu.VMEM((rows, depth), block.dtype),
            pltpu.VMEM((rows, n_cols), total.dtype),
            pltpu.SemaphoreType.DMA((n_cols // (2 * width),)),
        ],
        compiler_params=pltpu.CompilerParams(vmem_limit_bytes=held + 2 * MIB),
        cost_estimate=pl.CostEstimate(
            flops=2 * rows * depth * n_cols,
            bytes_accessed=16 * rows * n_cols,
            transcendentals=0,
        ),
        name="far_half",
    )(*amps, total, block)


def exchange(x, axis, flip):
    size = lax.axis_size(axis)
    return lax.ppermute(x, axis, [(i, i ^ flip) for i in range(size)])


def tie(late, *early):
    return lax.optimization_barrier((late, *early))


def body(amplitudes, packed_tiles, tile_ids, residual_in):
    n_col, n_row = lax.axis_size("col"), lax.axis_size("row")
    col, row = lax.axis_index("col"), lax.axis_index("row")
    inner = 2 ** (int(math.log2(n_col)) // 2)
    capacity = -(-packed_tiles.shape[1] // n_col)
    half = n_col // 2
    outgoing = list(pack(col, packed_tiles, tile_ids, n_col, capacity))

    amps = {0: amplitudes}
    for s in [*range(1, inner), *range(inner, half, inner), half]:
        amps[s] = exchange(amplitudes, "col", s)
    order = sorted(amps)[1:]
    outgoing[half:], got = tie(outgoing[half:], [amps[s] for s in order])
    amps.update(zip(order, got))

    chunks = [outgoing[0][None]]
    chunks += [exchange(outgoing[s][None], "col", s) for s in range(1, n_col)]
    for flip in range(inner, half, inner):
        for lane in range(1, inner):
            amps[flip ^ lane] = exchange(amps[flip], "col", lane)
        amps[flip ^ half] = exchange(amps[flip], "col", half)
    for lane in range(1, inner):
        amps[half ^ lane] = exchange(amps[half], "col", lane)

    early = [s for s in amps if 0 < s < half]
    late = [s for s in amps if half < s < half + inner]
    flips = range(CORES, n_row, CORES)
    cut = half + half // 2
    far_groups = [join(chunks[half:cut], WEIGHT), join(chunks[cut:], WEIGHT)]
    near_group = join(chunks[:half])
    far_passed = [[exchange(g, "row", flip) for flip in flips] for g in far_groups]
    near_passed = [exchange(near_group, "row", flip) for flip in flips]
    near_passed, got = tie(near_passed, [amps[s] for s in late])
    amps.update(zip(late, got))
    far_passed, got = tie(far_passed, [amps[s] for s in early])
    amps.update(zip(early, got))
    pieces, rows = [], []
    for held, passed in (
        (join(far_groups), [join(x) for x in zip(*far_passed)]),
        (near_group, near_passed),
    ):
        own, passed = tie(held, passed)
        for flip, mine in zip(range(0, n_row, CORES), [own, *passed]):
            pieces += [mine, exchange(mine, "row", 1)]
            rows += [row ^ flip, row ^ flip ^ 1]
    for flip in range(half + inner, n_col, inner):
        there = join([amps[flip]], WEIGHT_FAR)
        for lane in range(1, inner):
            amps[flip ^ lane] = exchange(there, "col", lane)

    where = jnp.stack(rows + [col]).astype(jnp.int32)
    near = [s for s in sorted(amps) if 0 < s < half]
    far = [s for s in sorted(amps) if s >= half]
    total, far_block = near_half(
        where, pieces, [amps[s] for s in near], near, amplitudes, residual_in, capacity
    )
    return far_half([amps[s] for s in far], far, total, far_block)


def solution(mesh):
    in_specs = (P("row", "col"), P("row", "col", None, None), P("row", "col"), P("row", "col"))
    out_specs = P("row", "col")
    return jax.shard_map(body, mesh=mesh, in_specs=in_specs, out_specs=out_specs, check_vma=False)
```

```python
import functools
import math

import jax
import jax.numpy as jnp
from jax import lax
from jax.experimental import pallas as pl
from jax.experimental.pallas import tpu as pltpu
from jax.sharding import PartitionSpec as P

KT_DEV = 2
QT_DEV = 8
CORES = 2
META = 16
MIB = 1024 * 1024
WEIGHT = 10**9
WEIGHT_FAR = 4 * 10**9


def pack_kernel(columns, capacity, me_ref, ids_hbm, tiles_hbm, *refs):
    outs = refs[:columns]
    ids_ref, tiles_ref, slot_tile, slot_place, count, ids_sem, tiles_sem = refs[columns:]
    ids_copy = pltpu.make_async_copy(ids_hbm, ids_ref, ids_sem)
    tiles_copy = pltpu.make_async_copy(tiles_hbm, tiles_ref, tiles_sem)
    ids_copy.start()
    for t in range(tiles_ref.shape[1]):
        pltpu.make_async_copy(tiles_hbm.at[0, t], tiles_ref.at[0, t], tiles_sem).start()
    per_device, width = tiles_ref.shape[1], tiles_ref.shape[2]
    shift = per_device.bit_length() - 1
    for d in range(columns):
        count[d] = 0
        for s in range(capacity):
            slot_place[d * capacity + s] = per_device
    ids_copy.wait()
    for t in range(per_device):
        tile_id = ids_ref[0, t]
        target = lax.shift_right_logical(tile_id, shift)
        rank = count[target]
        count[target] = rank + 1
        slot_tile[target * capacity + rank] = t
        slot_place[target * capacity + rank] = tile_id & (per_device - 1)
    tiles_copy.wait()
    lane = lax.broadcasted_iota(jnp.int32, (META, width), 1)
    for d, out in enumerate(outs):
        target = me_ref[0] ^ d
        row = jnp.full((META, width), per_device, jnp.int32)
        for s in range(capacity):
            place = slot_place[target * capacity + s]
            row = jnp.where(lane == s, place, row)

            @pl.when(place < per_device)
            def _():
                out[s * width : (s + 1) * width, :] = tiles_ref[
                    0, slot_tile[target * capacity + s]
                ]

        out[capacity * width :, :] = row.astype(jnp.float32).astype(jnp.bfloat16)


def pack(col, packed_tiles, tile_ids, columns, capacity):
    _, per_device, width, _ = packed_tiles.shape
    chunk = jax.ShapeDtypeStruct((capacity * width + META, width), packed_tiles.dtype)
    smem = pl.BlockSpec(memory_space=pltpu.SMEM)
    vmem = pl.BlockSpec(memory_space=pltpu.VMEM)
    hbm = pl.BlockSpec(memory_space=pltpu.HBM)
    return pl.pallas_call(
        functools.partial(pack_kernel, columns, capacity),
        out_shape=[chunk] * columns,
        in_specs=[smem, hbm, hbm],
        out_specs=[vmem] * columns,
        scratch_shapes=[
            pltpu.SMEM(tile_ids.shape, jnp.int32),
            pltpu.VMEM(packed_tiles.shape, packed_tiles.dtype),
            pltpu.SMEM((columns * capacity,), jnp.int32),
            pltpu.SMEM((columns * capacity,), jnp.int32),
            pltpu.SMEM((columns,), jnp.int32),
            pltpu.SemaphoreType.DMA,
            pltpu.SemaphoreType.DMA,
        ],
        compiler_params=pltpu.CompilerParams(vmem_limit_bytes=8 * MIB),
        name="pack",
    )(
        col[None],
        pltpu.with_memory_space_constraint(tile_ids, pltpu.HBM),
        pltpu.with_memory_space_constraint(packed_tiles, pltpu.HBM),
    )


def join_kernel(*refs):
    at = 0
    for part in refs[:-1]:
        refs[-1][at : at + part.shape[0]] = part[...]
        at += part.shape[0]


def join(chunks, flops=0):
    vmem = pl.BlockSpec(memory_space=pltpu.VMEM)
    total = sum(c.shape[0] for c in chunks)
    return pl.pallas_call(
        join_kernel,
        out_shape=jax.ShapeDtypeStruct((total, *chunks[0].shape[1:]), chunks[0].dtype),
        in_specs=[vmem] * len(chunks),
        out_specs=vmem,
        compiler_params=pltpu.CompilerParams(vmem_limit_bytes=8 * MIB),
        cost_estimate=pl.CostEstimate(flops=flops, bytes_accessed=0, transcendentals=0),
        name="join",
    )(*chunks)


def multiply(amp, block, first, start, out, sems, step):
    copies = []
    for n in range(block.shape[1] // step):
        cols = slice(n * step, (n + 1) * step)
        held = out[0] if sems is not None else out
        held[:, cols] = start[:, cols] + jnp.dot(
            amp[...],
            block[first : first + amp.shape[1], cols],
            preferred_element_type=jnp.float32,
        )
        if sems is not None:
            part = pl.ds(n * step, step)
            copies.append(
                pltpu.make_async_copy(held.at[:, part], out[1].at[:, part], sems.at[n])
            )
            copies[-1].start()
    for copy in copies:
        copy.wait()


def near_kernel(n_pieces, offsets, capacity, n_columns, where_ref, *refs):
    n_amps = len(offsets)
    pieces = refs[:n_pieces]
    amps = refs[n_pieces : n_pieces + n_amps]
    own, residual, total, block = refs[n_pieces + n_amps : n_pieces + n_amps + 4]
    places, table, amp, res, table_sem, own_sem, res_sem = refs[n_pieces + n_amps + 4 :]
    width = pieces[0].shape[2]
    per_device = KT_DEV * QT_DEV
    own_copy = pltpu.make_async_copy(own, amp.at[:, pl.ds(0, width)], own_sem)
    own_copy.start()
    res_copy = pltpu.make_async_copy(residual, res, res_sem)
    share = residual.shape[0] // 8
    for i in range(8):
        part = pl.ds(i * share, share)
        pltpu.make_async_copy(residual.at[part, :], res.at[part, :], res_sem).start()
    at = 0
    for piece in pieces:
        rows = piece[:, capacity * width :, :]
        places[at : at + piece.shape[0]] = jnp.max(rows.astype(jnp.float32), axis=1).astype(
            jnp.int32
        )
        at += piece.shape[0]
    table_copy = pltpu.make_async_copy(places, table, table_sem)
    table_copy.start()
    for source, slot in zip(amps, offsets):
        amp[:, slot * width : (slot + 1) * width] = source[...]
    table_copy.wait()
    col = where_ref[n_pieces]
    full = capacity * n_columns == per_device
    at = 0
    for p, piece in enumerate(pieces):
        row = where_ref[p]
        for c in range(piece.shape[0]):
            for s in range(capacity):
                position = table[at, s]

                def put(position=position, piece=piece, c=c, s=s, row=row):
                    k = row * KT_DEV + lax.shift_right_logical(
                        position, QT_DEV.bit_length() - 1
                    )
                    q = position & (QT_DEV - 1)
                    block[
                        pl.ds(pl.multiple_of((k ^ col) * width, width), width),
                        pl.ds(pl.multiple_of(q * width, width), width),
                    ] = piece[c, s * width : (s + 1) * width, :]

                if full:
                    put()
                else:
                    pl.when(position < per_device)(put)
            at += 1
    own_copy.wait()
    res_copy.wait()
    multiply(amp, block, 0, res, total, None, 2 * width)


def near_half(where, pieces, amps, offsets, own, residual, capacity):
    width = pieces[0].shape[2]
    n_pieces, n_amps = len(pieces), len(amps)
    chunks = sum(p.shape[0] for p in pieces)
    rows, n_cols = residual.shape
    depth = (1 + n_amps) * width
    hbm = pl.BlockSpec(memory_space=pltpu.HBM)
    vmem = pl.BlockSpec(memory_space=pltpu.VMEM)
    held = 2 * rows * depth + 4 * depth * n_cols + 8 * rows * n_cols
    held += sum(x.size * x.dtype.itemsize for x in pieces) // 2
    return pl.pallas_call(
        functools.partial(near_kernel, n_pieces, offsets, capacity, 1 + 2 * n_amps + 1),
        out_shape=[
            jax.ShapeDtypeStruct(residual.shape, residual.dtype),
            jax.ShapeDtypeStruct((2 * depth, n_cols), pieces[0].dtype),
        ],
        in_specs=[pl.BlockSpec(memory_space=pltpu.SMEM)]
        + [vmem] * (n_pieces + n_amps)
        + [hbm, hbm],
        out_specs=[vmem, vmem],
        scratch_shapes=[
            pltpu.VMEM((chunks, width), jnp.int32),
            pltpu.SMEM((chunks, width), jnp.int32),
            pltpu.VMEM((rows, depth), pieces[0].dtype),
            pltpu.VMEM((rows, n_cols), residual.dtype),
            pltpu.SemaphoreType.DMA,
            pltpu.SemaphoreType.DMA,
            pltpu.SemaphoreType.DMA,
        ],
        compiler_params=pltpu.CompilerParams(vmem_limit_bytes=held + 2 * MIB),
        cost_estimate=pl.CostEstimate(
            flops=2 * rows * depth * n_cols,
            bytes_accessed=16 * rows * n_cols,
            transcendentals=0,
        ),
        name="near_half",
    )(
        where,
        *pieces,
        *amps,
        pltpu.with_memory_space_constraint(own, pltpu.HBM),
        pltpu.with_memory_space_constraint(residual, pltpu.HBM),
    )


def far_kernel(offsets, half, *refs):
    amps = refs[: len(offsets)]
    start, block, out, amp, total, sems = refs[len(offsets) :]
    width = amps[0].shape[1]
    for source, slot in zip(amps, offsets):
        at = (slot - half) * width
        amp[:, at : at + width] = source[...]
    multiply(amp, block, block.shape[0] - amp.shape[1], start, (total, out), sems, 2 * width)


def far_half(amps, offsets, total, block):
    rows, n_cols = total.shape
    depth, width = block.shape[0] // 2, amps[0].shape[1]
    vmem = pl.BlockSpec(memory_space=pltpu.VMEM)
    held = 4 * rows * depth + 4 * depth * n_cols + 8 * rows * n_cols
    return pl.pallas_call(
        functools.partial(far_kernel, offsets, depth // width),
        out_shape=jax.ShapeDtypeStruct(total.shape, total.dtype),
        in_specs=[vmem] * (len(amps) + 2),
        out_specs=pl.BlockSpec(memory_space=pltpu.HBM),
        scratch_shapes=[
            pltpu.VMEM((rows, depth), block.dtype),
            pltpu.VMEM((rows, n_cols), total.dtype),
            pltpu.SemaphoreType.DMA((n_cols // (2 * width),)),
        ],
        compiler_params=pltpu.CompilerParams(vmem_limit_bytes=held + 2 * MIB),
        cost_estimate=pl.CostEstimate(
            flops=2 * rows * depth * n_cols,
            bytes_accessed=16 * rows * n_cols,
            transcendentals=0,
        ),
        name="far_half",
    )(*amps, total, block)


def exchange(x, axis, flip):
    size = lax.axis_size(axis)
    return lax.ppermute(x, axis, [(i, i ^ flip) for i in range(size)])


def tie(late, *early):
    return lax.optimization_barrier((late, *early))


def body(amplitudes, packed_tiles, tile_ids, residual_in):
    n_col, n_row = lax.axis_size("col"), lax.axis_size("row")
    col, row = lax.axis_index("col"), lax.axis_index("row")
    inner = 2 ** (int(math.log2(n_col)) // 2)
    capacity = -(-packed_tiles.shape[1] // n_col)
    half = n_col // 2
    outgoing = list(pack(col, packed_tiles, tile_ids, n_col, capacity))

    amps = {0: amplitudes}
    for s in [*range(1, inner), *range(inner, half, inner), half]:
        amps[s] = exchange(amplitudes, "col", s)
    outgoing[half:], amps = tie(outgoing[half:], amps)

    chunks = [outgoing[0][None]]
    chunks += [exchange(outgoing[s][None], "col", s) for s in range(1, n_col)]
    for flip in range(inner, half, inner):
        for lane in range(1, inner):
            amps[flip ^ lane] = exchange(amps[flip], "col", lane)
        amps[flip ^ half] = exchange(amps[flip], "col", half)
    for lane in range(1, inner):
        amps[half ^ lane] = exchange(amps[half], "col", lane)

    early = [s for s in amps if s and (s < half or half < s < half + inner)]
    flips = range(CORES, n_row, CORES)
    cut = half + half // 2
    far_groups = [join(chunks[half:cut], WEIGHT), join(chunks[cut:], WEIGHT)]
    near_group = join(chunks[:half])
    far_passed = [[exchange(g, "row", flip) for flip in flips] for g in far_groups]
    near_passed = [exchange(near_group, "row", flip) for flip in flips]
    far_passed, got = tie(far_passed, [amps[s] for s in early])
    amps.update(zip(early, got))
    pieces, rows = [], []
    for held, passed in (
        (join(far_groups), [join(x) for x in zip(*far_passed)]),
        (near_group, near_passed),
    ):
        own, passed = tie(held, passed)
        for flip, mine in zip(range(0, n_row, CORES), [own, *passed]):
            pieces += [mine, exchange(mine, "row", 1)]
            rows += [row ^ flip, row ^ flip ^ 1]
    for flip in range(half + inner, n_col, inner):
        there = join([amps[flip]], WEIGHT_FAR)
        for lane in range(1, inner):
            amps[flip ^ lane] = exchange(there, "col", lane)

    where = jnp.stack(rows + [col]).astype(jnp.int32)
    near = [s for s in sorted(amps) if 0 < s < half]
    far = [s for s in sorted(amps) if s >= half]
    total, far_block = near_half(
        where, pieces, [amps[s] for s in near], near, amplitudes, residual_in, capacity
    )
    return far_half([amps[s] for s in far], far, total, far_block)


def solution(mesh):
    in_specs = (P("row", "col"), P("row", "col", None, None), P("row", "col"), P("row", "col"))
    out_specs = P("row", "col")
    return jax.shard_map(body, mesh=mesh, in_specs=in_specs, out_specs=out_specs, check_vma=False)
```

```python
import functools
import math

import jax
import jax.numpy as jnp
from jax import lax
from jax.experimental import pallas as pl
from jax.experimental.pallas import tpu as pltpu
from jax.sharding import PartitionSpec as P

KT_DEV = 2
QT_DEV = 8
CORES = 2
META = 16
MIB = 1024 * 1024
WEIGHT = 10**9
WEIGHT_FAR = 4 * 10**9


def pack_kernel(columns, capacity, me_ref, ids_hbm, tiles_hbm, *refs):
    outs = refs[:columns]
    ids_ref, tiles_ref, slot_tile, slot_place, count, ids_sem, tiles_sem = refs[columns:]
    ids_copy = pltpu.make_async_copy(ids_hbm, ids_ref, ids_sem)
    tiles_copy = pltpu.make_async_copy(tiles_hbm, tiles_ref, tiles_sem)
    ids_copy.start()
    for t in range(tiles_ref.shape[1]):
        pltpu.make_async_copy(tiles_hbm.at[0, t], tiles_ref.at[0, t], tiles_sem).start()
    per_device, width = tiles_ref.shape[1], tiles_ref.shape[2]
    shift = per_device.bit_length() - 1
    for d in range(columns):
        count[d] = 0
        for s in range(capacity):
            slot_place[d * capacity + s] = per_device
    ids_copy.wait()
    for t in range(per_device):
        tile_id = ids_ref[0, t]
        target = lax.shift_right_logical(tile_id, shift)
        rank = count[target]
        count[target] = rank + 1
        slot_tile[target * capacity + rank] = t
        slot_place[target * capacity + rank] = tile_id & (per_device - 1)
    tiles_copy.wait()
    lane = lax.broadcasted_iota(jnp.int32, (META, width), 1)
    for d, out in enumerate(outs):
        target = me_ref[0] ^ d
        row = jnp.full((META, width), per_device, jnp.int32)
        for s in range(capacity):
            place = slot_place[target * capacity + s]
            row = jnp.where(lane == s, place, row)

            @pl.when(place < per_device)
            def _():
                out[s * width : (s + 1) * width, :] = tiles_ref[
                    0, slot_tile[target * capacity + s]
                ]

        out[capacity * width :, :] = row.astype(jnp.float32).astype(jnp.bfloat16)


def pack(col, packed_tiles, tile_ids, columns, capacity):
    _, per_device, width, _ = packed_tiles.shape
    chunk = jax.ShapeDtypeStruct((capacity * width + META, width), packed_tiles.dtype)
    smem = pl.BlockSpec(memory_space=pltpu.SMEM)
    vmem = pl.BlockSpec(memory_space=pltpu.VMEM)
    hbm = pl.BlockSpec(memory_space=pltpu.HBM)
    return pl.pallas_call(
        functools.partial(pack_kernel, columns, capacity),
        out_shape=[chunk] * columns,
        in_specs=[smem, hbm, hbm],
        out_specs=[vmem] * columns,
        scratch_shapes=[
            pltpu.SMEM(tile_ids.shape, jnp.int32),
            pltpu.VMEM(packed_tiles.shape, packed_tiles.dtype),
            pltpu.SMEM((columns * capacity,), jnp.int32),
            pltpu.SMEM((columns * capacity,), jnp.int32),
            pltpu.SMEM((columns,), jnp.int32),
            pltpu.SemaphoreType.DMA,
            pltpu.SemaphoreType.DMA,
        ],
        compiler_params=pltpu.CompilerParams(vmem_limit_bytes=8 * MIB),
        name="pack",
    )(
        col[None],
        pltpu.with_memory_space_constraint(tile_ids, pltpu.HBM),
        pltpu.with_memory_space_constraint(packed_tiles, pltpu.HBM),
    )


def join_kernel(*refs):
    at = 0
    for part in refs[:-1]:
        refs[-1][at : at + part.shape[0]] = part[...]
        at += part.shape[0]


def join(chunks, flops=0):
    vmem = pl.BlockSpec(memory_space=pltpu.VMEM)
    total = sum(c.shape[0] for c in chunks)
    return pl.pallas_call(
        join_kernel,
        out_shape=jax.ShapeDtypeStruct((total, *chunks[0].shape[1:]), chunks[0].dtype),
        in_specs=[vmem] * len(chunks),
        out_specs=vmem,
        compiler_params=pltpu.CompilerParams(vmem_limit_bytes=8 * MIB),
        cost_estimate=pl.CostEstimate(flops=flops, bytes_accessed=0, transcendentals=0),
        name="join",
    )(*chunks)


def multiply(amp, block, first, start, out, sems, step):
    copies = []
    for n in range(block.shape[1] // step):
        cols = slice(n * step, (n + 1) * step)
        held = out[0] if sems is not None else out
        held[:, cols] = start[:, cols] + jnp.dot(
            amp[...],
            block[first : first + amp.shape[1], cols],
            preferred_element_type=jnp.float32,
        )
        if sems is not None:
            part = pl.ds(n * step, step)
            copies.append(
                pltpu.make_async_copy(held.at[:, part], out[1].at[:, part], sems.at[n])
            )
            copies[-1].start()
    for copy in copies:
        copy.wait()


def near_kernel(n_pieces, offsets, capacity, n_columns, where_ref, *refs):
    n_amps = len(offsets)
    pieces = refs[:n_pieces]
    amps = refs[n_pieces : n_pieces + n_amps]
    own, residual, total, block = refs[n_pieces + n_amps : n_pieces + n_amps + 4]
    places, table, amp, res, table_sem, own_sem, res_sem = refs[n_pieces + n_amps + 4 :]
    width = pieces[0].shape[2]
    per_device = KT_DEV * QT_DEV
    own_copy = pltpu.make_async_copy(own, amp.at[:, pl.ds(0, width)], own_sem)
    own_copy.start()
    res_copy = pltpu.make_async_copy(residual, res, res_sem)
    share = residual.shape[0] // 8
    for i in range(8):
        part = pl.ds(i * share, share)
        pltpu.make_async_copy(residual.at[part, :], res.at[part, :], res_sem).start()
    at = 0
    for piece in pieces:
        rows = piece[:, capacity * width :, :]
        places[at : at + piece.shape[0]] = jnp.max(rows.astype(jnp.float32), axis=1).astype(
            jnp.int32
        )
        at += piece.shape[0]
    table_copy = pltpu.make_async_copy(places, table, table_sem)
    table_copy.start()
    for source, slot in zip(amps, offsets):
        amp[:, slot * width : (slot + 1) * width] = source[...]
    table_copy.wait()
    col = where_ref[n_pieces]
    full = capacity * n_columns == per_device
    at = 0
    for p, piece in enumerate(pieces):
        row = where_ref[p]
        for c in range(piece.shape[0]):
            for s in range(capacity):
                position = table[at, s]

                def put(position=position, piece=piece, c=c, s=s, row=row):
                    k = row * KT_DEV + lax.shift_right_logical(
                        position, QT_DEV.bit_length() - 1
                    )
                    q = position & (QT_DEV - 1)
                    block[
                        pl.ds(pl.multiple_of((k ^ col) * width, width), width),
                        pl.ds(pl.multiple_of(q * width, width), width),
                    ] = piece[c, s * width : (s + 1) * width, :]

                if full:
                    put()
                else:
                    pl.when(position < per_device)(put)
            at += 1
    own_copy.wait()
    res_copy.wait()
    multiply(amp, block, 0, res, total, None, 2 * width)


def near_half(where, pieces, amps, offsets, own, residual, capacity):
    width = pieces[0].shape[2]
    n_pieces, n_amps = len(pieces), len(amps)
    chunks = sum(p.shape[0] for p in pieces)
    rows, n_cols = residual.shape
    depth = (1 + n_amps) * width
    hbm = pl.BlockSpec(memory_space=pltpu.HBM)
    vmem = pl.BlockSpec(memory_space=pltpu.VMEM)
    held = 2 * rows * depth + 4 * depth * n_cols + 8 * rows * n_cols
    held += sum(x.size * x.dtype.itemsize for x in pieces) // 2
    return pl.pallas_call(
        functools.partial(near_kernel, n_pieces, offsets, capacity, 1 + 2 * n_amps + 1),
        out_shape=[
            jax.ShapeDtypeStruct(residual.shape, residual.dtype),
            jax.ShapeDtypeStruct((2 * depth, n_cols), pieces[0].dtype),
        ],
        in_specs=[pl.BlockSpec(memory_space=pltpu.SMEM)]
        + [vmem] * (n_pieces + n_amps)
        + [hbm, hbm],
        out_specs=[vmem, vmem],
        scratch_shapes=[
            pltpu.VMEM((chunks, width), jnp.int32),
            pltpu.SMEM((chunks, width), jnp.int32),
            pltpu.VMEM((rows, depth), pieces[0].dtype),
            pltpu.VMEM((rows, n_cols), residual.dtype),
            pltpu.SemaphoreType.DMA,
            pltpu.SemaphoreType.DMA,
            pltpu.SemaphoreType.DMA,
        ],
        compiler_params=pltpu.CompilerParams(vmem_limit_bytes=held + 2 * MIB),
        cost_estimate=pl.CostEstimate(
            flops=2 * rows * depth * n_cols,
            bytes_accessed=16 * rows * n_cols,
            transcendentals=0,
        ),
        name="near_half",
    )(
        where,
        *pieces,
        *amps,
        pltpu.with_memory_space_constraint(own, pltpu.HBM),
        pltpu.with_memory_space_constraint(residual, pltpu.HBM),
    )


def far_kernel(offsets, half, *refs):
    amps = refs[: len(offsets)]
    start, block, out, amp, total, sems = refs[len(offsets) :]
    width = amps[0].shape[1]
    for source, slot in zip(amps, offsets):
        at = (slot - half) * width
        amp[:, at : at + width] = source[...]
    multiply(amp, block, block.shape[0] - amp.shape[1], start, (total, out), sems, 2 * width)


def far_half(amps, offsets, total, block):
    rows, n_cols = total.shape
    depth, width = block.shape[0] // 2, amps[0].shape[1]
    vmem = pl.BlockSpec(memory_space=pltpu.VMEM)
    held = 4 * rows * depth + 4 * depth * n_cols + 8 * rows * n_cols
    return pl.pallas_call(
        functools.partial(far_kernel, offsets, depth // width),
        out_shape=jax.ShapeDtypeStruct(total.shape, total.dtype),
        in_specs=[vmem] * (len(amps) + 2),
        out_specs=pl.BlockSpec(memory_space=pltpu.HBM),
        scratch_shapes=[
            pltpu.VMEM((rows, depth), block.dtype),
            pltpu.VMEM((rows, n_cols), total.dtype),
            pltpu.SemaphoreType.DMA((n_cols // (2 * width),)),
        ],
        compiler_params=pltpu.CompilerParams(vmem_limit_bytes=held + 2 * MIB),
        cost_estimate=pl.CostEstimate(
            flops=2 * rows * depth * n_cols,
            bytes_accessed=16 * rows * n_cols,
            transcendentals=0,
        ),
        name="far_half",
    )(*amps, total, block)


def exchange(x, axis, flip):
    size = lax.axis_size(axis)
    return lax.ppermute(x, axis, [(i, i ^ flip) for i in range(size)])


def tie(late, *early):
    return lax.optimization_barrier((late, *early))


def body(amplitudes, packed_tiles, tile_ids, residual_in):
    n_col, n_row = lax.axis_size("col"), lax.axis_size("row")
    col, row = lax.axis_index("col"), lax.axis_index("row")
    inner = 2 ** (int(math.log2(n_col)) // 2)
    capacity = -(-packed_tiles.shape[1] // n_col)
    half = n_col // 2
    outgoing = list(pack(col, packed_tiles, tile_ids, n_col, capacity))

    amps = {0: amplitudes}
    for s in [*range(1, inner), *range(inner, half, inner), half]:
        amps[s] = exchange(amplitudes, "col", s)
    first = [*range(inner, half, inner), half]
    outgoing[half:], got = tie(outgoing[half:], [amps[s] for s in first])
    amps.update(zip(first, got))

    chunks = [outgoing[0][None]]
    chunks += [exchange(outgoing[s][None], "col", s) for s in range(1, n_col)]
    for flip in range(inner, half, inner):
        for lane in range(1, inner):
            amps[flip ^ lane] = exchange(amps[flip], "col", lane)
        amps[flip ^ half] = exchange(amps[flip], "col", half)
    for lane in range(1, inner):
        amps[half ^ lane] = exchange(amps[half], "col", lane)

    early = [s for s in amps if s and (s < half or half < s < half + inner)]
    flips = range(CORES, n_row, CORES)
    cut = half + half // 2
    far_groups = [join(chunks[half:cut], WEIGHT), join(chunks[cut:], WEIGHT)]
    near_group = join(chunks[:half])
    far_passed = [[exchange(g, "row", flip) for flip in flips] for g in far_groups]
    near_passed = [exchange(near_group, "row", flip) for flip in flips]
    far_passed, got = tie(far_passed, [amps[s] for s in early])
    amps.update(zip(early, got))
    pieces, rows = [], []
    for held, passed in (
        (join(far_groups), [join(x) for x in zip(*far_passed)]),
        (near_group, near_passed),
    ):
        own, passed = tie(held, passed)
        for flip, mine in zip(range(0, n_row, CORES), [own, *passed]):
            pieces += [mine, exchange(mine, "row", 1)]
            rows += [row ^ flip, row ^ flip ^ 1]
    for flip in range(half + inner, n_col, inner):
        there = join([amps[flip]], WEIGHT_FAR)
        for lane in range(1, inner):
            amps[flip ^ lane] = exchange(there, "col", lane)

    where = jnp.stack(rows + [col]).astype(jnp.int32)
    near = [s for s in sorted(amps) if 0 < s < half]
    far = [s for s in sorted(amps) if s >= half]
    total, far_block = near_half(
        where, pieces, [amps[s] for s in near], near, amplitudes, residual_in, capacity
    )
    return far_half([amps[s] for s in far], far, total, far_block)


def solution(mesh):
    in_specs = (P("row", "col"), P("row", "col", None, None), P("row", "col"), P("row", "col"))
    out_specs = P("row", "col")
    return jax.shard_map(body, mesh=mesh, in_specs=in_specs, out_specs=out_specs, check_vma=False)
```

```python
import functools
import math

import jax
import jax.numpy as jnp
from jax import lax
from jax.experimental import pallas as pl
from jax.experimental.pallas import tpu as pltpu
from jax.sharding import PartitionSpec as P

KT_DEV = 2
QT_DEV = 8
CORES = 2
META = 16
MIB = 1024 * 1024
WEIGHT = 10**9
WEIGHT_FAR = 4 * 10**9


def pack_kernel(columns, capacity, me_ref, ids_hbm, tiles_hbm, *refs):
    outs = refs[:columns]
    ids_ref, tiles_ref, slot_tile, slot_place, count, ids_sem, tiles_sem = refs[columns:]
    ids_copy = pltpu.make_async_copy(ids_hbm, ids_ref, ids_sem)
    tiles_copy = pltpu.make_async_copy(tiles_hbm, tiles_ref, tiles_sem)
    ids_copy.start()
    for t in range(tiles_ref.shape[1]):
        pltpu.make_async_copy(tiles_hbm.at[0, t], tiles_ref.at[0, t], tiles_sem).start()
    per_device, width = tiles_ref.shape[1], tiles_ref.shape[2]
    shift = per_device.bit_length() - 1
    for d in range(columns):
        count[d] = 0
        for s in range(capacity):
            slot_place[d * capacity + s] = per_device
    ids_copy.wait()
    for t in range(per_device):
        tile_id = ids_ref[0, t]
        target = lax.shift_right_logical(tile_id, shift)
        rank = count[target]
        count[target] = rank + 1
        slot_tile[target * capacity + rank] = t
        slot_place[target * capacity + rank] = tile_id & (per_device - 1)
    tiles_copy.wait()
    lane = lax.broadcasted_iota(jnp.int32, (META, width), 1)
    for d, out in enumerate(outs):
        target = me_ref[0] ^ d
        row = jnp.full((META, width), per_device, jnp.int32)
        for s in range(capacity):
            place = slot_place[target * capacity + s]
            row = jnp.where(lane == s, place, row)

            @pl.when(place < per_device)
            def _():
                out[s * width : (s + 1) * width, :] = tiles_ref[
                    0, slot_tile[target * capacity + s]
                ]

        out[capacity * width :, :] = row.astype(jnp.float32).astype(jnp.bfloat16)


def pack(col, packed_tiles, tile_ids, columns, capacity):
    _, per_device, width, _ = packed_tiles.shape
    chunk = jax.ShapeDtypeStruct((capacity * width + META, width), packed_tiles.dtype)
    smem = pl.BlockSpec(memory_space=pltpu.SMEM)
    vmem = pl.BlockSpec(memory_space=pltpu.VMEM)
    hbm = pl.BlockSpec(memory_space=pltpu.HBM)
    return pl.pallas_call(
        functools.partial(pack_kernel, columns, capacity),
        out_shape=[chunk] * columns,
        in_specs=[smem, hbm, hbm],
        out_specs=[vmem] * columns,
        scratch_shapes=[
            pltpu.SMEM(tile_ids.shape, jnp.int32),
            pltpu.VMEM(packed_tiles.shape, packed_tiles.dtype),
            pltpu.SMEM((columns * capacity,), jnp.int32),
            pltpu.SMEM((columns * capacity,), jnp.int32),
            pltpu.SMEM((columns,), jnp.int32),
            pltpu.SemaphoreType.DMA,
            pltpu.SemaphoreType.DMA,
        ],
        compiler_params=pltpu.CompilerParams(vmem_limit_bytes=8 * MIB),
        name="pack",
    )(
        col[None],
        pltpu.with_memory_space_constraint(tile_ids, pltpu.HBM),
        pltpu.with_memory_space_constraint(packed_tiles, pltpu.HBM),
    )


def join_kernel(*refs):
    at = 0
    for part in refs[:-1]:
        refs[-1][at : at + part.shape[0]] = part[...]
        at += part.shape[0]


def join(chunks, flops=0):
    vmem = pl.BlockSpec(memory_space=pltpu.VMEM)
    total = sum(c.shape[0] for c in chunks)
    return pl.pallas_call(
        join_kernel,
        out_shape=jax.ShapeDtypeStruct((total, *chunks[0].shape[1:]), chunks[0].dtype),
        in_specs=[vmem] * len(chunks),
        out_specs=vmem,
        compiler_params=pltpu.CompilerParams(vmem_limit_bytes=8 * MIB),
        cost_estimate=pl.CostEstimate(flops=flops, bytes_accessed=0, transcendentals=0),
        name="join",
    )(*chunks)


def multiply(amp, block, first, start, out, sems, step):
    copies = []
    for n in range(block.shape[1] // step):
        cols = slice(n * step, (n + 1) * step)
        held = out[0] if sems is not None else out
        held[:, cols] = start[:, cols] + jnp.dot(
            amp[...],
            block[first : first + amp.shape[1], cols],
            preferred_element_type=jnp.float32,
        )
        if sems is not None:
            part = pl.ds(n * step, step)
            copies.append(
                pltpu.make_async_copy(held.at[:, part], out[1].at[:, part], sems.at[n])
            )
            share = held.shape[0] // 4
            for i in range(4):
                rows = pl.ds(i * share, share)
                pltpu.make_async_copy(
                    held.at[rows, part], out[1].at[rows, part], sems.at[n]
                ).start()
    for copy in copies:
        copy.wait()


def near_kernel(n_pieces, offsets, capacity, n_columns, where_ref, *refs):
    n_amps = len(offsets)
    pieces = refs[:n_pieces]
    amps = refs[n_pieces : n_pieces + n_amps]
    own, residual, total, block = refs[n_pieces + n_amps : n_pieces + n_amps + 4]
    places, table, amp, res, table_sem, own_sem, res_sem = refs[n_pieces + n_amps + 4 :]
    width = pieces[0].shape[2]
    per_device = KT_DEV * QT_DEV
    own_copy = pltpu.make_async_copy(own, amp.at[:, pl.ds(0, width)], own_sem)
    own_copy.start()
    res_copy = pltpu.make_async_copy(residual, res, res_sem)
    share = residual.shape[0] // 8
    for i in range(8):
        part = pl.ds(i * share, share)
        pltpu.make_async_copy(residual.at[part, :], res.at[part, :], res_sem).start()
    at = 0
    for piece in pieces:
        rows = piece[:, capacity * width :, :]
        places[at : at + piece.shape[0]] = jnp.max(rows.astype(jnp.float32), axis=1).astype(
            jnp.int32
        )
        at += piece.shape[0]
    table_copy = pltpu.make_async_copy(places, table, table_sem)
    table_copy.start()
    for source, slot in zip(amps, offsets):
        amp[:, slot * width : (slot + 1) * width] = source[...]
    table_copy.wait()
    col = where_ref[n_pieces]
    full = capacity * n_columns == per_device
    at = 0
    for p, piece in enumerate(pieces):
        row = where_ref[p]
        for c in range(piece.shape[0]):
            for s in range(capacity):
                position = table[at, s]

                def put(position=position, piece=piece, c=c, s=s, row=row):
                    k = row * KT_DEV + lax.shift_right_logical(
                        position, QT_DEV.bit_length() - 1
                    )
                    q = position & (QT_DEV - 1)
                    block[
                        pl.ds(pl.multiple_of((k ^ col) * width, width), width),
                        pl.ds(pl.multiple_of(q * width, width), width),
                    ] = piece[c, s * width : (s + 1) * width, :]

                if full:
                    put()
                else:
                    pl.when(position < per_device)(put)
            at += 1
    own_copy.wait()
    res_copy.wait()
    multiply(amp, block, 0, res, total, None, 2 * width)


def near_half(where, pieces, amps, offsets, own, residual, capacity):
    width = pieces[0].shape[2]
    n_pieces, n_amps = len(pieces), len(amps)
    chunks = sum(p.shape[0] for p in pieces)
    rows, n_cols = residual.shape
    depth = (1 + n_amps) * width
    hbm = pl.BlockSpec(memory_space=pltpu.HBM)
    vmem = pl.BlockSpec(memory_space=pltpu.VMEM)
    held = 2 * rows * depth + 4 * depth * n_cols + 8 * rows * n_cols
    held += sum(x.size * x.dtype.itemsize for x in pieces) // 2
    return pl.pallas_call(
        functools.partial(near_kernel, n_pieces, offsets, capacity, 1 + 2 * n_amps + 1),
        out_shape=[
            jax.ShapeDtypeStruct(residual.shape, residual.dtype),
            jax.ShapeDtypeStruct((2 * depth, n_cols), pieces[0].dtype),
        ],
        in_specs=[pl.BlockSpec(memory_space=pltpu.SMEM)]
        + [vmem] * (n_pieces + n_amps)
        + [hbm, hbm],
        out_specs=[vmem, vmem],
        scratch_shapes=[
            pltpu.VMEM((chunks, width), jnp.int32),
            pltpu.SMEM((chunks, width), jnp.int32),
            pltpu.VMEM((rows, depth), pieces[0].dtype),
            pltpu.VMEM((rows, n_cols), residual.dtype),
            pltpu.SemaphoreType.DMA,
            pltpu.SemaphoreType.DMA,
            pltpu.SemaphoreType.DMA,
        ],
        compiler_params=pltpu.CompilerParams(vmem_limit_bytes=held + 2 * MIB),
        cost_estimate=pl.CostEstimate(
            flops=2 * rows * depth * n_cols,
            bytes_accessed=16 * rows * n_cols,
            transcendentals=0,
        ),
        name="near_half",
    )(
        where,
        *pieces,
        *amps,
        pltpu.with_memory_space_constraint(own, pltpu.HBM),
        pltpu.with_memory_space_constraint(residual, pltpu.HBM),
    )


def far_kernel(offsets, half, *refs):
    amps = refs[: len(offsets)]
    start, block, out, amp, total, sems = refs[len(offsets) :]
    width = amps[0].shape[1]
    for source, slot in zip(amps, offsets):
        at = (slot - half) * width
        amp[:, at : at + width] = source[...]
    multiply(amp, block, block.shape[0] - amp.shape[1], start, (total, out), sems, 2 * width)


def far_half(amps, offsets, total, block):
    rows, n_cols = total.shape
    depth, width = block.shape[0] // 2, amps[0].shape[1]
    vmem = pl.BlockSpec(memory_space=pltpu.VMEM)
    held = 4 * rows * depth + 4 * depth * n_cols + 8 * rows * n_cols
    return pl.pallas_call(
        functools.partial(far_kernel, offsets, depth // width),
        out_shape=jax.ShapeDtypeStruct(total.shape, total.dtype),
        in_specs=[vmem] * (len(amps) + 2),
        out_specs=pl.BlockSpec(memory_space=pltpu.HBM),
        scratch_shapes=[
            pltpu.VMEM((rows, depth), block.dtype),
            pltpu.VMEM((rows, n_cols), total.dtype),
            pltpu.SemaphoreType.DMA((n_cols // (2 * width),)),
        ],
        compiler_params=pltpu.CompilerParams(vmem_limit_bytes=held + 2 * MIB),
        cost_estimate=pl.CostEstimate(
            flops=2 * rows * depth * n_cols,
            bytes_accessed=16 * rows * n_cols,
            transcendentals=0,
        ),
        name="far_half",
    )(*amps, total, block)


def exchange(x, axis, flip):
    size = lax.axis_size(axis)
    return lax.ppermute(x, axis, [(i, i ^ flip) for i in range(size)])


def tie(late, *early):
    return lax.optimization_barrier((late, *early))


def body(amplitudes, packed_tiles, tile_ids, residual_in):
    n_col, n_row = lax.axis_size("col"), lax.axis_size("row")
    col, row = lax.axis_index("col"), lax.axis_index("row")
    inner = 2 ** (int(math.log2(n_col)) // 2)
    capacity = -(-packed_tiles.shape[1] // n_col)
    half = n_col // 2
    outgoing = list(pack(col, packed_tiles, tile_ids, n_col, capacity))

    amps = {0: amplitudes}
    for s in [*range(1, inner), *range(inner, half, inner), half]:
        amps[s] = exchange(amplitudes, "col", s)
    outgoing[half:], amps = tie(outgoing[half:], amps)

    chunks = [outgoing[0][None]]
    chunks += [exchange(outgoing[s][None], "col", s) for s in range(1, n_col)]
    for flip in range(inner, half, inner):
        for lane in range(1, inner):
            amps[flip ^ lane] = exchange(amps[flip], "col", lane)
        amps[flip ^ half] = exchange(amps[flip], "col", half)
    for lane in range(1, inner):
        amps[half ^ lane] = exchange(amps[half], "col", lane)

    early = [s for s in amps if s and (s < half or half < s < half + inner)]
    flips = range(CORES, n_row, CORES)
    cut = half + half // 2
    far_groups = [join(chunks[half:cut], WEIGHT), join(chunks[cut:], WEIGHT)]
    near_group = join(chunks[:half])
    far_passed = [[exchange(g, "row", flip) for flip in flips] for g in far_groups]
    near_passed = [exchange(near_group, "row", flip) for flip in flips]
    far_passed, got = tie(far_passed, [amps[s] for s in early])
    amps.update(zip(early, got))
    pieces, rows = [], []
    for held, passed in (
        (join(far_groups), [join(x) for x in zip(*far_passed)]),
        (near_group, near_passed),
    ):
        own, passed = tie(held, passed)
        for flip, mine in zip(range(0, n_row, CORES), [own, *passed]):
            pieces += [mine, exchange(mine, "row", 1)]
            rows += [row ^ flip, row ^ flip ^ 1]
    for flip in range(half + inner, n_col, inner):
        there = join([amps[flip]], WEIGHT_FAR)
        for lane in range(1, inner):
            amps[flip ^ lane] = exchange(there, "col", lane)

    where = jnp.stack(rows + [col]).astype(jnp.int32)
    near = [s for s in sorted(amps) if 0 < s < half]
    far = [s for s in sorted(amps) if s >= half]
    total, far_block = near_half(
        where, pieces, [amps[s] for s in near], near, amplitudes, residual_in, capacity
    )
    return far_half([amps[s] for s in far], far, total, far_block)


def solution(mesh):
    in_specs = (P("row", "col"), P("row", "col", None, None), P("row", "col"), P("row", "col"))
    out_specs = P("row", "col")
    return jax.shard_map(body, mesh=mesh, in_specs=in_specs, out_specs=out_specs, check_vma=False)
```

```python
import functools
import math

import jax
import jax.numpy as jnp
from jax import lax
from jax.experimental import pallas as pl
from jax.experimental.pallas import tpu as pltpu
from jax.sharding import PartitionSpec as P

KT_DEV = 2
QT_DEV = 8
CORES = 2
META = 16
MIB = 1024 * 1024
WEIGHT = 10**9
WEIGHT_FAR = 4 * 10**9


def pack_kernel(columns, capacity, me_ref, ids_hbm, tiles_hbm, *refs):
    outs = refs[:columns]
    ids_ref, tiles_ref, slot_tile, slot_place, count, ids_sem, tiles_sem = refs[columns:]
    ids_copy = pltpu.make_async_copy(ids_hbm, ids_ref, ids_sem)
    tiles_copy = pltpu.make_async_copy(tiles_hbm, tiles_ref, tiles_sem)
    ids_copy.start()
    for t in range(tiles_ref.shape[1]):
        pltpu.make_async_copy(tiles_hbm.at[0, t], tiles_ref.at[0, t], tiles_sem).start()
    per_device, width = tiles_ref.shape[1], tiles_ref.shape[2]
    shift = per_device.bit_length() - 1
    for d in range(columns):
        count[d] = 0
        for s in range(capacity):
            slot_place[d * capacity + s] = per_device
    ids_copy.wait()
    for t in range(per_device):
        tile_id = ids_ref[0, t]
        target = lax.shift_right_logical(tile_id, shift)
        rank = count[target]
        count[target] = rank + 1
        slot_tile[target * capacity + rank] = t
        slot_place[target * capacity + rank] = tile_id & (per_device - 1)
    tiles_copy.wait()
    lane = lax.broadcasted_iota(jnp.int32, (META, width), 1)
    for d, out in enumerate(outs):
        target = me_ref[0] ^ d
        row = jnp.full((META, width), per_device, jnp.int32)
        for s in range(capacity):
            place = slot_place[target * capacity + s]
            row = jnp.where(lane == s, place, row)

            @pl.when(place < per_device)
            def _():
                out[s * width : (s + 1) * width, :] = tiles_ref[
                    0, slot_tile[target * capacity + s]
                ]

        out[capacity * width :, :] = row.astype(jnp.float32).astype(jnp.bfloat16)


def pack(col, packed_tiles, tile_ids, columns, capacity):
    _, per_device, width, _ = packed_tiles.shape
    chunk = jax.ShapeDtypeStruct((capacity * width + META, width), packed_tiles.dtype)
    smem = pl.BlockSpec(memory_space=pltpu.SMEM)
    vmem = pl.BlockSpec(memory_space=pltpu.VMEM)
    hbm = pl.BlockSpec(memory_space=pltpu.HBM)
    return pl.pallas_call(
        functools.partial(pack_kernel, columns, capacity),
        out_shape=[chunk] * columns,
        in_specs=[smem, hbm, hbm],
        out_specs=[vmem] * columns,
        scratch_shapes=[
            pltpu.SMEM(tile_ids.shape, jnp.int32),
            pltpu.VMEM(packed_tiles.shape, packed_tiles.dtype),
            pltpu.SMEM((columns * capacity,), jnp.int32),
            pltpu.SMEM((columns * capacity,), jnp.int32),
            pltpu.SMEM((columns,), jnp.int32),
            pltpu.SemaphoreType.DMA,
            pltpu.SemaphoreType.DMA,
        ],
        compiler_params=pltpu.CompilerParams(vmem_limit_bytes=8 * MIB),
        name="pack",
    )(
        col[None],
        pltpu.with_memory_space_constraint(tile_ids, pltpu.HBM),
        pltpu.with_memory_space_constraint(packed_tiles, pltpu.HBM),
    )


def join_kernel(*refs):
    at = 0
    for part in refs[:-1]:
        refs[-1][at : at + part.shape[0]] = part[...]
        at += part.shape[0]


def join(chunks, flops=0):
    vmem = pl.BlockSpec(memory_space=pltpu.VMEM)
    total = sum(c.shape[0] for c in chunks)
    return pl.pallas_call(
        join_kernel,
        out_shape=jax.ShapeDtypeStruct((total, *chunks[0].shape[1:]), chunks[0].dtype),
        in_specs=[vmem] * len(chunks),
        out_specs=vmem,
        compiler_params=pltpu.CompilerParams(vmem_limit_bytes=8 * MIB),
        cost_estimate=pl.CostEstimate(flops=flops, bytes_accessed=0, transcendentals=0),
        name="join",
    )(*chunks)


def multiply(amp, block, first, start, out, sems, step):
    copies = []
    for n in range(block.shape[1] // step):
        cols = slice(n * step, (n + 1) * step)
        held = out[0] if sems is not None else out
        held[:, cols] = start[:, cols] + jnp.dot(
            amp[...],
            block[first : first + amp.shape[1], cols],
            preferred_element_type=jnp.float32,
        )
        if sems is not None:
            part = pl.ds(n * step, step)
            copies.append(
                pltpu.make_async_copy(held.at[:, part], out[1].at[:, part], sems.at[n])
            )
            copies[-1].start()
    for copy in copies:
        copy.wait()


def near_kernel(n_pieces, offsets, capacity, n_columns, where_ref, *refs):
    n_amps = len(offsets)
    pieces = refs[:n_pieces]
    amps = refs[n_pieces : n_pieces + n_amps]
    own, residual, total, block = refs[n_pieces + n_amps : n_pieces + n_amps + 4]
    places, table, amp, res, table_sem, own_sem, res_sem = refs[n_pieces + n_amps + 4 :]
    width = pieces[0].shape[2]
    per_device = KT_DEV * QT_DEV
    own_copy = pltpu.make_async_copy(own, amp.at[:, pl.ds(0, width)], own_sem)
    own_copy.start()
    res_copy = pltpu.make_async_copy(residual, res, res_sem)
    share = residual.shape[0] // 8
    for i in range(8):
        part = pl.ds(i * share, share)
        pltpu.make_async_copy(residual.at[part, :], res.at[part, :], res_sem).start()
    at = 0
    for piece in pieces:
        rows = piece[:, capacity * width :, :]
        places[at : at + piece.shape[0]] = jnp.max(rows.astype(jnp.float32), axis=1).astype(
            jnp.int32
        )
        at += piece.shape[0]
    table_copy = pltpu.make_async_copy(places, table, table_sem)
    table_copy.start()
    for source, slot in zip(amps, offsets):
        amp[:, slot * width : (slot + 1) * width] = source[...]
    table_copy.wait()
    col = where_ref[n_pieces]
    full = capacity * n_columns == per_device
    at = 0
    for p, piece in enumerate(pieces):
        row = where_ref[p]
        for c in range(piece.shape[0]):
            for s in range(capacity):
                position = table[at, s]

                def put(position=position, piece=piece, c=c, s=s, row=row):
                    k = row * KT_DEV + lax.shift_right_logical(
                        position, QT_DEV.bit_length() - 1
                    )
                    q = position & (QT_DEV - 1)
                    block[
                        pl.ds(pl.multiple_of((k ^ col) * width, width), width),
                        pl.ds(pl.multiple_of(q * width, width), width),
                    ] = piece[c, s * width : (s + 1) * width, :]

                if full:
                    put()
                else:
                    pl.when(position < per_device)(put)
            at += 1
    own_copy.wait()
    res_copy.wait()
    multiply(amp, block, 0, res, total, None, 4 * width)


def near_half(where, pieces, amps, offsets, own, residual, capacity):
    width = pieces[0].shape[2]
    n_pieces, n_amps = len(pieces), len(amps)
    chunks = sum(p.shape[0] for p in pieces)
    rows, n_cols = residual.shape
    depth = (1 + n_amps) * width
    hbm = pl.BlockSpec(memory_space=pltpu.HBM)
    vmem = pl.BlockSpec(memory_space=pltpu.VMEM)
    held = 2 * rows * depth + 4 * depth * n_cols + 8 * rows * n_cols
    held += sum(x.size * x.dtype.itemsize for x in pieces) // 2
    return pl.pallas_call(
        functools.partial(near_kernel, n_pieces, offsets, capacity, 1 + 2 * n_amps + 1),
        out_shape=[
            jax.ShapeDtypeStruct(residual.shape, residual.dtype),
            jax.ShapeDtypeStruct((2 * depth, n_cols), pieces[0].dtype),
        ],
        in_specs=[pl.BlockSpec(memory_space=pltpu.SMEM)]
        + [vmem] * (n_pieces + n_amps)
        + [hbm, hbm],
        out_specs=[vmem, vmem],
        scratch_shapes=[
            pltpu.VMEM((chunks, width), jnp.int32),
            pltpu.SMEM((chunks, width), jnp.int32),
            pltpu.VMEM((rows, depth), pieces[0].dtype),
            pltpu.VMEM((rows, n_cols), residual.dtype),
            pltpu.SemaphoreType.DMA,
            pltpu.SemaphoreType.DMA,
            pltpu.SemaphoreType.DMA,
        ],
        compiler_params=pltpu.CompilerParams(vmem_limit_bytes=held + 2 * MIB),
        cost_estimate=pl.CostEstimate(
            flops=2 * rows * depth * n_cols,
            bytes_accessed=16 * rows * n_cols,
            transcendentals=0,
        ),
        name="near_half",
    )(
        where,
        *pieces,
        *amps,
        pltpu.with_memory_space_constraint(own, pltpu.HBM),
        pltpu.with_memory_space_constraint(residual, pltpu.HBM),
    )


def far_kernel(offsets, half, *refs):
    amps = refs[: len(offsets)]
    start, block, out, amp, total, sems = refs[len(offsets) :]
    width = amps[0].shape[1]
    for source, slot in zip(amps, offsets):
        at = (slot - half) * width
        amp[:, at : at + width] = source[...]
    multiply(amp, block, block.shape[0] - amp.shape[1], start, (total, out), sems, 2 * width)


def far_half(amps, offsets, total, block):
    rows, n_cols = total.shape
    depth, width = block.shape[0] // 2, amps[0].shape[1]
    vmem = pl.BlockSpec(memory_space=pltpu.VMEM)
    held = 4 * rows * depth + 4 * depth * n_cols + 8 * rows * n_cols
    return pl.pallas_call(
        functools.partial(far_kernel, offsets, depth // width),
        out_shape=jax.ShapeDtypeStruct(total.shape, total.dtype),
        in_specs=[vmem] * (len(amps) + 2),
        out_specs=pl.BlockSpec(memory_space=pltpu.HBM),
        scratch_shapes=[
            pltpu.VMEM((rows, depth), block.dtype),
            pltpu.VMEM((rows, n_cols), total.dtype),
            pltpu.SemaphoreType.DMA((n_cols // (2 * width),)),
        ],
        compiler_params=pltpu.CompilerParams(vmem_limit_bytes=held + 2 * MIB),
        cost_estimate=pl.CostEstimate(
            flops=2 * rows * depth * n_cols,
            bytes_accessed=16 * rows * n_cols,
            transcendentals=0,
        ),
        name="far_half",
    )(*amps, total, block)


def exchange(x, axis, flip):
    size = lax.axis_size(axis)
    return lax.ppermute(x, axis, [(i, i ^ flip) for i in range(size)])


def tie(late, *early):
    return lax.optimization_barrier((late, *early))


def body(amplitudes, packed_tiles, tile_ids, residual_in):
    n_col, n_row = lax.axis_size("col"), lax.axis_size("row")
    col, row = lax.axis_index("col"), lax.axis_index("row")
    inner = 2 ** (int(math.log2(n_col)) // 2)
    capacity = -(-packed_tiles.shape[1] // n_col)
    half = n_col // 2
    outgoing = list(pack(col, packed_tiles, tile_ids, n_col, capacity))

    amps = {0: amplitudes}
    for s in [*range(1, inner), *range(inner, half, inner), half]:
        amps[s] = exchange(amplitudes, "col", s)
    outgoing[half:], amps = tie(outgoing[half:], amps)

    chunks = [outgoing[0][None]]
    chunks += [exchange(outgoing[s][None], "col", s) for s in range(1, n_col)]
    for flip in range(inner, half, inner):
        for lane in range(1, inner):
            amps[flip ^ lane] = exchange(amps[flip], "col", lane)
        amps[flip ^ half] = exchange(amps[flip], "col", half)
    for lane in range(1, inner):
        amps[half ^ lane] = exchange(amps[half], "col", lane)

    early = [s for s in amps if s and (s < half or half < s < half + inner)]
    flips = range(CORES, n_row, CORES)
    cut = half + half // 2
    far_groups = [join(chunks[half:cut], WEIGHT), join(chunks[cut:], WEIGHT)]
    near_group = join(chunks[:half])
    far_passed = [[exchange(g, "row", flip) for flip in flips] for g in far_groups]
    near_passed = [exchange(near_group, "row", flip) for flip in flips]
    far_passed, got = tie(far_passed, [amps[s] for s in early])
    amps.update(zip(early, got))
    pieces, rows = [], []
    for held, passed in (
        (join(far_groups), [join(x) for x in zip(*far_passed)]),
        (near_group, near_passed),
    ):
        own, passed = tie(held, passed)
        for flip, mine in zip(range(0, n_row, CORES), [own, *passed]):
            pieces += [mine, exchange(mine, "row", 1)]
            rows += [row ^ flip, row ^ flip ^ 1]
    for flip in range(half + inner, n_col, inner):
        there = join([amps[flip]], WEIGHT_FAR)
        for lane in range(1, inner):
            amps[flip ^ lane] = exchange(there, "col", lane)

    where = jnp.stack(rows + [col]).astype(jnp.int32)
    near = [s for s in sorted(amps) if 0 < s < half]
    far = [s for s in sorted(amps) if s >= half]
    total, far_block = near_half(
        where, pieces, [amps[s] for s in near], near, amplitudes, residual_in, capacity
    )
    return far_half([amps[s] for s in far], far, total, far_block)


def solution(mesh):
    in_specs = (P("row", "col"), P("row", "col", None, None), P("row", "col"), P("row", "col"))
    out_specs = P("row", "col")
    return jax.shard_map(body, mesh=mesh, in_specs=in_specs, out_specs=out_specs, check_vma=False)
```

```python
import functools
import math

import jax
import jax.numpy as jnp
from jax import lax
from jax.experimental import pallas as pl
from jax.experimental.pallas import tpu as pltpu
from jax.sharding import PartitionSpec as P

KT_DEV = 2
QT_DEV = 8
CORES = 2
META = 16
MIB = 1024 * 1024
WEIGHT = 10**9
WEIGHT_FAR = 4 * 10**9


def pack_kernel(columns, capacity, me_ref, ids_hbm, tiles_hbm, *refs):
    outs = refs[:columns]
    ids_ref, tiles_ref, slot_tile, slot_place, count, ids_sem, tiles_sem = refs[columns:]
    ids_copy = pltpu.make_async_copy(ids_hbm, ids_ref, ids_sem)
    tiles_copy = pltpu.make_async_copy(tiles_hbm, tiles_ref, tiles_sem)
    ids_copy.start()
    for t in range(tiles_ref.shape[1]):
        pltpu.make_async_copy(tiles_hbm.at[0, t], tiles_ref.at[0, t], tiles_sem).start()
    per_device, width = tiles_ref.shape[1], tiles_ref.shape[2]
    shift = per_device.bit_length() - 1
    for d in range(columns):
        count[d] = 0
        for s in range(capacity):
            slot_place[d * capacity + s] = per_device
    ids_copy.wait()
    for t in range(per_device):
        tile_id = ids_ref[0, t]
        target = lax.shift_right_logical(tile_id, shift)
        rank = count[target]
        count[target] = rank + 1
        slot_tile[target * capacity + rank] = t
        slot_place[target * capacity + rank] = tile_id & (per_device - 1)
    tiles_copy.wait()
    lane = lax.broadcasted_iota(jnp.int32, (META, width), 1)
    for d, out in enumerate(outs):
        target = me_ref[0] ^ d
        row = jnp.full((META, width), per_device, jnp.int32)
        for s in range(capacity):
            place = slot_place[target * capacity + s]
            row = jnp.where(lane == s, place, row)

            @pl.when(place < per_device)
            def _():
                out[s * width : (s + 1) * width, :] = tiles_ref[
                    0, slot_tile[target * capacity + s]
                ]

        out[capacity * width :, :] = row.astype(jnp.float32).astype(jnp.bfloat16)


def pack(col, packed_tiles, tile_ids, columns, capacity):
    _, per_device, width, _ = packed_tiles.shape
    chunk = jax.ShapeDtypeStruct((capacity * width + META, width), packed_tiles.dtype)
    smem = pl.BlockSpec(memory_space=pltpu.SMEM)
    vmem = pl.BlockSpec(memory_space=pltpu.VMEM)
    hbm = pl.BlockSpec(memory_space=pltpu.HBM)
    return pl.pallas_call(
        functools.partial(pack_kernel, columns, capacity),
        out_shape=[chunk] * columns,
        in_specs=[smem, hbm, hbm],
        out_specs=[vmem] * columns,
        scratch_shapes=[
            pltpu.SMEM(tile_ids.shape, jnp.int32),
            pltpu.VMEM(packed_tiles.shape, packed_tiles.dtype),
            pltpu.SMEM((columns * capacity,), jnp.int32),
            pltpu.SMEM((columns * capacity,), jnp.int32),
            pltpu.SMEM((columns,), jnp.int32),
            pltpu.SemaphoreType.DMA,
            pltpu.SemaphoreType.DMA,
        ],
        compiler_params=pltpu.CompilerParams(vmem_limit_bytes=8 * MIB),
        name="pack",
    )(
        col[None],
        pltpu.with_memory_space_constraint(tile_ids, pltpu.HBM),
        pltpu.with_memory_space_constraint(packed_tiles, pltpu.HBM),
    )


def join_kernel(*refs):
    at = 0
    for part in refs[:-1]:
        refs[-1][at : at + part.shape[0]] = part[...]
        at += part.shape[0]


def join(chunks, flops=0):
    vmem = pl.BlockSpec(memory_space=pltpu.VMEM)
    total = sum(c.shape[0] for c in chunks)
    return pl.pallas_call(
        join_kernel,
        out_shape=jax.ShapeDtypeStruct((total, *chunks[0].shape[1:]), chunks[0].dtype),
        in_specs=[vmem] * len(chunks),
        out_specs=vmem,
        compiler_params=pltpu.CompilerParams(vmem_limit_bytes=8 * MIB),
        cost_estimate=pl.CostEstimate(flops=flops, bytes_accessed=0, transcendentals=0),
        name="join",
    )(*chunks)


def multiply(amp, block, first, start, out, sems, step):
    copies = []
    for n in range(block.shape[1] // step):
        cols = slice(n * step, (n + 1) * step)
        held = out[0] if sems is not None else out
        held[:, cols] = start[:, cols] + jnp.dot(
            amp[...],
            block[first : first + amp.shape[1], cols],
            preferred_element_type=jnp.float32,
        )
        if sems is not None:
            part = pl.ds(n * step, step)
            copies.append(
                pltpu.make_async_copy(held.at[:, part], out[1].at[:, part], sems.at[n])
            )
            copies[-1].start()
    for copy in copies:
        copy.wait()


def near_kernel(n_pieces, offsets, capacity, n_columns, where_ref, *refs):
    n_amps = len(offsets)
    pieces = refs[:n_pieces]
    amps = refs[n_pieces : n_pieces + n_amps]
    own, residual, total, block = refs[n_pieces + n_amps : n_pieces + n_amps + 4]
    places, table, amp, res, table_sem, own_sem, res_sem = refs[n_pieces + n_amps + 4 :]
    width = pieces[0].shape[2]
    per_device = KT_DEV * QT_DEV
    own_copy = pltpu.make_async_copy(own, amp.at[:, pl.ds(0, width)], own_sem)
    own_copy.start()
    res_copy = pltpu.make_async_copy(residual, res, res_sem)
    share = residual.shape[0] // 8
    for i in range(8):
        part = pl.ds(i * share, share)
        pltpu.make_async_copy(residual.at[part, :], res.at[part, :], res_sem).start()
    at = 0
    for piece in pieces:
        rows = piece[:, capacity * width :, :]
        places[at : at + piece.shape[0]] = jnp.max(rows.astype(jnp.float32), axis=1).astype(
            jnp.int32
        )
        at += piece.shape[0]
    table_copy = pltpu.make_async_copy(places, table, table_sem)
    table_copy.start()
    for source, slot in zip(amps, offsets):
        amp[:, slot * width : (slot + 1) * width] = source[...]
    table_copy.wait()
    col = where_ref[n_pieces]
    full = capacity * n_columns == per_device
    at = 0
    for p, piece in enumerate(pieces):
        row = where_ref[p]
        for c in range(piece.shape[0]):
            for s in range(capacity):
                position = table[at, s]

                def put(position=position, piece=piece, c=c, s=s, row=row):
                    k = row * KT_DEV + lax.shift_right_logical(
                        position, QT_DEV.bit_length() - 1
                    )
                    q = position & (QT_DEV - 1)
                    block[
                        pl.ds(pl.multiple_of((k ^ col) * width, width), width),
                        pl.ds(pl.multiple_of(q * width, width), width),
                    ] = piece[c, s * width : (s + 1) * width, :]

                if full:
                    put()
                else:
                    pl.when(position < per_device)(put)
            at += 1
    own_copy.wait()
    res_copy.wait()
    multiply(amp, block, 0, res, total, None, block.shape[1])


def near_half(where, pieces, amps, offsets, own, residual, capacity):
    width = pieces[0].shape[2]
    n_pieces, n_amps = len(pieces), len(amps)
    chunks = sum(p.shape[0] for p in pieces)
    rows, n_cols = residual.shape
    depth = (1 + n_amps) * width
    hbm = pl.BlockSpec(memory_space=pltpu.HBM)
    vmem = pl.BlockSpec(memory_space=pltpu.VMEM)
    held = 2 * rows * depth + 4 * depth * n_cols + 8 * rows * n_cols
    held += sum(x.size * x.dtype.itemsize for x in pieces) // 2
    return pl.pallas_call(
        functools.partial(near_kernel, n_pieces, offsets, capacity, 1 + 2 * n_amps + 1),
        out_shape=[
            jax.ShapeDtypeStruct(residual.shape, residual.dtype),
            jax.ShapeDtypeStruct((2 * depth, n_cols), pieces[0].dtype),
        ],
        in_specs=[pl.BlockSpec(memory_space=pltpu.SMEM)]
        + [vmem] * (n_pieces + n_amps)
        + [hbm, hbm],
        out_specs=[vmem, vmem],
        scratch_shapes=[
            pltpu.VMEM((chunks, width), jnp.int32),
            pltpu.SMEM((chunks, width), jnp.int32),
            pltpu.VMEM((rows, depth), pieces[0].dtype),
            pltpu.VMEM((rows, n_cols), residual.dtype),
            pltpu.SemaphoreType.DMA,
            pltpu.SemaphoreType.DMA,
            pltpu.SemaphoreType.DMA,
        ],
        compiler_params=pltpu.CompilerParams(vmem_limit_bytes=held + 2 * MIB),
        cost_estimate=pl.CostEstimate(
            flops=2 * rows * depth * n_cols,
            bytes_accessed=16 * rows * n_cols,
            transcendentals=0,
        ),
        name="near_half",
    )(
        where,
        *pieces,
        *amps,
        pltpu.with_memory_space_constraint(own, pltpu.HBM),
        pltpu.with_memory_space_constraint(residual, pltpu.HBM),
    )


def far_kernel(offsets, half, *refs):
    amps = refs[: len(offsets)]
    start, block, out, amp, total, sems = refs[len(offsets) :]
    width = amps[0].shape[1]
    for source, slot in zip(amps, offsets):
        at = (slot - half) * width
        amp[:, at : at + width] = source[...]
    multiply(amp, block, block.shape[0] - amp.shape[1], start, (total, out), sems, 2 * width)


def far_half(amps, offsets, total, block):
    rows, n_cols = total.shape
    depth, width = block.shape[0] // 2, amps[0].shape[1]
    vmem = pl.BlockSpec(memory_space=pltpu.VMEM)
    held = 4 * rows * depth + 4 * depth * n_cols + 8 * rows * n_cols
    return pl.pallas_call(
        functools.partial(far_kernel, offsets, depth // width),
        out_shape=jax.ShapeDtypeStruct(total.shape, total.dtype),
        in_specs=[vmem] * (len(amps) + 2),
        out_specs=pl.BlockSpec(memory_space=pltpu.HBM),
        scratch_shapes=[
            pltpu.VMEM((rows, depth), block.dtype),
            pltpu.VMEM((rows, n_cols), total.dtype),
            pltpu.SemaphoreType.DMA((n_cols // (2 * width),)),
        ],
        compiler_params=pltpu.CompilerParams(vmem_limit_bytes=held + 2 * MIB),
        cost_estimate=pl.CostEstimate(
            flops=2 * rows * depth * n_cols,
            bytes_accessed=16 * rows * n_cols,
            transcendentals=0,
        ),
        name="far_half",
    )(*amps, total, block)


def exchange(x, axis, flip):
    size = lax.axis_size(axis)
    return lax.ppermute(x, axis, [(i, i ^ flip) for i in range(size)])


def tie(late, *early):
    return lax.optimization_barrier((late, *early))


def body(amplitudes, packed_tiles, tile_ids, residual_in):
    n_col, n_row = lax.axis_size("col"), lax.axis_size("row")
    col, row = lax.axis_index("col"), lax.axis_index("row")
    inner = 2 ** (int(math.log2(n_col)) // 2)
    capacity = -(-packed_tiles.shape[1] // n_col)
    half = n_col // 2
    outgoing = list(pack(col, packed_tiles, tile_ids, n_col, capacity))

    amps = {0: amplitudes}
    for s in [*range(1, inner), *range(inner, half, inner), half]:
        amps[s] = exchange(amplitudes, "col", s)
    outgoing[half:], amps = tie(outgoing[half:], amps)

    chunks = [outgoing[0][None]]
    chunks += [exchange(outgoing[s][None], "col", s) for s in range(1, n_col)]
    for flip in range(inner, half, inner):
        for lane in range(1, inner):
            amps[flip ^ lane] = exchange(amps[flip], "col", lane)
        amps[flip ^ half] = exchange(amps[flip], "col", half)
    for lane in range(1, inner):
        amps[half ^ lane] = exchange(amps[half], "col", lane)

    early = [s for s in amps if s and (s < half or half < s < half + inner)]
    flips = range(CORES, n_row, CORES)
    cut = half + half // 2
    far_groups = [join(chunks[half:cut], WEIGHT), join(chunks[cut:], WEIGHT)]
    near_group = join(chunks[:half])
    far_passed = [[exchange(g, "row", flip) for flip in flips] for g in far_groups]
    near_passed = [exchange(near_group, "row", flip) for flip in flips]
    far_passed, got = tie(far_passed, [amps[s] for s in early])
    amps.update(zip(early, got))
    pieces, rows = [], []
    for held, passed in (
        (join(far_groups), [join(x) for x in zip(*far_passed)]),
        (near_group, near_passed),
    ):
        own, passed = tie(held, passed)
        for flip, mine in zip(range(0, n_row, CORES), [own, *passed]):
            pieces += [mine, exchange(mine, "row", 1)]
            rows += [row ^ flip, row ^ flip ^ 1]
    for flip in range(half + inner, n_col, inner):
        there = join([amps[flip]], WEIGHT_FAR)
        for lane in range(1, inner):
            amps[flip ^ lane] = exchange(there, "col", lane)

    where = jnp.stack(rows + [col]).astype(jnp.int32)
    near = [s for s in sorted(amps) if 0 < s < half]
    far = [s for s in sorted(amps) if s >= half]
    total, far_block = near_half(
        where, pieces, [amps[s] for s in near], near, amplitudes, residual_in, capacity
    )
    return far_half([amps[s] for s in far], far, total, far_block)


def solution(mesh):
    in_specs = (P("row", "col"), P("row", "col", None, None), P("row", "col"), P("row", "col"))
    out_specs = P("row", "col")
    return jax.shard_map(body, mesh=mesh, in_specs=in_specs, out_specs=out_specs, check_vma=False)
```
